32 devices in a mesh: group: 2 (over y), expert: 4 (over z), tensor: 4 (over x, core).
Axes of the slice: x: 2, y: 2, z: 4, core: 2. Of those that a mesh axis runs over, the one named last changes fastest.
Arguments:
- inputs: bfloat16 [1024, 1024], P(('group', 'expert')), parts along dimension 0, may hold values from -6 to 6
- cotangent: bfloat16 [1024, 1024], P(('group', 'expert')), parts along dimension 0, may hold values from -6 to 6
- gate_values: float32 [1024, 2], P(('group', 'expert')), parts along dimension 0, may hold values from 0.25 to 1
- routes: int32 [1024, 2], P(('group', 'expert')), parts along dimension 0, may hold values from 0 to 7, all different within a row; in each aligned block of 128 rows (0 to 127, 128 to 255, ...) at most 64 rows name the same one
- pair_weight: bfloat16 [8, 256, 1024], P('expert', None, 'tensor'), may hold values from -1.5 to 1.5
- up_weight: bfloat16 [8, 1024, 2048], P('expert', None, 'tensor'), may hold values from -0.1875 to 0.1875
- down_weight: bfloat16 [8, 2048, 1024], P('expert', 'tensor'), may hold values from -0.125 to 0.125
Outputs:
- mixed: bfloat16 [1024, 1024], P(('group', 'expert'), 'tensor'), parts along dimension 0
- grad_input: bfloat16 [1024, 1024], P(('group', 'expert'), 'tensor'), parts along dimension 0
- grad_pair: bfloat16 [16, 256, 1024], P(('group', 'expert'), None, 'tensor'), parts along dimension 0
- grad_up: bfloat16 [16, 1024, 2048], P(('group', 'expert'), None, 'tensor'), parts along dimension 0
- grad_down: bfloat16 [16, 2048, 1024], P(('group', 'expert'), 'tensor'), parts along dimension 0
The draws below stay inside these ranges and needn't reach their ends.
There are 2 independent parts, one for each index of `group`. The reference program is written for one: setup_inputs(seed, part) draws one part's arguments, and reference() takes and returns one part's arrays. A program takes and returns all parts, laid end to end along the dimension named above; an argument that names none is the same for every part. Nothing has to cross between parts.
Inputs may be any that keep to these rules, and one draw needn't show every extreme that they name: `routes`: the 2 experts of one example differ. Among the rows of one device (aligned blocks of 128 examples) no expert is named more than 64 times, and in every draw some expert is named exactly 64 times in some block.
All inputs are finite; a program needn't handle non-finite values.
Results may differ from the reference program's by a relative error of at most 0.011.
Values may be sent and summed in bfloat16 or wider, within the bound.
No kernel may reach another device: no remote copies, remote signals or barrier semaphores. Data moves between devices by JAX's collectives and lax.ppermute only.
A program may use at most 64 MiB of HBM per device.

```python
import math
import jax
import jax.numpy as jnp
import numpy as np
from jax import lax

NF = 16
DE = 64
D = 1024
FF = 2048
TOK_DEV = 128
TOP = 2
EXPERTS = 8
TOKENS = 512
CAP = 64
PAIRS = 256
N_EXPERT = 4
N_TENSOR = 4


def block_levels(rng, dims, pieces, least, top_value):
    def one(axis_at, shards_of):
        steps = jax.random.uniform(jax.random.fold_in(jax.random.fold_in(rng, 6), axis_at), (shards_of,), jnp.float32, least / len(pieces), top_value / len(pieces))
        return jnp.repeat(jnp.exp(steps), dims[axis_at] // shards_of).reshape((-1,) + (1,) * (len(dims) - axis_at - 1))

    factor_of = one(*pieces[0])
    for cut in pieces[1:]:
        factor_of = factor_of * one(*cut)
    return factor_of


def routed_block(rng, own, number, rows, number_of, top, bound, lean):
    sequence = jax.random.permutation(rng, number_of)
    crowded, ordinary = shares(number_of, rows * top, bound, lean, True), shares(number_of, rows * top, bound, lean, False)
    places = jnp.arange(number_of)

    def named(lengths, offset_by):
        used = int((lengths > 0).sum())
        fixed = max(1, used // 4)
        shifted = fixed + (places - fixed + offset_by * (used - fixed)) % max(1, number_of - fixed)
        return jnp.zeros((number_of,), jnp.int32).at[sequence[jnp.where(places < fixed, places, shifted)]].set(jnp.asarray(lengths, jnp.int32))

    lengths = jnp.where(number % 4 == 0, named(crowded, number // 4), named(ordinary, number - number // 4 - 1))
    mixed = jax.random.permutation(jax.random.fold_in(own, 3), number_of)
    giver, sink = mixed[0:number_of // 2 * 2:2], mixed[1:number_of // 2 * 2:2]
    room = jnp.minimum(lengths[giver] - 1, bound - lengths[sink]) // 2
    room = jnp.where((giver == sequence[0]) | (sink == sequence[0]) | (lengths[sink] == 0), 0, jnp.maximum(room, 0))
    shifted = jax.random.randint(jax.random.fold_in(own, 4), (number_of // 2,), 0, 1 << 20) % (room + 1)
    lengths = lengths.at[giver].add(-shifted).at[sink].add(shifted)
    items = jnp.searchsorted(jnp.cumsum(lengths), jnp.arange(rows * top), side="right").astype(jnp.int32)
    table = items.reshape(top, rows).T
    table = table[jax.random.permutation(jax.random.fold_in(own, 1), rows)]
    offset_by = jax.random.randint(jax.random.fold_in(own, 2), (rows, 1), 0, top)
    return jnp.take_along_axis(table, (jnp.arange(top)[None, :] + offset_by) % top, axis=1)


def shares(number_of, total, reach, slope, full):
    portions = [(1 << 20) // math.isqrt(standing ** slope) + 1 for standing in range(1, number_of + 1)]
    largest = reach if full else min(reach, max(-(-total // number_of), total * portions[0] // sum(portions)))
    least = 1 if total - largest >= number_of - 1 else 0
    given, spare = [largest] + [least] * (number_of - 1), total - largest - least * (number_of - 1)
    while spare > 0:
        movable = [i for i in range(1, number_of) if given[i] < largest] or [i for i in range(1, number_of) if given[i] < reach]
        pool, remaining = sum([portions[i] for i in movable]), spare
        for i in movable:
            extra = min(reach - given[i], max(1, remaining * portions[i] // pool), spare)
            given[i] = given[i] + extra
            spare = spare - extra
    return np.array(given)


def gaussian(stream_key, extent, spread, bound, cuts=(), kind=jnp.bfloat16):
    entries = spread * jax.random.normal(stream_key, extent, jnp.float32)
    if cuts:
        entries = entries * block_levels(stream_key, extent, cuts, -0.22, 0.18)
    return jnp.clip(entries, -bound, bound).astype(kind)


def setup_inputs(seed: int = 0, part: int = 0) -> dict:
    key_list = jax.random.split(jax.random.key(seed), 8)
    part_splits = jax.random.split(jax.random.fold_in(key_list[7], part), 8)
    inputs = gaussian(part_splits[0], (TOKENS, D), 1.0, 6.0, ((0, 4),))
    cotangent = gaussian(part_splits[1], (TOKENS, D), 1.0, 6.0, ((0, 4),))
    gate_values = jnp.clip(0.25 + 0.75 * jax.random.uniform(part_splits[2], (TOKENS, TOP), jnp.float32) ** block_levels(part_splits[2], (TOKENS, TOP), ((0, 4),), -0.2, 0.2), 0.25, 1.0)
    routes_keys = jax.random.split(jax.random.fold_in(part_splits[3], 1), TOKENS // TOK_DEV)
    routes_turns = jax.random.permutation(jax.random.fold_in(part_splits[3], 3), TOKENS // TOK_DEV)
    routes = jax.vmap(lambda own, number: routed_block(jax.random.fold_in(part_splits[3], 2), own, number, TOK_DEV, EXPERTS, TOP, CAP, 2))(routes_keys, routes_turns).reshape((TOKENS, TOP))
    pair_weight = gaussian(key_list[4], (EXPERTS, PAIRS, D), NF ** -0.5, 1.5, ((0, 4), (2, 4)))
    up_weight = gaussian(key_list[5], (EXPERTS, D, FF), D ** -0.5, 0.1875, ((0, 4), (2, 4)))
    down_weight = gaussian(key_list[6], (EXPERTS, FF, D), FF ** -0.5, 0.125, ((0, 4), (1, 4)))
    return dict(inputs=inputs, cotangent=cotangent, gate_values=gate_values, routes=routes, pair_weight=pair_weight, up_weight=up_weight, down_weight=down_weight)


def rounded_sum(terms):
    rounded = lax.optimization_barrier(terms.astype(jnp.bfloat16))
    return jnp.sum(rounded.astype(jnp.float32), axis=0)


def expert_pass(packed):
    input_rows, grad_rows, pair_weight, up_weight, down_weight = packed
    row_count = input_rows.shape[0]
    block_width = FF // N_TENSOR
    cells = input_rows.astype(jnp.float32).reshape(row_count, NF, DE)
    gram = jnp.einsum("rid,rjd->rij", cells, cells, precision=lax.Precision.HIGHEST) / DE
    gram_flat = gram.reshape(row_count, PAIRS).astype(jnp.bfloat16)
    cross = (input_rows.astype(jnp.float32) + jnp.dot(gram_flat, pair_weight, preferred_element_type=jnp.float32)).astype(jnp.bfloat16)
    hidden_pre = jnp.dot(cross, up_weight, preferred_element_type=jnp.float32)
    hidden_act = jax.nn.silu(hidden_pre).astype(jnp.bfloat16)
    act_blocks = hidden_act.astype(jnp.float32).reshape(row_count, N_TENSOR, block_width)
    down_blocks = down_weight.astype(jnp.float32).reshape(N_TENSOR, block_width, D)
    out_rows = rounded_sum(jnp.einsum("rjh,jhd->jrd", act_blocks, down_blocks)).astype(jnp.bfloat16)
    grad_act = jnp.dot(grad_rows, down_weight.T, preferred_element_type=jnp.float32)
    sigmoid_pre = jax.nn.sigmoid(hidden_pre)
    grad_pre = (grad_act * sigmoid_pre * (1.0 + hidden_pre * (1.0 - sigmoid_pre))).astype(jnp.bfloat16)
    grad_down = jnp.dot(hidden_act.T, grad_rows, preferred_element_type=jnp.float32).astype(jnp.bfloat16)
    grad_up = jnp.dot(cross.T, grad_pre, preferred_element_type=jnp.float32).astype(jnp.bfloat16)
    pre_blocks = grad_pre.astype(jnp.float32).reshape(row_count, N_TENSOR, block_width)
    up_blocks = up_weight.astype(jnp.float32).reshape(D, N_TENSOR, block_width)
    grad_cross = rounded_sum(jnp.einsum("rjh,djh->jrd", pre_blocks, up_blocks)).astype(jnp.bfloat16)
    grad_pair = jnp.dot(gram_flat.T, grad_cross, preferred_element_type=jnp.float32).astype(jnp.bfloat16)
    grad_gram = jnp.dot(grad_cross, pair_weight.T, preferred_element_type=jnp.float32).reshape(row_count, NF, NF)
    symmetric = grad_gram + jnp.swapaxes(grad_gram, 1, 2)
    gram_back = jnp.einsum("rij,rjd->rid", symmetric, cells, precision=lax.Precision.HIGHEST).reshape(row_count, D) / DE
    grad_row = (grad_cross.astype(jnp.float32) + gram_back).astype(jnp.bfloat16)
    return out_rows, grad_row, grad_pair, grad_up, grad_down


def reference(inputs, cotangent, gate_values, routes, pair_weight, up_weight, down_weight):
    device_routes = routes.reshape(N_EXPERT, TOK_DEV * TOP)
    onehot = (device_routes[:, :, None] == jnp.arange(EXPERTS, dtype=jnp.int32)[None, None, :]).astype(jnp.int32)
    before = jnp.cumsum(onehot, axis=1) - onehot
    position = jnp.sum(before * onehot, axis=2).astype(jnp.int32)
    row_place = (jnp.arange(N_EXPERT, dtype=jnp.int32)[:, None] * CAP + position).reshape(-1)
    flat_expert = device_routes.reshape(-1)
    example_index = (jnp.arange(TOKENS * TOP, dtype=jnp.int32) // TOP).astype(jnp.int32)
    scaled = (gate_values[:, :, None] * cotangent[:, None, :].astype(jnp.float32)).astype(jnp.bfloat16)
    scaled = scaled.reshape(TOKENS * TOP, D)
    input_slots = jnp.zeros((EXPERTS, N_EXPERT * CAP, D), jnp.bfloat16).at[flat_expert, row_place].set(inputs[example_index])
    grad_slots = jnp.zeros((EXPERTS, N_EXPERT * CAP, D), jnp.bfloat16).at[flat_expert, row_place].set(scaled)
    out_slots, back_slots, grad_pair, grad_up, grad_down = lax.map(expert_pass, (input_slots, grad_slots, pair_weight, up_weight, down_weight))
    picked = out_slots[flat_expert, row_place].reshape(TOKENS, TOP, D).astype(jnp.float32)
    mixed = (inputs.astype(jnp.float32) + jnp.sum(gate_values[:, :, None] * picked, axis=1)).astype(jnp.bfloat16)
    backed = back_slots[flat_expert, row_place].reshape(TOKENS, TOP, D).astype(jnp.float32)
    grad_input = (cotangent.astype(jnp.float32) + jnp.sum(backed, axis=1)).astype(jnp.bfloat16)
    return mixed, grad_input, grad_pair, grad_up, grad_down
```

```python
import functools

import jax
import jax.numpy as jnp
from jax import lax
from jax.experimental import pallas as pl
from jax.experimental.pallas import tpu as pltpu
from jax.sharding import PartitionSpec as P

NF = 16
DE = 64


def dispatch_tables(routes, expert_total, capacity):
    row_count, pick_count = routes.shape
    flat_ids = routes.reshape(-1)
    onehot = (flat_ids[:, None] == jnp.arange(expert_total, dtype=jnp.int32)[None, :]).astype(
        jnp.int32
    )
    before = jnp.cumsum(onehot, axis=0) - onehot
    position = jnp.sum(before * onehot, axis=1)
    slot_index = flat_ids * capacity + position
    slot_count = expert_total * capacity
    tables = slot_index[:, None] == jnp.arange(slot_count, dtype=jnp.int32)[None, :]
    tables = tables.reshape(row_count, pick_count, slot_count)
    return jnp.transpose(tables, (1, 2, 0)).astype(jnp.bfloat16)


def body(inputs, cotangent, gate_values, routes, pair_weight, up_weight, down_weight):
    local_count = up_weight.shape[0]
    expert_count = lax.axis_size("expert")
    tensor_count = lax.axis_size("tensor")
    expert_total = local_count * expert_count
    row_count, pick_count = routes.shape
    feature_width = inputs.shape[1]
    capacity = 2 * row_count * pick_count // expert_total
    expert_rows = expert_count * capacity
    part_width = feature_width // tensor_count
    tensor_index = lax.axis_index("tensor")
    feature_start = tensor_index * part_width
    tables = dispatch_tables(routes, expert_total, capacity)
    any_table = jnp.sum(tables, axis=0)
    scaled = (gate_values[:, :, None] * cotangent[:, None, :].astype(jnp.float32)).astype(
        jnp.bfloat16
    )
    input_slice = lax.dynamic_slice_in_dim(inputs, feature_start, part_width, 1)
    cotangent_slice = lax.dynamic_slice_in_dim(cotangent, feature_start, part_width, 1)
    input_slots = jnp.dot(any_table, inputs, preferred_element_type=jnp.float32).astype(
        jnp.bfloat16
    )
    grad_slots = jnp.einsum(
        "ksr,rkd->sd", tables, scaled, preferred_element_type=jnp.float32
    ).astype(jnp.bfloat16)
    send_shape = (expert_count, local_count, capacity, feature_width)
    input_homes, grad_homes = (
        lax.all_to_all(
            input_slots.reshape(send_shape), "expert", split_axis=0, concat_axis=2, tiled=True
        ),
        lax.all_to_all(
            grad_slots.reshape(send_shape), "expert", split_axis=0, concat_axis=2, tiled=True
        ),
    )
    input_rows = input_homes.reshape(local_count, expert_rows, feature_width)
    grad_rows = grad_homes.reshape(local_count, expert_rows, feature_width)
    cells = jnp.transpose(input_rows.reshape(local_count, expert_rows, NF, DE), (0, 2, 3, 1))
    gram = jnp.einsum("eidr,ejdr->eijr", cells, cells, preferred_element_type=jnp.float32) / DE
    gram_flat = gram.reshape(local_count, NF * NF, expert_rows).astype(jnp.bfloat16)
    input_mine = lax.dynamic_slice_in_dim(input_rows, feature_start, part_width, 2)
    cross_sum = input_mine.astype(jnp.float32) + jnp.einsum(
        "epr,epd->erd", gram_flat, pair_weight, preferred_element_type=jnp.float32
    )
    cross_part = cross_sum.astype(jnp.bfloat16)
    cross_whole = lax.all_gather(cross_part, "tensor", axis=2, tiled=True)
    hidden_pre = jnp.einsum(
        "erd,edh->erh", cross_whole, up_weight, preferred_element_type=jnp.float32
    )
    hidden_act = jax.nn.silu(hidden_pre).astype(jnp.bfloat16)
    out_terms = jnp.einsum(
        "erh,ehd->erd", hidden_act, down_weight, preferred_element_type=jnp.float32
    )
    out_mine = lax.psum_scatter(
        out_terms.astype(jnp.bfloat16), "tensor", scatter_dimension=2, tiled=True
    )
    grad_act = jnp.einsum(
        "erd,ehd->erh", grad_rows, down_weight, preferred_element_type=jnp.float32
    )
    sigmoid_pre = jax.nn.sigmoid(hidden_pre)
    grad_pre = (grad_act * sigmoid_pre * (1.0 + hidden_pre * (1.0 - sigmoid_pre))).astype(
        jnp.bfloat16
    )
    grad_down = jnp.einsum(
        "erh,erd->ehd", hidden_act, grad_rows, preferred_element_type=jnp.float32
    ).astype(jnp.bfloat16)
    grad_up = jnp.einsum(
        "erd,erh->edh", cross_whole, grad_pre, preferred_element_type=jnp.float32
    ).astype(jnp.bfloat16)
    cross_terms = jnp.einsum(
        "erh,edh->erd", grad_pre, up_weight, preferred_element_type=jnp.float32
    )
    grad_cross = lax.psum_scatter(
        cross_terms.astype(jnp.bfloat16), "tensor", scatter_dimension=2, tiled=True
    )
    grad_pair = jnp.einsum(
        "epr,erd->epd", gram_flat, grad_cross, preferred_element_type=jnp.float32
    ).astype(jnp.bfloat16)
    pair_terms = jnp.einsum(
        "erd,epd->epr", grad_cross, pair_weight, preferred_element_type=jnp.float32
    )
    grad_gram = (
        lax.psum(pair_terms.astype(jnp.bfloat16), "tensor")
        .astype(jnp.float32)
        .reshape(local_count, NF, NF, expert_rows)
    )
    symmetric = grad_gram + jnp.swapaxes(grad_gram, 1, 2)
    field_count = part_width // DE
    symmetric_mine = lax.dynamic_slice_in_dim(symmetric, tensor_index * field_count, field_count, 1)
    gram_back = (
        jnp.einsum(
            "eijr,ejdr->eidr",
            symmetric_mine,
            cells.astype(jnp.float32),
            precision=lax.Precision.HIGHEST,
        )
        / DE
    )
    gram_back = jnp.transpose(gram_back, (0, 3, 1, 2)).reshape(local_count, expert_rows, part_width)
    grad_mine = (grad_cross.astype(jnp.float32) + gram_back).astype(jnp.bfloat16)
    back_shape = (1, local_count, expert_rows, part_width)
    out_back, grad_back = (
        lax.all_to_all(
            out_mine.reshape(back_shape), "expert", split_axis=2, concat_axis=0, tiled=True
        ),
        lax.all_to_all(
            grad_mine.reshape(back_shape), "expert", split_axis=2, concat_axis=0, tiled=True
        ),
    )
    out_back = out_back.reshape(expert_total * capacity, part_width)
    grad_back = grad_back.reshape(expert_total * capacity, part_width)
    picked = jnp.einsum("ksr,sd->rkd", tables, out_back, preferred_element_type=jnp.float32)
    mixed = (
        input_slice.astype(jnp.float32) + jnp.sum(gate_values[:, :, None] * picked, axis=1)
    ).astype(jnp.bfloat16)
    grad_input = (
        cotangent_slice.astype(jnp.float32)
        + jnp.dot(any_table.T, grad_back, preferred_element_type=jnp.float32)
    ).astype(jnp.bfloat16)
    return (mixed, grad_input, grad_pair, grad_up, grad_down)


F32 = jnp.float32
BF16 = jnp.bfloat16
NT = (((1,), (1,)), ((), ()))
TN = (((0,), (0,)), ((), ()))


def mm(a, b, dims=None):
    if dims is None:
        return jnp.dot(a, b, preferred_element_type=F32)
    return lax.dot_general(a, b, dims, preferred_element_type=F32)


def kernel_call(kernel, out_shape, scratch=(), flops=0, nbytes=0):
    return pl.pallas_call(
        kernel,
        out_shape=out_shape,
        scratch_shapes=list(scratch),
        compiler_params=pltpu.CompilerParams(vmem_limit_bytes=48 * 1024 * 1024),
        cost_estimate=pl.CostEstimate(flops=flops, bytes_accessed=nbytes, transcendentals=0),
    )


def shape(dims, dtype=BF16):
    return jax.ShapeDtypeStruct(dims, dtype)


def meta_kernel(gates_ref, routes_ref, meta_ref):
    rows = gates_ref.shape[0]
    eye = lax.broadcasted_iota(jnp.int32, (rows, rows), 0) == lax.broadcasted_iota(
        jnp.int32, (rows, rows), 1
    )

    def row_of(column):
        return jnp.sum(jnp.where(eye, column, 0.0), axis=0, keepdims=True)

    routes = routes_ref[...].astype(F32)
    gates = gates_ref[...]
    for k in range(2):
        meta_ref[k : k + 1, :] = row_of(routes[:, k : k + 1])
        meta_ref[2 + k : 3 + k, :] = row_of(gates[:, k : k + 1])
    meta_ref[4:8, :] = jnp.zeros((4, rows), F32)


def gather_rows(whole, own_ref, near, far, core):
    half = own_ref.shape[0] // 2
    whole[0 : 2 * half, :] = own_ref[...]
    for r in range(3):
        start = 2 * half * (r + 1)
        whole[pl.ds(pl.multiple_of(start + core * half, half), half), :] = near[r][...]
        whole[pl.ds(pl.multiple_of(start + (1 - core) * half, half), half), :] = far[r][...]


def forward_kernel(*refs):
    (xo, x1, x2, x3, y1, y2, y3, m0, m1, m2, m3, p0, p1, p2, p3, up, down) = refs[:17]
    keep, send, cross_o, act_o, dfac_o, gram_o, pick_o, gate_o, pair_o = refs[17:26]
    whole, flipped = refs[26:]
    j = lax.axis_index("tensor")
    core = lax.rem(j, 2)
    xi = j // 2
    first = lax.axis_index("expert") * 2
    gather_rows(whole, xo, (x1, x2, x3), (y1, y2, y3), core)
    for k, piece in enumerate((p0, p1, p2, p3)):
        at = pl.multiple_of((j ^ k) * 256, 256)
        for e in range(2):
            pair_o[e, :, pl.ds(at, 256)] = piece[e]
    meta = jnp.concatenate([m0[...], m1[...], m2[...], m3[...]], axis=1)
    tokens = meta.shape[1]
    before = (
        lax.broadcasted_iota(jnp.int32, (tokens, tokens), 0)
        < lax.broadcasted_iota(jnp.int32, (tokens, tokens), 1)
    ).astype(F32).astype(BF16)
    for e in range(2):
        mine = (first + e).astype(F32)
        s0 = meta[0:1, :] == mine
        s1 = meta[1:2, :] == mine
        named = jnp.where(s0, 1.0, 0.0) + jnp.where(s1, 1.0, 0.0)
        gate = jnp.where(s0, meta[2:3, :], 0.0) + jnp.where(s1, meta[3:4, :], 0.0)
        place = mm(jnp.broadcast_to(named, (8, tokens)).astype(BF16), before)[0:1, :]
        place = jnp.where(named > 0.5, place, -1.0)
        slot = lax.broadcasted_iota(jnp.int32, (256, tokens), 0).astype(F32)
        hit = slot == place
        pick = jnp.where(hit, 1.0, 0.0).astype(BF16)
        gate_o[e] = jnp.broadcast_to(
            jnp.sum(jnp.where(hit, gate, 0.0), axis=1, keepdims=True), (256, 128)
        )
        pick_o[e] = pick
        rows = mm(pick, whole[...])
        flipped[...] = rows.T

        def gram_step(i, carry):
            left = flipped[pl.ds(pl.multiple_of(i * 64, 64), 64), :]
            out = []
            for q in range(16):
                prod = left * flipped[q * 64 : q * 64 + 64, :]
                out.append(jnp.sum(prod, axis=0, keepdims=True))
            block = jnp.concatenate(out, axis=0) * (1.0 / DE)
            gram_o[e, pl.ds(pl.multiple_of(i * 16, 16), 16), :] = block.astype(BF16)
            return carry

        lax.fori_loop(0, 16, gram_step, 0)
        cross = (rows + mm(gram_o[e], pair_o[e], TN)).astype(BF16)
        cross_o[e] = cross
        pre = mm(cross, up[e])
        sig = jax.nn.sigmoid(pre)
        act = (pre * sig).astype(BF16)
        act_o[e] = act
        dfac_o[e] = sig * (1.0 + pre * (1.0 - sig))
        for xr in range(2):
            for part in range(2):
                block = 2 * (xi ^ xr) + (core ^ part)
                at = pl.multiple_of(block * 256, 256)
                term = mm(act, down[e, :, pl.ds(at, 256)]).astype(BF16)
                (keep, send)[part][xr, e * 256 : e * 256 + 256, :] = term


def backward_kernel(*refs):
    (co, c1, c2, c3, d1, d2, d3, pick, gate, dfac, pair, up, down) = refs[:13]
    keep, send, grad_o, pre_o = refs[13:17]
    whole, terms = refs[17:]
    j = lax.axis_index("tensor")
    core = lax.rem(j, 2)
    xi = j // 2
    gather_rows(whole, co, (c1, c2, c3), (d1, d2, d3), core)
    a = lax.broadcasted_iota(jnp.int32, (256, 256), 0)
    b = lax.broadcasted_iota(jnp.int32, (256, 256), 1)
    swapped = (a % 16) * 16 + a // 16
    both = (jnp.where(a == b, 1.0, 0.0) + jnp.where(swapped == b, 1.0, 0.0)).astype(BF16)
    for e in range(2):
        grad = (gate[e][:, 0:1] * mm(pick[e], whole[...])).astype(BF16)
        grad_o[e] = grad
        grad_act = mm(grad, down[e], NT)
        pre = (grad_act * dfac[e]).astype(BF16)
        pre_o[e] = pre
        terms[...] = mm(pre, up[e], NT).astype(BF16)
        back = mm(pair[e], terms[...], NT).astype(BF16)
        back = mm(both, back).astype(BF16)
        wide = back.reshape(4, 64, 256)
        for xr in range(2):
            for part in range(2):
                block = 2 * (xi ^ xr) + (core ^ part)
                at = pl.multiple_of(block * 256, 256)
                dst = (keep, send)[part]
                dst[xr, e * 256 : e * 256 + 256, :] = terms[:, pl.ds(at, 256)]
        for q in range(4):
            rel = q ^ j

            for xr in range(2):
                for part in range(2):
                    @pl.when(rel == 2 * xr + part)
                    def _():
                        dst = (keep, send)[part]
                        dst[xr, 512 + e * 64 : 512 + e * 64 + 64, :] = wide[q]


def weights_kernel(act, grad, cross, pre, down_o, up_o):
    for e in range(2):
        down_o[e] = mm(act[e], grad[e], TN).astype(BF16)
        up_o[e] = mm(cross[e], pre[e], TN).astype(BF16)


def add2(a, b):
    return (a.astype(F32) + b.astype(F32)).astype(BF16)


def mixed_kernel(mine, theirs, pick, gate, out_o):
    total = jnp.zeros((512, 256), F32)
    for e in range(2):
        at = slice(e * 256, e * 256 + 256)
        rows = add2(mine[at, :], theirs[at, :]).astype(F32)
        rows = (rows * gate[e][:, 0:1]).astype(BF16)
        total = total + mm(pick[e], rows, TN)
    total = total.astype(BF16)
    for r in range(4):
        out_o[r] = total[r * 128 : r * 128 + 128, :]


def combine_kernel(mine, theirs, pick, out_o, rows_o):
    total = jnp.zeros((512, 256), F32)
    back = jnp.zeros((64, 512), F32)
    for e in range(2):
        at = slice(e * 256, e * 256 + 256)
        rows = add2(mine[at, :], theirs[at, :])
        rows_o[e] = rows
        total = total + mm(pick[e], rows, TN)
        sat = slice(512 + e * 64, 512 + e * 64 + 64)
        back = back + mm(add2(mine[sat, :], theirs[sat, :]), pick[e])
    total = total.astype(BF16)
    back = back.astype(BF16)
    for r in range(4):
        out_o[r, 0:128, :] = total[r * 128 : r * 128 + 128, :]
        part = back[:, r * 128 : r * 128 + 128]
        out_o[r, 128:160, 0:128] = part[0:32]
        out_o[r, 128:160, 128:256] = part[32:64]


def pair_kernel(gram, rows, out_o):
    for e in range(2):
        out_o[e] = mm(gram[e], rows[e]).astype(BF16)


def final_kernel(x, c, n0, n1, n2, n3, g0, g1, g2, g3, mixed_o, grad_o, flipped):
    j = lax.axis_index("tensor")
    at = pl.multiple_of(j * 256, 256)
    total = x[:, pl.ds(at, 256)].astype(F32)
    for n in (n0, n1, n2, n3):
        total = total + n[...].astype(F32)
    mixed_o[...] = total.astype(BF16)
    flipped[...] = x[...].astype(F32).T
    total = c[:, pl.ds(at, 256)].astype(F32)
    back = jnp.zeros((32, 256), F32)
    for g in (g0, g1, g2, g3):
        total = total + g[0:128, :].astype(F32)
        back = back + g[128:160, :].astype(F32)
    back = jnp.concatenate([back[:, 0:128], back[:, 128:256]], axis=0)
    pieces = []
    for i in range(4):
        acc = jnp.zeros((64, 128), F32)
        for q in range(16):
            acc = acc + back[i * 16 + q : i * 16 + q + 1, :] * flipped[q * 64 : q * 64 + 64, :]
        pieces.append(acc)
    gram_back = jnp.concatenate(pieces, axis=0) * (1.0 / DE)
    grad_o[...] = (total + gram_back.T).astype(BF16)


def swap(value, axis, mask):
    size = lax.axis_size(axis)
    return lax.ppermute(value, axis, [(i, i ^ mask) for i in range(size)])


def gathered_body(inputs, cotangent, gate_values, routes, pair_weight, up_weight, down_weight):
    core = lax.axis_index("tensor") % 2
    half = inputs.shape[0] // 2
    x_half = lax.dynamic_slice_in_dim(inputs, core * half, half, 0)
    c_half = lax.dynamic_slice_in_dim(cotangent, core * half, half, 0)
    meta = kernel_call(meta_kernel, shape((8, 128), F32))(gate_values, routes)
    x_near = [swap(x_half, "expert", r) for r in (1, 2, 3)]
    metas = [meta] + [swap(meta, "expert", r) for r in (1, 2, 3)]
    c_near = [swap(c_half, "expert", r) for r in (1, 2, 3)]
    pair_x = swap(pair_weight, "tensor", 2)
    pair_c = swap(pair_weight, "tensor", 1)
    x_far = [swap(v, "tensor", 1) for v in x_near]
    pair_d = swap(pair_x, "tensor", 1)
    forward = kernel_call(
        forward_kernel,
        (
            shape((2, 512, 256)),
            shape((2, 512, 256)),
            shape((2, 256, 1024)),
            shape((2, 256, 512)),
            shape((2, 256, 512), F32),
            shape((2, 256, 256)),
            shape((2, 256, 512)),
            shape((2, 256, 128), F32),
            shape((2, 256, 1024)),
        ),
        scratch=[pltpu.VMEM((512, 1024), BF16), pltpu.VMEM((1024, 256), F32)],
        flops=4_000_000_000,
        nbytes=10_000_000,
    )
    keep, send, cross, act, dfac, gram, pick, gate, pair_all = forward(
        inputs, *x_near, *x_far, *metas, pair_weight, pair_c, pair_x, pair_d, up_weight, down_weight
    )
    got = swap(send, "tensor", 1)
    out_there = swap(add2(keep[1], got[1]), "tensor", 2)
    out_here = add2(keep[0], got[0])
    c_far = [swap(v, "tensor", 1) for v in c_near]
    backward = kernel_call(
        backward_kernel,
        (
            shape((2, 640, 256)),
            shape((2, 640, 256)),
            shape((2, 256, 1024)),
            shape((2, 256, 512)),
        ),
        scratch=[pltpu.VMEM((512, 1024), BF16), pltpu.VMEM((256, 1024), BF16)],
        flops=2_000_000_000,
        nbytes=10_000_000,
    )
    bkeep, bsend, grad, pre = backward(
        cotangent, *c_near, *c_far, pick, gate, dfac, pair_all, up_weight, down_weight
    )
    bgot = swap(bsend, "tensor", 1)
    back_there = swap(add2(bkeep[1], bgot[1]), "tensor", 2)
    back_here = add2(bkeep[0], bgot[0])
    mixed_parts = kernel_call(
        mixed_kernel, shape((4, 128, 256)), flops=300_000_000, nbytes=2_000_000
    )(out_here, out_there, pick, gate)
    mixed_got = [mixed_parts[0]] + [swap(mixed_parts[r], "expert", r) for r in (1, 2, 3)]
    grad_down, grad_up = kernel_call(
        weights_kernel,
        (shape((2, 512, 1024)), shape((2, 1024, 512))),
        flops=3_000_000_000,
        nbytes=8_000_000,
    )(act, grad, cross, pre)
    grad_parts, rows = kernel_call(
        combine_kernel,
        (shape((4, 160, 256)), shape((2, 256, 256))),
        flops=300_000_000,
        nbytes=2_000_000,
    )(back_here, back_there, pick)
    grad_got = [grad_parts[0]] + [swap(grad_parts[r], "expert", r) for r in (1, 2, 3)]
    grad_pair = kernel_call(
        pair_kernel, shape((2, 256, 256)), flops=300_000_000, nbytes=2_000_000
    )(gram, rows)
    mixed, grad_input = kernel_call(
        final_kernel,
        (shape((128, 256)), shape((128, 256))),
        scratch=[pltpu.VMEM((1024, 128), F32)],
        flops=100_000_000,
        nbytes=1_000_000,
    )(inputs, cotangent, *mixed_got, *grad_got)
    return mixed, grad_input, grad_pair, grad_up, grad_down


def solution(mesh):
    placed = (
        P(("group", "expert"), None),
        P(("group", "expert"), None),
        P(("group", "expert"), None),
        P(("group", "expert"), None),
        P("expert", None, "tensor"),
        P("expert", None, "tensor"),
        P("expert", "tensor", None),
    )
    small = mesh.shape["expert"] == 4 and mesh.shape["tensor"] == 4
    return jax.shard_map(
        gathered_body if small else body,
        mesh=mesh,
        in_specs=placed,
        out_specs=(
            P(("group", "expert"), "tensor"),
            P(("group", "expert"), "tensor"),
            P(("group", "expert"), None, "tensor"),
            P(("group", "expert"), None, "tensor"),
            P(("group", "expert"), "tensor", None),
        ),
        check_vma=False,
    )
```

```python
import functools

import jax
import jax.numpy as jnp
from jax import lax
from jax.experimental import pallas as pl
from jax.experimental.pallas import tpu as pltpu
from jax.sharding import PartitionSpec as P

NF = 16
DE = 64


def dispatch_tables(routes, expert_total, capacity):
    row_count, pick_count = routes.shape
    flat_ids = routes.reshape(-1)
    onehot = (flat_ids[:, None] == jnp.arange(expert_total, dtype=jnp.int32)[None, :]).astype(
        jnp.int32
    )
    before = jnp.cumsum(onehot, axis=0) - onehot
    position = jnp.sum(before * onehot, axis=1)
    slot_index = flat_ids * capacity + position
    slot_count = expert_total * capacity
    tables = slot_index[:, None] == jnp.arange(slot_count, dtype=jnp.int32)[None, :]
    tables = tables.reshape(row_count, pick_count, slot_count)
    return jnp.transpose(tables, (1, 2, 0)).astype(jnp.bfloat16)


def body(inputs, cotangent, gate_values, routes, pair_weight, up_weight, down_weight):
    local_count = up_weight.shape[0]
    expert_count = lax.axis_size("expert")
    tensor_count = lax.axis_size("tensor")
    expert_total = local_count * expert_count
    row_count, pick_count = routes.shape
    feature_width = inputs.shape[1]
    capacity = 2 * row_count * pick_count // expert_total
    expert_rows = expert_count * capacity
    part_width = feature_width // tensor_count
    tensor_index = lax.axis_index("tensor")
    feature_start = tensor_index * part_width
    tables = dispatch_tables(routes, expert_total, capacity)
    any_table = jnp.sum(tables, axis=0)
    scaled = (gate_values[:, :, None] * cotangent[:, None, :].astype(jnp.float32)).astype(
        jnp.bfloat16
    )
    input_slice = lax.dynamic_slice_in_dim(inputs, feature_start, part_width, 1)
    cotangent_slice = lax.dynamic_slice_in_dim(cotangent, feature_start, part_width, 1)
    input_slots = jnp.dot(any_table, inputs, preferred_element_type=jnp.float32).astype(
        jnp.bfloat16
    )
    grad_slots = jnp.einsum(
        "ksr,rkd->sd", tables, scaled, preferred_element_type=jnp.float32
    ).astype(jnp.bfloat16)
    send_shape = (expert_count, local_count, capacity, feature_width)
    input_homes, grad_homes = (
        lax.all_to_all(
            input_slots.reshape(send_shape), "expert", split_axis=0, concat_axis=2, tiled=True
        ),
        lax.all_to_all(
            grad_slots.reshape(send_shape), "expert", split_axis=0, concat_axis=2, tiled=True
        ),
    )
    input_rows = input_homes.reshape(local_count, expert_rows, feature_width)
    grad_rows = grad_homes.reshape(local_count, expert_rows, feature_width)
    cells = jnp.transpose(input_rows.reshape(local_count, expert_rows, NF, DE), (0, 2, 3, 1))
    gram = jnp.einsum("eidr,ejdr->eijr", cells, cells, preferred_element_type=jnp.float32) / DE
    gram_flat = gram.reshape(local_count, NF * NF, expert_rows).astype(jnp.bfloat16)
    input_mine = lax.dynamic_slice_in_dim(input_rows, feature_start, part_width, 2)
    cross_sum = input_mine.astype(jnp.float32) + jnp.einsum(
        "epr,epd->erd", gram_flat, pair_weight, preferred_element_type=jnp.float32
    )
    cross_part = cross_sum.astype(jnp.bfloat16)
    cross_whole = lax.all_gather(cross_part, "tensor", axis=2, tiled=True)
    hidden_pre = jnp.einsum(
        "erd,edh->erh", cross_whole, up_weight, preferred_element_type=jnp.float32
    )
    hidden_act = jax.nn.silu(hidden_pre).astype(jnp.bfloat16)
    out_terms = jnp.einsum(
        "erh,ehd->erd", hidden_act, down_weight, preferred_element_type=jnp.float32
    )
    out_mine = lax.psum_scatter(
        out_terms.astype(jnp.bfloat16), "tensor", scatter_dimension=2, tiled=True
    )
    grad_act = jnp.einsum(
        "erd,ehd->erh", grad_rows, down_weight, preferred_element_type=jnp.float32
    )
    sigmoid_pre = jax.nn.sigmoid(hidden_pre)
    grad_pre = (grad_act * sigmoid_pre * (1.0 + hidden_pre * (1.0 - sigmoid_pre))).astype(
        jnp.bfloat16
    )
    grad_down = jnp.einsum(
        "erh,erd->ehd", hidden_act, grad_rows, preferred_element_type=jnp.float32
    ).astype(jnp.bfloat16)
    grad_up = jnp.einsum(
        "erd,erh->edh", cross_whole, grad_pre, preferred_element_type=jnp.float32
    ).astype(jnp.bfloat16)
    cross_terms = jnp.einsum(
        "erh,edh->erd", grad_pre, up_weight, preferred_element_type=jnp.float32
    )
    grad_cross = lax.psum_scatter(
        cross_terms.astype(jnp.bfloat16), "tensor", scatter_dimension=2, tiled=True
    )
    grad_pair = jnp.einsum(
        "epr,erd->epd", gram_flat, grad_cross, preferred_element_type=jnp.float32
    ).astype(jnp.bfloat16)
    pair_terms = jnp.einsum(
        "erd,epd->epr", grad_cross, pair_weight, preferred_element_type=jnp.float32
    )
    grad_gram = (
        lax.psum(pair_terms.astype(jnp.bfloat16), "tensor")
        .astype(jnp.float32)
        .reshape(local_count, NF, NF, expert_rows)
    )
    symmetric = grad_gram + jnp.swapaxes(grad_gram, 1, 2)
    field_count = part_width // DE
    symmetric_mine = lax.dynamic_slice_in_dim(symmetric, tensor_index * field_count, field_count, 1)
    gram_back = (
        jnp.einsum(
            "eijr,ejdr->eidr",
            symmetric_mine,
            cells.astype(jnp.float32),
            precision=lax.Precision.HIGHEST,
        )
        / DE
    )
    gram_back = jnp.transpose(gram_back, (0, 3, 1, 2)).reshape(local_count, expert_rows, part_width)
    grad_mine = (grad_cross.astype(jnp.float32) + gram_back).astype(jnp.bfloat16)
    back_shape = (1, local_count, expert_rows, part_width)
    out_back, grad_back = (
        lax.all_to_all(
            out_mine.reshape(back_shape), "expert", split_axis=2, concat_axis=0, tiled=True
        ),
        lax.all_to_all(
            grad_mine.reshape(back_shape), "expert", split_axis=2, concat_axis=0, tiled=True
        ),
    )
    out_back = out_back.reshape(expert_total * capacity, part_width)
    grad_back = grad_back.reshape(expert_total * capacity, part_width)
    picked = jnp.einsum("ksr,sd->rkd", tables, out_back, preferred_element_type=jnp.float32)
    mixed = (
        input_slice.astype(jnp.float32) + jnp.sum(gate_values[:, :, None] * picked, axis=1)
    ).astype(jnp.bfloat16)
    grad_input = (
        cotangent_slice.astype(jnp.float32)
        + jnp.dot(any_table.T, grad_back, preferred_element_type=jnp.float32)
    ).astype(jnp.bfloat16)
    return (mixed, grad_input, grad_pair, grad_up, grad_down)


F32 = jnp.float32
BF16 = jnp.bfloat16
NT = (((1,), (1,)), ((), ()))
TN = (((0,), (0,)), ((), ()))


def mm(a, b, dims=None):
    if dims is None:
        return jnp.dot(a, b, preferred_element_type=F32)
    return lax.dot_general(a, b, dims, preferred_element_type=F32)


def kernel_call(kernel, out_shape, scratch=(), flops=0, nbytes=0, waits=0, operands=0, vmem=20):
    specs = {}
    if waits:
        specs["in_specs"] = [pl.BlockSpec(memory_space=pltpu.VMEM)] * (operands - waits) + [
            pl.BlockSpec(memory_space=pl.ANY)
        ] * waits
    return pl.pallas_call(
        kernel,
        out_shape=out_shape,
        scratch_shapes=list(scratch),
        compiler_params=pltpu.CompilerParams(vmem_limit_bytes=vmem * 1024 * 1024),
        cost_estimate=pl.CostEstimate(flops=flops, bytes_accessed=nbytes, transcendentals=0),
        **specs,
    )


def shape(dims, dtype=BF16):
    return jax.ShapeDtypeStruct(dims, dtype)


def input_kernel(x, gates, routes, out_o):
    rows, width = x.shape
    half = rows // 2
    core = lax.rem(lax.axis_index("tensor"), 2)
    start = pl.multiple_of(core * half, half)
    high = gates[...].astype(BF16).astype(F32)
    low = gates[...] - high
    meta = jnp.concatenate(
        [routes[...].astype(F32), high, low, jnp.zeros((rows - 6, rows), F32)], axis=0
    )
    out_o[:, 0:width] = x[pl.ds(start, half), :]
    columns = meta.T
    out_o[:, width:] = jnp.where(core == 0, columns[0:half], columns[half:]).astype(BF16)


def cotangent_kernel(c, after, out_o):
    half = c.shape[0] // 2
    core = lax.rem(lax.axis_index("tensor"), 2)
    out_o[...] = c[pl.ds(pl.multiple_of(core * half, half), half), :]


def gather_rows(whole, own_ref, near, far, core):
    half = own_ref.shape[0] // 2
    whole[0 : 2 * half, :] = own_ref[...]
    for r in range(3):
        start = 2 * half * (r + 1)
        whole[pl.ds(pl.multiple_of(start + core * half, half), half), :] = near[r][:, 0:1024]
        whole[pl.ds(pl.multiple_of(start + (1 - core) * half, half), half), :] = far[r][:, 0:1024]


def forward_kernel(*refs):
    (xo, x1, x2, x3, y1, y2, y3, gates, routes, p0, p1, p2, p3, up, down) = refs[:15]
    keep, send0, send1, send2, cross_o, act_o, dfac_o, gram_o, pick_o, gate_o, pair_o = refs[15:26]
    whole, flipped, info, partial, half_gram = refs[26:]
    j = lax.axis_index("tensor")
    core = lax.rem(j, 2)
    xi = j // 2
    first = lax.axis_index("expert") * 2
    near, far = (x1, x2, x3), (y1, y2, y3)
    gather_rows(whole, xo, near, far, core)
    for r in range(3):
        start = 128 * r
        info[pl.ds(pl.multiple_of(start + core * 64, 64), 64), :] = near[r][:, 1024:]
        info[pl.ds(pl.multiple_of(start + (1 - core) * 64, 64), 64), :] = far[r][:, 1024:]
    for k, piece in enumerate((p0, p1, p2, p3)):
        at = pl.multiple_of((j ^ k) * 256, 256)
        for e in range(2):
            pair_o[e, :, pl.ds(at, 256)] = piece[e]
    others = info[...].astype(F32).T
    mine_info = jnp.concatenate([routes[...].astype(F32), gates[...]], axis=0)
    there = jnp.concatenate([others[0:2], others[2:4] + others[4:6]], axis=0)
    meta = jnp.concatenate([mine_info, there], axis=1)
    tokens = meta.shape[1]
    before = (
        lax.broadcasted_iota(jnp.int32, (tokens, tokens), 0)
        < lax.broadcasted_iota(jnp.int32, (tokens, tokens), 1)
    ).astype(F32).astype(BF16)
    a = lax.broadcasted_iota(jnp.int32, (256, 144), 0)
    n = lax.broadcasted_iota(jnp.int32, (256, 144), 1)
    low = jnp.minimum(a // 16, a % 16)
    high = jnp.maximum(a // 16, a % 16)
    spread = jnp.where(low * 16 - low * (low - 1) // 2 + high - low == n, 1.0, 0.0).astype(BF16)
    half_gram[136:144, :] = jnp.zeros((8, 256), F32)
    for e in range(2):
        mine = (first + e).astype(F32)
        s0 = meta[0:1, :] == mine
        s1 = meta[1:2, :] == mine
        named = jnp.where(s0, 1.0, 0.0) + jnp.where(s1, 1.0, 0.0)
        gate = jnp.where(s0, meta[2:3, :], 0.0) + jnp.where(s1, meta[3:4, :], 0.0)
        place = mm(jnp.broadcast_to(named, (8, tokens)).astype(BF16), before)[0:1, :]
        place = jnp.where(named > 0.5, place, -1.0)
        slot = lax.broadcasted_iota(jnp.int32, (256, tokens), 0).astype(F32)
        hit = slot == place
        pick = jnp.where(hit, 1.0, 0.0).astype(BF16)
        gate_o[e] = jnp.broadcast_to(
            jnp.sum(jnp.where(hit, gate, 0.0), axis=1, keepdims=True), (256, 128)
        )
        pick_o[e] = pick
        rows = mm(pick, whole[...])
        flipped[...] = rows.T

        at = 0
        for i in range(16):
            left = flipped[i * 64 : i * 64 + 64, :]
            for q in range(i, 16):
                prod = left * flipped[q * 64 : q * 64 + 64, :]
                part = jnp.sum(prod.reshape(8, 8, 256), axis=0)
                for lane in range(2):
                    partial[lane, at * 8 : at * 8 + 8, :] = part[:, lane * 128 : lane * 128 + 128]
                at += 1
        for g in range(17):
            for lane in range(2):
                acc = partial[lane, pl.ds(g * 64, 8, stride=8), :]
                for q in range(1, 8):
                    acc = acc + partial[lane, pl.ds(g * 64 + q, 8, stride=8), :]
                half_gram[g * 8 : g * 8 + 8, lane * 128 : lane * 128 + 128] = acc * (1.0 / DE)
        gram_o[e] = mm(spread, half_gram[...].astype(BF16)).astype(BF16)
        cross = (rows + mm(gram_o[e], pair_o[e], TN)).astype(BF16)
        cross_o[e] = cross
        pre = mm(cross, up[e])
        sig = jax.nn.sigmoid(pre)
        act = (pre * sig).astype(BF16)
        act_o[e] = act
        dfac_o[e] = sig * (1.0 + pre * (1.0 - sig))
        for xr in range(2):
            for part in range(2):
                block = 2 * (xi ^ xr) + (core ^ part)
                at = pl.multiple_of(block * 256, 256)
                term = mm(act, down[e, :, pl.ds(at, 256)]).astype(BF16)
                if part == 1 and xr == 1:
                    (send1, send2)[e][...] = term
                else:
                    (keep.at[xr], send0)[part][e * 256 : e * 256 + 256, :] = term


def backward_kernel(*refs):
    (co, c1, c2, c3, d1, d2, d3, pick, gate, dfac, pair, up, down, after) = refs[:14]
    keep, send0, send1, send2, grad_o, pre_o = refs[14:20]
    whole, terms = refs[20:]
    j = lax.axis_index("tensor")
    core = lax.rem(j, 2)
    xi = j // 2
    gather_rows(whole, co, (c1, c2, c3), (d1, d2, d3), core)
    a = lax.broadcasted_iota(jnp.int32, (256, 256), 0)
    b = lax.broadcasted_iota(jnp.int32, (256, 256), 1)
    swapped = (a % 16) * 16 + a // 16
    both = (jnp.where(a == b, 1.0, 0.0) + jnp.where(swapped == b, 1.0, 0.0)).astype(BF16)
    for e in range(2):
        grad = (gate[e][:, 0:1] * mm(pick[e], whole[...])).astype(BF16)
        grad_o[e] = grad
        grad_act = mm(grad, down[e], NT)
        pre = (grad_act * dfac[e]).astype(BF16)
        pre_o[e] = pre
        terms[...] = mm(pre, up[e], NT).astype(BF16)
        back = mm(pair[e], terms[...], NT).astype(BF16)
        back = mm(both, back).astype(BF16)
        wide = back.reshape(4, 64, 256)
        for xr in range(2):
            for part in range(2):
                block = 2 * (xi ^ xr) + (core ^ part)
                at = pl.multiple_of(block * 256, 256)
                if part == 1 and xr == 1:
                    dst, row = (send1, send2)[e], 0
                else:
                    dst, row = (keep.at[xr], send0)[part], e * 320
                dst[row : row + 256, :] = terms[:, pl.ds(at, 256)]
                for q in range(4):
                    def put(dst=dst, row=row, q=q):
                        dst[row + 256 : row + 320, :] = wide[q]

                    pl.when(block == q)(put)


def weights_kernel(act, grad, cross, pre, down_o, up_o):
    for e in range(2):
        down_o[e] = mm(act[e], grad[e], TN).astype(BF16)
        up_o[e] = mm(cross[e], pre[e], TN).astype(BF16)


def add2(a, b):
    return (a.astype(F32) + b.astype(F32)).astype(BF16)


def mixed_kernel(mine, other, theirs, pick, gate, out_o):
    total = jnp.zeros((512, 256), F32)
    for e in range(2):
        at = slice(e * 256, e * 256 + 256)
        rows = add2(add2(mine[0, at, :], other[at, :]), theirs[at, :]).astype(F32)
        rows = (rows * gate[e][:, 0:1]).astype(BF16)
        total = total + mm(pick[e], rows, TN)
    total = total.astype(BF16)
    for r in range(4):
        out_o[r] = total[r * 128 : r * 128 + 128, :]


def combine_kernel(mine, other, theirs, pick, out_o, rows_o):
    total = jnp.zeros((512, 256), F32)
    back = jnp.zeros((64, 512), F32)
    for e in range(2):
        at = slice(e * 320, e * 320 + 320)
        both = add2(add2(mine[0, at, :], other[at, :]), theirs[at, :])
        rows = both[0:256]
        rows_o[e] = rows
        total = total + mm(pick[e], rows, TN)
        back = back + mm(both[256:320], pick[e])
    total = total.astype(BF16)
    back = back.astype(BF16)
    for r in range(4):
        out_o[r, 0:128, :] = total[r * 128 : r * 128 + 128, :]
        part = back[:, r * 128 : r * 128 + 128]
        out_o[r, 128:160, 0:128] = part[0:32]
        out_o[r, 128:160, 128:256] = part[32:64]


def pair_kernel(gram, rows, out_o):
    for e in range(2):
        out_o[e] = mm(gram[e], rows[e]).astype(BF16)


def final_kernel(x, c, n0, n1, n2, n3, g0, g1, g2, g3, mixed_o, grad_o, flipped):
    j = lax.axis_index("tensor")
    at = pl.multiple_of(j * 256, 256)
    total = x[:, pl.ds(at, 256)].astype(F32)
    for n in (n0, n1, n2, n3):
        total = total + n[...].astype(F32)
    mixed_o[...] = total.astype(BF16)
    flipped[...] = x[...].astype(F32).T
    total = c[:, pl.ds(at, 256)].astype(F32)
    back = jnp.zeros((32, 256), F32)
    for g in (g0, g1, g2, g3):
        total = total + g[0:128, :].astype(F32)
        back = back + g[128:160, :].astype(F32)
    back = jnp.concatenate([back[:, 0:128], back[:, 128:256]], axis=0)
    pieces = []
    for i in range(4):
        acc = jnp.zeros((64, 128), F32)
        for q in range(16):
            acc = acc + back[i * 16 + q : i * 16 + q + 1, :] * flipped[q * 64 : q * 64 + 64, :]
        pieces.append(acc)
    gram_back = jnp.concatenate(pieces, axis=0) * (1.0 / DE)
    grad_o[...] = (total + gram_back.T).astype(BF16)


def swap(value, axis, mask):
    size = lax.axis_size(axis)
    return lax.ppermute(value, axis, [(i, i ^ mask) for i in range(size)])


def gathered_body(inputs, cotangent, gate_values, routes, pair_weight, up_weight, down_weight):
    half = inputs.shape[0] // 2
    width = inputs.shape[1]
    gates, choices = gate_values.T, routes.T
    x_half = kernel_call(input_kernel, shape((half, width + 128)))(inputs, gates, choices)
    x_near = [swap(x_half, "expert", r) for r in (1, 2, 3)]
    pair_x = swap(pair_weight, "tensor", 2)
    pair_c = swap(pair_weight, "tensor", 1)
    x_far = [swap(v, "tensor", 1) for v in x_near]
    pair_d = swap(pair_x, "tensor", 1)
    c_half = kernel_call(cotangent_kernel, shape((half, width)), waits=1, operands=2)(cotangent, x_near[0])
    c_near = [swap(c_half, "expert", r) for r in (1, 2, 3)]
    forward = kernel_call(
        forward_kernel,
        (
            shape((2, 512, 256)),
            shape((512, 256)),
            shape((256, 256)),
            shape((256, 256)),
            shape((2, 256, 1024)),
            shape((2, 256, 512)),
            shape((2, 256, 512), F32),
            shape((2, 256, 256)),
            shape((2, 256, 512)),
            shape((2, 256, 128), F32),
            shape((2, 256, 1024)),
        ),
        scratch=[
            pltpu.VMEM((512, 1024), BF16),
            pltpu.VMEM((1024, 256), F32),
            pltpu.VMEM((384, 128), BF16),
            pltpu.VMEM((2, 1088, 128), F32),
            pltpu.VMEM((144, 256), F32),
        ],
        flops=4_000_000_000,
        nbytes=10_000_000,
    )
    keep, send0, send1, send2, cross, act, dfac, gram, pick, gate, pair_all = forward(
        inputs, *x_near, *x_far, gates, choices, pair_weight, pair_c, pair_x, pair_d, up_weight, down_weight
    )
    got_here = swap(send0, "tensor", 1)
    got_away = [swap(v, "tensor", 1) for v in (send1, send2)]
    out_away = add2(keep[1], jnp.concatenate(got_away, axis=0))
    out_there = swap(out_away, "tensor", 2)
    c_far = [swap(v, "tensor", 1) for v in c_near]
    backward = kernel_call(
        backward_kernel,
        (
            shape((2, 640, 256)),
            shape((640, 256)),
            shape((320, 256)),
            shape((320, 256)),
            shape((2, 256, 1024)),
            shape((2, 256, 512)),
        ),
        scratch=[pltpu.VMEM((512, 1024), BF16), pltpu.VMEM((256, 1024), BF16)],
        waits=1,
        operands=14,
        flops=2_000_000_000,
        nbytes=10_000_000,
    )
    bkeep, bsend0, bsend1, bsend2, grad, pre = backward(
        cotangent, *c_near, *c_far, pick, gate, dfac, pair_all, up_weight, down_weight, out_away
    )
    bgot_here = swap(bsend0, "tensor", 1)
    bgot_away = [swap(v, "tensor", 1) for v in (bsend1, bsend2)]
    back_there = swap(add2(bkeep[1], jnp.concatenate(bgot_away, axis=0)), "tensor", 2)
    mixed_parts = kernel_call(
        mixed_kernel, shape((4, 128, 256)), flops=300_000_000, nbytes=2_000_000
    )(keep, got_here, out_there, pick, gate)
    mixed_got = [mixed_parts[0]] + [swap(mixed_parts[r], "expert", r) for r in (1, 2, 3)]
    grad_down, grad_up = kernel_call(
        weights_kernel,
        (shape((2, 512, 1024)), shape((2, 1024, 512))),
        flops=3_000_000_000,
        nbytes=8_000_000,
    )(act, grad, cross, pre)
    grad_parts, rows = kernel_call(
        combine_kernel,
        (shape((4, 160, 256)), shape((2, 256, 256))),
        flops=300_000_000,
        nbytes=2_000_000,
    )(bkeep, bgot_here, back_there, pick)
    grad_got = [grad_parts[0]] + [swap(grad_parts[r], "expert", r) for r in (1, 2, 3)]
    grad_pair = kernel_call(
        pair_kernel, shape((2, 256, 256)), flops=300_000_000, nbytes=2_000_000
    )(gram, rows)
    mixed, grad_input = kernel_call(
        final_kernel,
        (shape((128, 256)), shape((128, 256))),
        scratch=[pltpu.VMEM((1024, 128), F32)],
        flops=100_000_000,
        nbytes=1_000_000,
    )(inputs, cotangent, *mixed_got, *grad_got)
    return mixed, grad_input, grad_pair, grad_up, grad_down


def solution(mesh):
    placed = (
        P(("group", "expert"), None),
        P(("group", "expert"), None),
        P(("group", "expert"), None),
        P(("group", "expert"), None),
        P("expert", None, "tensor"),
        P("expert", None, "tensor"),
        P("expert", "tensor", None),
    )
    small = mesh.shape["expert"] == 4 and mesh.shape["tensor"] == 4
    return jax.shard_map(
        gathered_body if small else body,
        mesh=mesh,
        in_specs=placed,
        out_specs=(
            P(("group", "expert"), "tensor"),
            P(("group", "expert"), "tensor"),
            P(("group", "expert"), None, "tensor"),
            P(("group", "expert"), None, "tensor"),
            P(("group", "expert"), "tensor", None),
        ),
        check_vma=False,
    )
```

```python
import functools

import jax
import jax.numpy as jnp
from jax import lax
from jax.experimental import pallas as pl
from jax.experimental.pallas import tpu as pltpu
from jax.sharding import PartitionSpec as P

NF = 16
DE = 64


def dispatch_tables(routes, expert_total, capacity):
    row_count, pick_count = routes.shape
    flat_ids = routes.reshape(-1)
    onehot = (flat_ids[:, None] == jnp.arange(expert_total, dtype=jnp.int32)[None, :]).astype(
        jnp.int32
    )
    before = jnp.cumsum(onehot, axis=0) - onehot
    position = jnp.sum(before * onehot, axis=1)
    slot_index = flat_ids * capacity + position
    slot_count = expert_total * capacity
    tables = slot_index[:, None] == jnp.arange(slot_count, dtype=jnp.int32)[None, :]
    tables = tables.reshape(row_count, pick_count, slot_count)
    return jnp.transpose(tables, (1, 2, 0)).astype(jnp.bfloat16)


def body(inputs, cotangent, gate_values, routes, pair_weight, up_weight, down_weight):
    local_count = up_weight.shape[0]
    expert_count = lax.axis_size("expert")
    tensor_count = lax.axis_size("tensor")
    expert_total = local_count * expert_count
    row_count, pick_count = routes.shape
    feature_width = inputs.shape[1]
    capacity = 2 * row_count * pick_count // expert_total
    expert_rows = expert_count * capacity
    part_width = feature_width // tensor_count
    tensor_index = lax.axis_index("tensor")
    feature_start = tensor_index * part_width
    tables = dispatch_tables(routes, expert_total, capacity)
    any_table = jnp.sum(tables, axis=0)
    scaled = (gate_values[:, :, None] * cotangent[:, None, :].astype(jnp.float32)).astype(
        jnp.bfloat16
    )
    input_slice = lax.dynamic_slice_in_dim(inputs, feature_start, part_width, 1)
    cotangent_slice = lax.dynamic_slice_in_dim(cotangent, feature_start, part_width, 1)
    input_slots = jnp.dot(any_table, inputs, preferred_element_type=jnp.float32).astype(
        jnp.bfloat16
    )
    grad_slots = jnp.einsum(
        "ksr,rkd->sd", tables, scaled, preferred_element_type=jnp.float32
    ).astype(jnp.bfloat16)
    send_shape = (expert_count, local_count, capacity, feature_width)
    input_homes, grad_homes = (
        lax.all_to_all(
            input_slots.reshape(send_shape), "expert", split_axis=0, concat_axis=2, tiled=True
        ),
        lax.all_to_all(
            grad_slots.reshape(send_shape), "expert", split_axis=0, concat_axis=2, tiled=True
        ),
    )
    input_rows = input_homes.reshape(local_count, expert_rows, feature_width)
    grad_rows = grad_homes.reshape(local_count, expert_rows, feature_width)
    cells = jnp.transpose(input_rows.reshape(local_count, expert_rows, NF, DE), (0, 2, 3, 1))
    gram = jnp.einsum("eidr,ejdr->eijr", cells, cells, preferred_element_type=jnp.float32) / DE
    gram_flat = gram.reshape(local_count, NF * NF, expert_rows).astype(jnp.bfloat16)
    input_mine = lax.dynamic_slice_in_dim(input_rows, feature_start, part_width, 2)
    cross_sum = input_mine.astype(jnp.float32) + jnp.einsum(
        "epr,epd->erd", gram_flat, pair_weight, preferred_element_type=jnp.float32
    )
    cross_part = cross_sum.astype(jnp.bfloat16)
    cross_whole = lax.all_gather(cross_part, "tensor", axis=2, tiled=True)
    hidden_pre = jnp.einsum(
        "erd,edh->erh", cross_whole, up_weight, preferred_element_type=jnp.float32
    )
    hidden_act = jax.nn.silu(hidden_pre).astype(jnp.bfloat16)
    out_terms = jnp.einsum(
        "erh,ehd->erd", hidden_act, down_weight, preferred_element_type=jnp.float32
    )
    out_mine = lax.psum_scatter(
        out_terms.astype(jnp.bfloat16), "tensor", scatter_dimension=2, tiled=True
    )
    grad_act = jnp.einsum(
        "erd,ehd->erh", grad_rows, down_weight, preferred_element_type=jnp.float32
    )
    sigmoid_pre = jax.nn.sigmoid(hidden_pre)
    grad_pre = (grad_act * sigmoid_pre * (1.0 + hidden_pre * (1.0 - sigmoid_pre))).astype(
        jnp.bfloat16
    )
    grad_down = jnp.einsum(
        "erh,erd->ehd", hidden_act, grad_rows, preferred_element_type=jnp.float32
    ).astype(jnp.bfloat16)
    grad_up = jnp.einsum(
        "erd,erh->edh", cross_whole, grad_pre, preferred_element_type=jnp.float32
    ).astype(jnp.bfloat16)
    cross_terms = jnp.einsum(
        "erh,edh->erd", grad_pre, up_weight, preferred_element_type=jnp.float32
    )
    grad_cross = lax.psum_scatter(
        cross_terms.astype(jnp.bfloat16), "tensor", scatter_dimension=2, tiled=True
    )
    grad_pair = jnp.einsum(
        "epr,erd->epd", gram_flat, grad_cross, preferred_element_type=jnp.float32
    ).astype(jnp.bfloat16)
    pair_terms = jnp.einsum(
        "erd,epd->epr", grad_cross, pair_weight, preferred_element_type=jnp.float32
    )
    grad_gram = (
        lax.psum(pair_terms.astype(jnp.bfloat16), "tensor")
        .astype(jnp.float32)
        .reshape(local_count, NF, NF, expert_rows)
    )
    symmetric = grad_gram + jnp.swapaxes(grad_gram, 1, 2)
    field_count = part_width // DE
    symmetric_mine = lax.dynamic_slice_in_dim(symmetric, tensor_index * field_count, field_count, 1)
    gram_back = (
        jnp.einsum(
            "eijr,ejdr->eidr",
            symmetric_mine,
            cells.astype(jnp.float32),
            precision=lax.Precision.HIGHEST,
        )
        / DE
    )
    gram_back = jnp.transpose(gram_back, (0, 3, 1, 2)).reshape(local_count, expert_rows, part_width)
    grad_mine = (grad_cross.astype(jnp.float32) + gram_back).astype(jnp.bfloat16)
    back_shape = (1, local_count, expert_rows, part_width)
    out_back, grad_back = (
        lax.all_to_all(
            out_mine.reshape(back_shape), "expert", split_axis=2, concat_axis=0, tiled=True
        ),
        lax.all_to_all(
            grad_mine.reshape(back_shape), "expert", split_axis=2, concat_axis=0, tiled=True
        ),
    )
    out_back = out_back.reshape(expert_total * capacity, part_width)
    grad_back = grad_back.reshape(expert_total * capacity, part_width)
    picked = jnp.einsum("ksr,sd->rkd", tables, out_back, preferred_element_type=jnp.float32)
    mixed = (
        input_slice.astype(jnp.float32) + jnp.sum(gate_values[:, :, None] * picked, axis=1)
    ).astype(jnp.bfloat16)
    grad_input = (
        cotangent_slice.astype(jnp.float32)
        + jnp.dot(any_table.T, grad_back, preferred_element_type=jnp.float32)
    ).astype(jnp.bfloat16)
    return (mixed, grad_input, grad_pair, grad_up, grad_down)


F32 = jnp.float32
BF16 = jnp.bfloat16
NT = (((1,), (1,)), ((), ()))
TN = (((0,), (0,)), ((), ()))
WIDTH = 1024
HALF = 64


def mm(a, b, dims=None):
    if dims is None:
        return jnp.dot(a, b, preferred_element_type=F32)
    return lax.dot_general(a, b, dims, preferred_element_type=F32)


def kernel_call(kernel, out_shape, where, scratch=(), flops=0, nbytes=0, vmem=48):
    kinds = {"v": pltpu.VMEM, "a": pl.ANY, "h": pltpu.HBM}
    return pl.pallas_call(
        kernel,
        out_shape=out_shape,
        in_specs=[pl.BlockSpec(memory_space=kinds[w]) for w in where],
        scratch_shapes=list(scratch),
        compiler_params=pltpu.CompilerParams(vmem_limit_bytes=vmem * 1024 * 1024),
        cost_estimate=pl.CostEstimate(flops=flops, bytes_accessed=nbytes, transcendentals=0),
    )


def shape(dims, dtype=BF16):
    return jax.ShapeDtypeStruct(dims, dtype)


def load(pairs, sems):
    copies = [pltpu.make_async_copy(a, b, sems.at[n]) for n, (a, b) in enumerate(pairs)]
    for copy in copies:
        copy.start()
    return copies


def payload_kernel(x, c, gates_in, routes_in, pair_in, out_o, pair_o, gates, routes, sems):
    core = lax.rem(lax.axis_index("tensor"), 2)
    mine = pl.ds(pl.multiple_of(core * HALF, HALF), HALF)
    copies = load(
        [
            (gates_in, gates),
            (routes_in, routes),
            (x.at[mine, :], out_o.at[:, 0:WIDTH]),
            (c.at[mine, :], out_o.at[:, WIDTH : 2 * WIDTH]),
            (pair_in, pair_o),
        ],
        sems,
    )
    copies[0].wait()
    copies[1].wait()
    high = gates[...].astype(BF16).astype(F32)
    low = gates[...] - high
    meta = jnp.concatenate(
        [routes[...].astype(F32), high, low, jnp.zeros((122, 128), F32)], axis=0
    )
    columns = meta.T
    out_o[:, 2 * WIDTH :] = jnp.where(core == 0, columns[0:HALF], columns[HALF:]).astype(BF16)
    for copy in copies[2:]:
        copy.wait()


def join_kernel(a, b, after, out_o):
    out_o[0:HALF, :] = a[...]
    out_o[HALF : 2 * HALF, :] = b[...]


def place_rows(whole, info, block, core, near, far):
    for at, piece in ((core, near), (1 - core, far)):
        rows = pl.ds(pl.multiple_of(block * 128 + at * HALF, HALF), HALF)
        whole[rows, :] = piece[:, 0 : 2 * WIDTH]
        info[rows, :] = piece[:, 2 * WIDTH :]


def towers(meta, whole, up, down, ready, pair, outs, scratch):
    keep, send_here, send_away, send_last, cross_o, act_o, grad_o, pre_o, gram_o, pick_o, gate_o = outs
    flipped, partial, half_gram, terms = scratch
    j = lax.axis_index("tensor")
    core = lax.rem(j, 2)
    xi = j // 2
    first = lax.axis_index("expert") * 2
    tokens = meta.shape[1]
    before = (
        lax.broadcasted_iota(jnp.int32, (tokens, tokens), 0)
        < lax.broadcasted_iota(jnp.int32, (tokens, tokens), 1)
    ).astype(F32).astype(BF16)
    a = lax.broadcasted_iota(jnp.int32, (256, 144), 0)
    n = lax.broadcasted_iota(jnp.int32, (256, 144), 1)
    low = jnp.minimum(a // 16, a % 16)
    high = jnp.maximum(a // 16, a % 16)
    spread = jnp.where(low * 16 - low * (low - 1) // 2 + high - low == n, 1.0, 0.0).astype(BF16)
    a = lax.broadcasted_iota(jnp.int32, (256, 256), 0)
    b = lax.broadcasted_iota(jnp.int32, (256, 256), 1)
    swapped = (a % 16) * 16 + a // 16
    both = (jnp.where(a == b, 1.0, 0.0) + jnp.where(swapped == b, 1.0, 0.0)).astype(BF16)
    half_gram[136:144, :] = jnp.zeros((8, 128), F32)
    for e in range(2):
        mine = (first + e).astype(F32)
        s0 = meta[0:1, :] == mine
        s1 = meta[1:2, :] == mine
        named = jnp.where(s0, 1.0, 0.0) + jnp.where(s1, 1.0, 0.0)
        gate = jnp.where(s0, meta[2:3, :], 0.0) + jnp.where(s1, meta[3:4, :], 0.0)
        place = mm(jnp.broadcast_to(named, (8, tokens)).astype(BF16), before)[0:1, :]
        place = jnp.where(named > 0.5, place, -1.0)
        hit = lax.broadcasted_iota(jnp.int32, (128, tokens), 0).astype(F32) == place
        pick = jnp.where(hit, 1.0, 0.0).astype(BF16)
        weight = jnp.sum(jnp.where(hit, gate, 0.0), axis=1, keepdims=True)
        gate_o[e] = jnp.broadcast_to(weight, (128, 128))
        pick_o[e] = pick
        rows = mm(pick, whole[:, 0:WIDTH])
        grad = (weight * mm(pick, whole[:, WIDTH : 2 * WIDTH])).astype(BF16)
        grad_o[e] = grad
        flipped[...] = rows.T
        at = 0
        for i in range(16):
            left = flipped[i * 64 : i * 64 + 64, :]
            for q in range(i, 16):
                prod = left * flipped[q * 64 : q * 64 + 64, :]
                partial[at * 8 : at * 8 + 8, :] = jnp.sum(prod.reshape(8, 8, 128), axis=0)
                at += 1
        for g in range(17):
            acc = partial[pl.ds(g * 64, 8, stride=8), :]
            for q in range(1, 8):
                acc = acc + partial[pl.ds(g * 64 + q, 8, stride=8), :]
            half_gram[g * 8 : g * 8 + 8, :] = acc * (1.0 / DE)
        gram = mm(spread, half_gram[...].astype(BF16)).astype(BF16)
        gram_o[e] = gram
        cross = (rows + mm(gram, pair[e], TN)).astype(BF16)
        cross_o[e] = cross
        if e == 0:
            for copy in ready:
                copy.wait()
        pre = mm(cross, up[e])
        sig = jax.nn.sigmoid(pre)
        act = (pre * sig).astype(BF16)
        act_o[e] = act
        slope = sig * (1.0 + pre * (1.0 - sig))
        dpre = (mm(grad, down[e], NT) * slope).astype(BF16)
        pre_o[e] = dpre
        terms[...] = mm(dpre, up[e], NT).astype(BF16)
        back = mm(both, mm(pair[e], terms[...], NT).astype(BF16)).astype(BF16)
        for xr in (1, 0):
            for part in (1, 0):
                block = 2 * (xi ^ xr) + (core ^ part)
                cols = pl.ds(pl.multiple_of(block * 256, 256), 256)
                if part == 0:
                    low, high = keep.at[xr, 0:320], keep.at[xr, 320:576]
                elif xr == 0:
                    low, high = send_here.at[0:320], send_here.at[320:576]
                else:
                    low, high = send_away, send_last
                low[e * 128 : e * 128 + 128, :] = terms[:, cols]
                high[e * 128 : e * 128 + 128, :] = mm(act, down[e, :, cols]).astype(BF16)
                for q in range(4):
                    def put(low=low, q=q):
                        low[256:320, e * 128 : e * 128 + 128] = back[q * 64 : q * 64 + 64, :]

                    pl.when(block == q)(put)


def own_chunk_kernel(*refs):
    x, c, gates_in, routes_in, near, far, p0, p1, p2, p3, up_in, down_in = refs[:12]
    outs, pair_o = refs[12:23], refs[23]
    whole, info, gates, routes, up, down, sems = refs[24:31]
    j = lax.axis_index("tensor")
    copies = load(
        [
            (gates_in, gates),
            (routes_in, routes),
            (x, whole.at[0:128, 0:WIDTH]),
            (c, whole.at[0:128, WIDTH : 2 * WIDTH]),
            (up_in, up),
            (down_in, down),
        ],
        sems,
    )
    place_rows(whole, info, 1, lax.rem(j, 2), near, far)
    for k, piece in enumerate((p0, p1, p2, p3)):
        cols = pl.ds(pl.multiple_of((j ^ k) * 256, 256), 256)
        for e in range(2):
            pair_o[e, :, cols] = piece[e]
    for copy in copies[:4]:
        copy.wait()
    other = info[128:256, :].astype(F32).T
    meta = jnp.concatenate(
        [
            jnp.concatenate([routes[...].astype(F32), other[0:2]], axis=1),
            jnp.concatenate([gates[...], other[2:4] + other[4:6]], axis=1),
        ],
        axis=0,
    )
    towers(meta, whole, up, down, copies[4:], pair_o, outs, refs[31:])


def far_chunk_kernel(*refs):
    near, far, pair, up_in, down_in = refs[:5]
    outs = refs[5:16]
    whole, info, up, down, sems = refs[16:21]
    core = lax.rem(lax.axis_index("tensor"), 2)
    copies = load([(up_in, up), (down_in, down)], sems)
    for r in range(2):
        rows = slice(r * HALF, r * HALF + HALF)
        place_rows(whole, info, r, core, near.at[rows, :], far.at[rows, :])
    other = info[...].astype(F32).T
    meta = jnp.concatenate([other[0:2], other[2:4] + other[4:6]], axis=0)
    towers(meta, whole, up, down, copies, pair, outs, refs[21:])


def weights_kernel(act0, grad0, cross0, pre0, act1, grad1, cross1, pre1, down_o, up_o):
    def stack(a, b):
        return jnp.concatenate([a, b], axis=0)

    for e in range(2):
        down_o[e] = mm(stack(act0[e], act1[e]), stack(grad0[e], grad1[e]), TN).astype(BF16)
        up_o[e] = mm(stack(cross0[e], cross1[e]), stack(pre0[e], pre1[e]), TN).astype(BF16)


def add2(a, b):
    return (a.astype(F32) + b.astype(F32)).astype(BF16)


def combine_kernel(mine, other, theirs, pick, gate, first_o, second_o, rows_o):
    both = add2(add2(mine[0], other[...]), theirs[...])
    grads = jnp.zeros((256, 256), F32)
    mixed = jnp.zeros((256, 256), F32)
    back = jnp.zeros((64, 256), F32)
    for e in range(2):
        rows = both[e * 128 : e * 128 + 128]
        rows_o[e] = rows
        grads = grads + mm(pick[e], rows, TN)
        back = back + mm(both[256:320, e * 128 : e * 128 + 128], pick[e])
        out = both[320 + e * 128 : 448 + e * 128].astype(F32) * gate[e][:, 0:1]
        mixed = mixed + mm(pick[e], out.astype(BF16), TN)
    for p, dst in enumerate((first_o, second_o)):
        rows = slice(p * 128, p * 128 + 128)
        dst[0:128, :] = grads[rows].astype(BF16)
        part = back[:, rows].astype(BF16)
        dst[128:160, 0:128] = part[0:32]
        dst[128:160, 128:256] = part[32:64]
        dst[160:288, :] = mixed[rows].astype(BF16)


def pair_kernel(gram0, rows0, gram1, rows1, out_o):
    for e in range(2):
        out_o[e] = (mm(gram0[e], rows0[e]) + mm(gram1[e], rows1[e])).astype(BF16)


def final_kernel(x_in, c_in, g0, g1, g2, g3, mixed_o, grad_o, x, c, flipped, sems):
    copies = load([(x_in, x), (c_in, c)], sems)
    for copy in copies:
        copy.wait()
    cols = pl.ds(pl.multiple_of(lax.axis_index("tensor") * 256, 256), 256)
    mixed = x[:, cols].astype(F32)
    total = c[:, cols].astype(F32)
    back = jnp.zeros((32, 256), F32)
    for g in (g0, g1, g2, g3):
        total = total + g[0:128, :].astype(F32)
        back = back + g[128:160, :].astype(F32)
        mixed = mixed + g[160:288, :].astype(F32)
    mixed_o[...] = mixed.astype(BF16)
    flipped[...] = x[...].astype(F32).T
    back = jnp.concatenate([back[:, 0:128], back[:, 128:256]], axis=0)
    pieces = []
    for i in range(4):
        acc = jnp.zeros((64, 128), F32)
        for q in range(16):
            acc = acc + back[i * 16 + q : i * 16 + q + 1, :] * flipped[q * 64 : q * 64 + 64, :]
        pieces.append(acc)
    gram_back = jnp.concatenate(pieces, axis=0) * (1.0 / DE)
    grad_o[...] = (total + gram_back.T).astype(BF16)


def swap(value, axis, mask):
    size = lax.axis_size(axis)
    return lax.ppermute(value, axis, [(i, i ^ mask) for i in range(size)])


def chunk_outs():
    return (
        shape((2, 576, 256)),
        shape((576, 256)),
        shape((320, 256)),
        shape((256, 256)),
        shape((2, 128, 1024)),
        shape((2, 128, 512)),
        shape((2, 128, 1024)),
        shape((2, 128, 512)),
        shape((2, 256, 128)),
        shape((2, 128, 256)),
        shape((2, 128, 128), F32),
    )


def chunk_scratch():
    return [
        pltpu.VMEM((1024, 128), F32),
        pltpu.VMEM((1088, 128), F32),
        pltpu.VMEM((144, 128), F32),
        pltpu.VMEM((128, 1024), BF16),
    ]


def weight_scratch():
    return [pltpu.VMEM((2, 1024, 512), BF16), pltpu.VMEM((2, 512, 1024), BF16)]


def away_kernel(keep, low, high, *rest):
    out_o = rest[-1]
    rows = low.shape[0]
    out_o[0:rows, :] = add2(keep[1, 0:rows], low[...])
    out_o[rows:, :] = add2(keep[1, rows:], high[...])


def sums_over_tensor(keep, send_here, send_away, send_last, after=()):
    got = (swap(send_away, "tensor", 1), swap(send_last, "tensor", 1))
    add = kernel_call(away_kernel, shape((576, 256)), "vvv" + "a" * len(after))
    there = swap(add(keep, *got, *after), "tensor", 2)
    return swap(send_here, "tensor", 1), there


def gathered_body(inputs, cotangent, gate_values, routes, pair_weight, up_weight, down_weight):
    gates, choices = gate_values.T, routes.T
    payload, pair_own = kernel_call(
        payload_kernel,
        (shape((HALF, 2 * WIDTH + 128)), shape((2, 256, 256))),
        "hhhhh",
        scratch=[
            pltpu.VMEM((2, 128), F32),
            pltpu.VMEM((2, 128), jnp.int32),
            pltpu.SemaphoreType.DMA((5,)),
        ],
    )(inputs, cotangent, gates, choices, pair_weight)
    got = [swap(payload, "expert", 1), swap(payload, "expert", 2)]
    got.append(swap(got[1], "expert", 1))
    pair_x = swap(pair_own, "tensor", 2)
    pair_c = swap(pair_own, "tensor", 1)
    pair_d = swap(pair_x, "tensor", 1)
    near_other = swap(got[0], "tensor", 1)
    chunk = kernel_call(
        own_chunk_kernel,
        chunk_outs() + (shape((2, 256, 1024)),),
        "hhhhvvvvvvhh",
        scratch=[
            pltpu.VMEM((256, 2048), BF16),
            pltpu.VMEM((256, 128), BF16),
            pltpu.VMEM((2, 128), F32),
            pltpu.VMEM((2, 128), jnp.int32),
        ]
        + weight_scratch()
        + [pltpu.SemaphoreType.DMA((6,))]
        + chunk_scratch(),
        flops=4_000_000_000,
        nbytes=10_000_000,
    )(
        inputs, cotangent, gates, choices, got[0], near_other,
        pair_own, pair_c, pair_x, pair_d, up_weight, down_weight,
    )
    keep, here, away, last, cross, act, grad, pre, gram, pick, gate, pair_all = chunk
    other, theirs = sums_over_tensor(keep, here, away, last)
    part = shape((288, 256))
    combine = kernel_call(
        combine_kernel,
        (part, part, shape((2, 128, 256))),
        "vvvvv",
        flops=300_000_000,
        nbytes=2_000_000,
    )
    own_part, near_part, rows = combine(keep, other, theirs, pick, gate)
    far_mine = kernel_call(join_kernel, shape((2 * HALF, 2 * WIDTH + 128)), "vva")(
        got[1], got[2], gate
    )
    far_other = swap(far_mine, "tensor", 1)
    chunk = kernel_call(
        far_chunk_kernel,
        chunk_outs(),
        "vvvhh",
        scratch=[pltpu.VMEM((256, 2048), BF16), pltpu.VMEM((256, 128), BF16)]
        + weight_scratch()
        + [pltpu.SemaphoreType.DMA((2,))]
        + chunk_scratch(),
        flops=4_000_000_000,
        nbytes=10_000_000,
    )(far_mine, far_other, pair_all, up_weight, down_weight)
    fkeep, fhere, faway, flast, fcross, fact, fgrad, fpre, fgram, fpick, fgate = chunk
    fother, ftheirs = sums_over_tensor(fkeep, fhere, faway, flast, after=(theirs,))
    near_got = swap(near_part, "expert", 1)
    part2, part3, frows = combine(fkeep, fother, ftheirs, fpick, fgate)
    got2, got3 = swap(part2, "expert", 2), swap(part3, "expert", 3)
    grad_down, grad_up = kernel_call(
        weights_kernel,
        (shape((2, 512, 1024)), shape((2, 1024, 512))),
        "vvvvvvvv",
        flops=3_000_000_000,
        nbytes=8_000_000,
    )(act, grad, cross, pre, fact, fgrad, fcross, fpre)
    grad_pair = kernel_call(
        pair_kernel, shape((2, 256, 256)), "vvvv", flops=300_000_000, nbytes=2_000_000
    )(gram, rows, fgram, frows)
    mixed, grad_input = kernel_call(
        final_kernel,
        (shape((128, 256)), shape((128, 256))),
        "hhvvvv",
        scratch=[
            pltpu.VMEM((128, 1024), BF16),
            pltpu.VMEM((128, 1024), BF16),
            pltpu.VMEM((1024, 128), F32),
            pltpu.SemaphoreType.DMA((2,)),
        ],
        flops=100_000_000,
        nbytes=1_000_000,
    )(inputs, cotangent, own_part, near_got, got2, got3)
    return mixed, grad_input, grad_pair, grad_up, grad_down


def solution(mesh):
    placed = (
        P(("group", "expert"), None),
        P(("group", "expert"), None),
        P(("group", "expert"), None),
        P(("group", "expert"), None),
        P("expert", None, "tensor"),
        P("expert", None, "tensor"),
        P("expert", "tensor", None),
    )
    small = mesh.shape["expert"] == 4 and mesh.shape["tensor"] == 4
    return jax.shard_map(
        gathered_body if small else body,
        mesh=mesh,
        in_specs=placed,
        out_specs=(
            P(("group", "expert"), "tensor"),
            P(("group", "expert"), "tensor"),
            P(("group", "expert"), None, "tensor"),
            P(("group", "expert"), None, "tensor"),
            P(("group", "expert"), "tensor", None),
        ),
        check_vma=False,
    )
```

```python
import functools

import jax
import jax.numpy as jnp
from jax import lax
from jax.experimental import pallas as pl
from jax.experimental.pallas import tpu as pltpu
from jax.sharding import PartitionSpec as P

NF = 16
DE = 64


def dispatch_tables(routes, expert_total, capacity):
    row_count, pick_count = routes.shape
    flat_ids = routes.reshape(-1)
    onehot = (flat_ids[:, None] == jnp.arange(expert_total, dtype=jnp.int32)[None, :]).astype(
        jnp.int32
    )
    before = jnp.cumsum(onehot, axis=0) - onehot
    position = jnp.sum(before * onehot, axis=1)
    slot_index = flat_ids * capacity + position
    slot_count = expert_total * capacity
    tables = slot_index[:, None] == jnp.arange(slot_count, dtype=jnp.int32)[None, :]
    tables = tables.reshape(row_count, pick_count, slot_count)
    return jnp.transpose(tables, (1, 2, 0)).astype(jnp.bfloat16)


def body(inputs, cotangent, gate_values, routes, pair_weight, up_weight, down_weight):
    local_count = up_weight.shape[0]
    expert_count = lax.axis_size("expert")
    tensor_count = lax.axis_size("tensor")
    expert_total = local_count * expert_count
    row_count, pick_count = routes.shape
    feature_width = inputs.shape[1]
    capacity = 2 * row_count * pick_count // expert_total
    expert_rows = expert_count * capacity
    part_width = feature_width // tensor_count
    tensor_index = lax.axis_index("tensor")
    feature_start = tensor_index * part_width
    tables = dispatch_tables(routes, expert_total, capacity)
    any_table = jnp.sum(tables, axis=0)
    scaled = (gate_values[:, :, None] * cotangent[:, None, :].astype(jnp.float32)).astype(
        jnp.bfloat16
    )
    input_slice = lax.dynamic_slice_in_dim(inputs, feature_start, part_width, 1)
    cotangent_slice = lax.dynamic_slice_in_dim(cotangent, feature_start, part_width, 1)
    input_slots = jnp.dot(any_table, inputs, preferred_element_type=jnp.float32).astype(
        jnp.bfloat16
    )
    grad_slots = jnp.einsum(
        "ksr,rkd->sd", tables, scaled, preferred_element_type=jnp.float32
    ).astype(jnp.bfloat16)
    send_shape = (expert_count, local_count, capacity, feature_width)
    input_homes, grad_homes = (
        lax.all_to_all(
            input_slots.reshape(send_shape), "expert", split_axis=0, concat_axis=2, tiled=True
        ),
        lax.all_to_all(
            grad_slots.reshape(send_shape), "expert", split_axis=0, concat_axis=2, tiled=True
        ),
    )
    input_rows = input_homes.reshape(local_count, expert_rows, feature_width)
    grad_rows = grad_homes.reshape(local_count, expert_rows, feature_width)
    cells = jnp.transpose(input_rows.reshape(local_count, expert_rows, NF, DE), (0, 2, 3, 1))
    gram = jnp.einsum("eidr,ejdr->eijr", cells, cells, preferred_element_type=jnp.float32) / DE
    gram_flat = gram.reshape(local_count, NF * NF, expert_rows).astype(jnp.bfloat16)
    input_mine = lax.dynamic_slice_in_dim(input_rows, feature_start, part_width, 2)
    cross_sum = input_mine.astype(jnp.float32) + jnp.einsum(
        "epr,epd->erd", gram_flat, pair_weight, preferred_element_type=jnp.float32
    )
    cross_part = cross_sum.astype(jnp.bfloat16)
    cross_whole = lax.all_gather(cross_part, "tensor", axis=2, tiled=True)
    hidden_pre = jnp.einsum(
        "erd,edh->erh", cross_whole, up_weight, preferred_element_type=jnp.float32
    )
    hidden_act = jax.nn.silu(hidden_pre).astype(jnp.bfloat16)
    out_terms = jnp.einsum(
        "erh,ehd->erd", hidden_act, down_weight, preferred_element_type=jnp.float32
    )
    out_mine = lax.psum_scatter(
        out_terms.astype(jnp.bfloat16), "tensor", scatter_dimension=2, tiled=True
    )
    grad_act = jnp.einsum(
        "erd,ehd->erh", grad_rows, down_weight, preferred_element_type=jnp.float32
    )
    sigmoid_pre = jax.nn.sigmoid(hidden_pre)
    grad_pre = (grad_act * sigmoid_pre * (1.0 + hidden_pre * (1.0 - sigmoid_pre))).astype(
        jnp.bfloat16
    )
    grad_down = jnp.einsum(
        "erh,erd->ehd", hidden_act, grad_rows, preferred_element_type=jnp.float32
    ).astype(jnp.bfloat16)
    grad_up = jnp.einsum(
        "erd,erh->edh", cross_whole, grad_pre, preferred_element_type=jnp.float32
    ).astype(jnp.bfloat16)
    cross_terms = jnp.einsum(
        "erh,edh->erd", grad_pre, up_weight, preferred_element_type=jnp.float32
    )
    grad_cross = lax.psum_scatter(
        cross_terms.astype(jnp.bfloat16), "tensor", scatter_dimension=2, tiled=True
    )
    grad_pair = jnp.einsum(
        "epr,erd->epd", gram_flat, grad_cross, preferred_element_type=jnp.float32
    ).astype(jnp.bfloat16)
    pair_terms = jnp.einsum(
        "erd,epd->epr", grad_cross, pair_weight, preferred_element_type=jnp.float32
    )
    grad_gram = (
        lax.psum(pair_terms.astype(jnp.bfloat16), "tensor")
        .astype(jnp.float32)
        .reshape(local_count, NF, NF, expert_rows)
    )
    symmetric = grad_gram + jnp.swapaxes(grad_gram, 1, 2)
    field_count = part_width // DE
    symmetric_mine = lax.dynamic_slice_in_dim(symmetric, tensor_index * field_count, field_count, 1)
    gram_back = (
        jnp.einsum(
            "eijr,ejdr->eidr",
            symmetric_mine,
            cells.astype(jnp.float32),
            precision=lax.Precision.HIGHEST,
        )
        / DE
    )
    gram_back = jnp.transpose(gram_back, (0, 3, 1, 2)).reshape(local_count, expert_rows, part_width)
    grad_mine = (grad_cross.astype(jnp.float32) + gram_back).astype(jnp.bfloat16)
    back_shape = (1, local_count, expert_rows, part_width)
    out_back, grad_back = (
        lax.all_to_all(
            out_mine.reshape(back_shape), "expert", split_axis=2, concat_axis=0, tiled=True
        ),
        lax.all_to_all(
            grad_mine.reshape(back_shape), "expert", split_axis=2, concat_axis=0, tiled=True
        ),
    )
    out_back = out_back.reshape(expert_total * capacity, part_width)
    grad_back = grad_back.reshape(expert_total * capacity, part_width)
    picked = jnp.einsum("ksr,sd->rkd", tables, out_back, preferred_element_type=jnp.float32)
    mixed = (
        input_slice.astype(jnp.float32) + jnp.sum(gate_values[:, :, None] * picked, axis=1)
    ).astype(jnp.bfloat16)
    grad_input = (
        cotangent_slice.astype(jnp.float32)
        + jnp.dot(any_table.T, grad_back, preferred_element_type=jnp.float32)
    ).astype(jnp.bfloat16)
    return (mixed, grad_input, grad_pair, grad_up, grad_down)


F32 = jnp.float32
BF16 = jnp.bfloat16
NT = (((1,), (1,)), ((), ()))
TN = (((0,), (0,)), ((), ()))
WIDTH = 1024
HALF = 64


def mm(a, b, dims=None):
    if dims is None:
        return jnp.dot(a, b, preferred_element_type=F32)
    return lax.dot_general(a, b, dims, preferred_element_type=F32)


def kernel_call(kernel, out_shape, where, scratch=(), flops=0, nbytes=0, vmem=48):
    kinds = {"v": pltpu.VMEM, "a": pl.ANY, "h": pltpu.HBM}
    return pl.pallas_call(
        kernel,
        out_shape=out_shape,
        in_specs=[pl.BlockSpec(memory_space=kinds[w]) for w in where],
        scratch_shapes=list(scratch),
        compiler_params=pltpu.CompilerParams(vmem_limit_bytes=vmem * 1024 * 1024),
        cost_estimate=pl.CostEstimate(flops=flops, bytes_accessed=nbytes, transcendentals=0),
    )


def shape(dims, dtype=BF16):
    return jax.ShapeDtypeStruct(dims, dtype)


def load(pairs, sems):
    copies = [pltpu.make_async_copy(a, b, sems.at[n]) for n, (a, b) in enumerate(pairs)]
    for copy in copies:
        copy.start()
    return copies


def payload_kernel(x, c, gates_in, routes_in, pair_in, out_o, own_o, pair_o, gates, routes, sems):
    core = lax.rem(lax.axis_index("tensor"), 2)
    mine = pl.ds(pl.multiple_of(core * HALF, HALF), HALF)
    copies = load(
        [
            (gates_in, gates),
            (routes_in, routes),
            (x.at[mine, :], out_o.at[:, 0:WIDTH]),
            (c.at[mine, :], out_o.at[:, WIDTH : 2 * WIDTH]),
            (x, own_o.at[:, 0:WIDTH]),
            (c, own_o.at[:, WIDTH : 2 * WIDTH]),
            (pair_in, pair_o),
        ],
        sems,
    )
    copies[0].wait()
    copies[1].wait()
    high = gates[...].astype(BF16).astype(F32)
    low = gates[...] - high
    meta = jnp.concatenate(
        [routes[...].astype(F32), high, low, jnp.zeros((122, 128), F32)], axis=0
    )
    columns = meta.T
    own_o[:, 2 * WIDTH :] = columns.astype(BF16)
    out_o[:, 2 * WIDTH :] = jnp.where(core == 0, columns[0:HALF], columns[HALF:]).astype(BF16)
    for copy in copies[2:]:
        copy.wait()


def join_kernel(a, b, after, out_o):
    out_o[0:HALF, :] = a[...]
    out_o[HALF : 2 * HALF, :] = b[...]


def place_rows(whole, info, block, core, near, far):
    for at, piece in ((core, near), (1 - core, far)):
        rows = pl.ds(pl.multiple_of(block * 128 + at * HALF, HALF), HALF)
        whole[rows, :] = piece[:, 0 : 2 * WIDTH]
        info[rows, :] = piece[:, 2 * WIDTH :]


def towers(meta, whole, up, down, ready, pair, outs, scratch):
    keep, send_here, send_away, send_last, cross_o, act_o, grad_o, pre_o, gram_o, pick_o, gate_o = outs
    flipped, partial, half_gram, terms, rows, slope, outs_s, backs = scratch
    j = lax.axis_index("tensor")
    core = lax.rem(j, 2)
    xi = j // 2
    first = lax.axis_index("expert") * 2
    tokens = meta.shape[1]
    before = (
        lax.broadcasted_iota(jnp.int32, (tokens, tokens), 0)
        < lax.broadcasted_iota(jnp.int32, (tokens, tokens), 1)
    ).astype(F32).astype(BF16)
    a = lax.broadcasted_iota(jnp.int32, (256, 144), 0)
    n = lax.broadcasted_iota(jnp.int32, (256, 144), 1)
    low = jnp.minimum(a // 16, a % 16)
    high = jnp.maximum(a // 16, a % 16)
    spread = jnp.where(low * 16 - low * (low - 1) // 2 + high - low == n, 1.0, 0.0).astype(BF16)
    a = lax.broadcasted_iota(jnp.int32, (256, 256), 0)
    b = lax.broadcasted_iota(jnp.int32, (256, 256), 1)
    swapped = (a % 16) * 16 + a // 16
    both = (jnp.where(a == b, 1.0, 0.0) + jnp.where(swapped == b, 1.0, 0.0)).astype(BF16)
    slots = lax.broadcasted_iota(jnp.int32, (128, tokens), 0).astype(F32)
    both_e = range(2)
    for e in both_e:
        mine = (first + e).astype(F32)
        s0 = meta[0:1, :] == mine
        s1 = meta[1:2, :] == mine
        named = jnp.where(s0, 1.0, 0.0) + jnp.where(s1, 1.0, 0.0)
        gate = jnp.where(s0, meta[2:3, :], 0.0) + jnp.where(s1, meta[3:4, :], 0.0)
        place = mm(jnp.broadcast_to(named, (8, tokens)).astype(BF16), before)[0:1, :]
        place = jnp.where(named > 0.5, place, -1.0)
        hit = slots == place
        pick_o[e] = jnp.where(hit, 1.0, 0.0).astype(BF16)
        weight = jnp.sum(jnp.where(hit, gate, 0.0), axis=1, keepdims=True)
        gate_o[e] = jnp.broadcast_to(weight, (128, 128))
    for e in both_e:
        rows[e] = mm(pick_o[e], whole[:, 0:WIDTH])
    for e in both_e:
        flipped[e] = rows[e].T
    for e in both_e:
        grad = mm(pick_o[e], whole[:, WIDTH : 2 * WIDTH])
        grad_o[e] = (gate_o[e][:, 0:1] * grad).astype(BF16)
    for e in both_e:
        half_gram[e, 136:144, :] = jnp.zeros((8, 128), F32)
        at = 0
        for i in range(16):
            left = flipped[e, i * 64 : i * 64 + 64, :]
            for q in range(i, 16):
                prod = left * flipped[e, q * 64 : q * 64 + 64, :]
                partial[e, at * 8 : at * 8 + 8, :] = jnp.sum(prod.reshape(8, 8, 128), axis=0)
                at += 1
        for g in range(17):
            acc = partial[e, pl.ds(g * 64, 8, stride=8), :]
            for q in range(1, 8):
                acc = acc + partial[e, pl.ds(g * 64 + q, 8, stride=8), :]
            half_gram[e, g * 8 : g * 8 + 8, :] = acc * (1.0 / DE)
        gram_o[e] = mm(spread, half_gram[e].astype(BF16)).astype(BF16)
    for e in both_e:
        cross_o[e] = (rows[e] + mm(gram_o[e], pair[e], TN)).astype(BF16)
    for copy in ready:
        copy.wait()
    for e in both_e:
        slope[e] = mm(grad_o[e], down[e], NT)
    for e in both_e:
        pre = mm(cross_o[e], up[e])
        sig = jax.nn.sigmoid(pre)
        act_o[e] = (pre * sig).astype(BF16)
        pre_o[e] = (slope[e] * sig * (1.0 + pre * (1.0 - sig))).astype(BF16)
    for e in both_e:
        terms[e] = mm(pre_o[e], up[e], NT).astype(BF16)
    for e in both_e:
        outs_s[e] = mm(act_o[e], down[e]).astype(BF16)
    for e in both_e:
        back = mm(pair[e], terms[e], NT).astype(BF16)
        backs[e] = mm(both, back).astype(BF16)
    for xr in (1, 0):
        for part in (1, 0):
            block = 2 * (xi ^ xr) + (core ^ part)
            cols = pl.ds(pl.multiple_of(block * 256, 256), 256)
            if part == 0:
                low, high = keep.at[xr, 0:320], keep.at[xr, 320:576]
            elif xr == 0:
                low, high = send_here.at[0:320], send_here.at[320:576]
            else:
                low, high = send_away, send_last
            for e in both_e:
                mine = slice(e * 128, e * 128 + 128)
                low[mine, :] = terms[e, :, cols]
                high[mine, :] = outs_s[e, :, cols]
                rows64 = pl.ds(pl.multiple_of(block * 64, 64), 64)
                low[256:320, mine] = backs[e, rows64, :]


def read_meta(info):
    rows = info[...].astype(F32).T
    return jnp.concatenate([rows[0:2], rows[2:4] + rows[4:6]], axis=0)


def own_chunk_kernel(*refs):
    own, near, far, p0, p1, x0, x1, d0, d1, up_in, down_in = refs[:11]
    outs, pair_o = refs[11:22], refs[22]
    whole, info, up, down, sems = refs[23:28]
    j = lax.axis_index("tensor")
    copies = load([(up_in, up), (down_in, down)], sems)
    whole[0:128, :] = own[:, 0 : 2 * WIDTH]
    info[0:128, :] = own[:, 2 * WIDTH :]
    place_rows(whole, info, 1, lax.rem(j, 2), near, far)
    for k, piece in enumerate((p0, p1, (x0, x1), (d0, d1))):
        cols = pl.ds(pl.multiple_of((j ^ k) * 256, 256), 256)
        for e in range(2):
            pair_o[e, :, cols] = piece[e][...]
    towers(read_meta(info), whole, up, down, copies, pair_o, outs, refs[28:])


def far_chunk_kernel(*refs):
    near, far, pair, up_in, down_in = refs[:5]
    outs = refs[5:16]
    whole, info, up, down, sems = refs[16:21]
    core = lax.rem(lax.axis_index("tensor"), 2)
    copies = load([(up_in, up), (down_in, down)], sems)
    for r in range(2):
        rows = slice(r * HALF, r * HALF + HALF)
        place_rows(whole, info, r, core, near.at[rows, :], far.at[rows, :])
    towers(read_meta(info), whole, up, down, copies, pair, outs, refs[21:])


def weights_kernel(act0, grad0, cross0, pre0, act1, grad1, cross1, pre1, down_o, up_o, done_o):
    done_o[...] = jnp.zeros((8, 128), F32)

    def stack(a, b):
        return jnp.concatenate([a, b], axis=0)

    for e in range(2):
        down_o[e] = mm(stack(act0[e], act1[e]), stack(grad0[e], grad1[e]), TN).astype(BF16)
        up_o[e] = mm(stack(cross0[e], cross1[e]), stack(pre0[e], pre1[e]), TN).astype(BF16)


def add2(a, b):
    return (a.astype(F32) + b.astype(F32)).astype(BF16)


def combine_kernel(mine, other, theirs, pick, gate, *rest):
    first_o, second_o, rows_o = rest[-3:]
    both = add2(add2(mine[0], other[...]), theirs[...])
    grads = jnp.zeros((256, 256), F32)
    mixed = jnp.zeros((256, 256), F32)
    back = jnp.zeros((64, 256), F32)
    for e in range(2):
        rows = both[e * 128 : e * 128 + 128]
        rows_o[e] = rows
        grads = grads + mm(pick[e], rows, TN)
        back = back + mm(both[256:320, e * 128 : e * 128 + 128], pick[e])
        out = both[320 + e * 128 : 448 + e * 128].astype(F32) * gate[e][:, 0:1]
        mixed = mixed + mm(pick[e], out.astype(BF16), TN)
    for p, dst in enumerate((first_o, second_o)):
        rows = slice(p * 128, p * 128 + 128)
        dst[0:128, :] = grads[rows].astype(BF16)
        part = back[:, rows].astype(BF16)
        dst[128:160, 0:128] = part[0:32]
        dst[128:160, 128:256] = part[32:64]
        dst[160:288, :] = mixed[rows].astype(BF16)


def pair_kernel(gram0, rows0, gram1, rows1, out_o):
    for e in range(2):
        out_o[e] = (mm(gram0[e], rows0[e]) + mm(gram1[e], rows1[e])).astype(BF16)


def final_kernel(own, g0, g1, g2, g3, mixed_o, grad_o, flipped):
    column = pl.multiple_of(lax.axis_index("tensor") * 256, 256)
    mixed = own[:, pl.ds(column, 256)].astype(F32)
    total = own[:, pl.ds(WIDTH + column, 256)].astype(F32)
    back = jnp.zeros((32, 256), F32)
    for g in (g0, g1, g2, g3):
        total = total + g[0:128, :].astype(F32)
        back = back + g[128:160, :].astype(F32)
        mixed = mixed + g[160:288, :].astype(F32)
    mixed_o[...] = mixed.astype(BF16)
    flipped[...] = own[:, 0:WIDTH].astype(F32).T
    back = jnp.concatenate([back[:, 0:128], back[:, 128:256]], axis=0)
    pieces = []
    for i in range(4):
        acc = jnp.zeros((64, 128), F32)
        for q in range(16):
            acc = acc + back[i * 16 + q : i * 16 + q + 1, :] * flipped[q * 64 : q * 64 + 64, :]
        pieces.append(acc)
    gram_back = jnp.concatenate(pieces, axis=0) * (1.0 / DE)
    grad_o[...] = (total + gram_back.T).astype(BF16)


def swap(value, axis, mask):
    size = lax.axis_size(axis)
    return lax.ppermute(value, axis, [(i, i ^ mask) for i in range(size)])


def chunk_outs():
    return (
        shape((2, 576, 256)),
        shape((576, 256)),
        shape((320, 256)),
        shape((256, 256)),
        shape((2, 128, 1024)),
        shape((2, 128, 512)),
        shape((2, 128, 1024)),
        shape((2, 128, 512)),
        shape((2, 256, 128)),
        shape((2, 128, 256)),
        shape((2, 128, 128), F32),
    )


def chunk_scratch():
    return [
        pltpu.VMEM((2, 1024, 128), F32),
        pltpu.VMEM((2, 1088, 128), F32),
        pltpu.VMEM((2, 144, 128), F32),
        pltpu.VMEM((2, 128, 1024), BF16),
        pltpu.VMEM((2, 128, 1024), F32),
        pltpu.VMEM((2, 128, 512), F32),
        pltpu.VMEM((2, 128, 1024), BF16),
        pltpu.VMEM((2, 256, 128), BF16),
    ]


def weight_scratch():
    return [pltpu.VMEM((2, 1024, 512), BF16), pltpu.VMEM((2, 512, 1024), BF16)]


def away_kernel(keep, low, high, *rest):
    out_o = rest[-1]
    rows = low.shape[0]
    out_o[0:rows, :] = add2(keep[1, 0:rows], low[...])
    out_o[rows:, :] = add2(keep[1, rows:], high[...])


def sums_over_tensor(keep, send_here, send_away, send_last, after=()):
    got = (swap(send_away, "tensor", 1), swap(send_last, "tensor", 1))
    add = kernel_call(away_kernel, shape((576, 256)), "vvv" + "a" * len(after))
    there = swap(add(keep, *got, *after), "tensor", 2)
    return swap(send_here, "tensor", 1), there


def gathered_body(inputs, cotangent, gate_values, routes, pair_weight, up_weight, down_weight):
    gates, choices = gate_values.T, routes.T
    width = 2 * WIDTH + 128
    payload, own, pair_own = kernel_call(
        payload_kernel,
        (shape((HALF, width)), shape((2 * HALF, width)), shape((2, 256, 256))),
        "hhhhh",
        scratch=[
            pltpu.VMEM((2, 128), F32),
            pltpu.VMEM((2, 128), jnp.int32),
            pltpu.SemaphoreType.DMA((7,)),
        ],
        vmem=60,
    )(inputs, cotangent, gates, choices, pair_weight)
    got = [swap(payload, "expert", 1), swap(payload, "expert", 2)]
    got.append(swap(got[1], "expert", 1))
    pair_x = [swap(pair_own[e], "tensor", 2) for e in range(2)]
    pair_c = swap(pair_own, "tensor", 1)
    pair_d = [swap(v, "tensor", 1) for v in pair_x]
    near_other = swap(got[0], "tensor", 1)
    chunk = kernel_call(
        own_chunk_kernel,
        chunk_outs() + (shape((2, 256, 1024)),),
        "vvvvvvvvvhh",
        scratch=[
            pltpu.VMEM((256, 2048), BF16),
            pltpu.VMEM((256, 128), BF16),
        ]
        + weight_scratch()
        + [pltpu.SemaphoreType.DMA((2,))]
        + chunk_scratch(),
        flops=4_000_000_000,
        nbytes=10_000_000,
    )(
        own, got[0], near_other,
        pair_own, pair_c, *pair_x, *pair_d, up_weight, down_weight,
    )
    keep, here, away, last, cross, act, grad, pre, gram, pick, gate, pair_all = chunk
    other, theirs = sums_over_tensor(keep, here, away, last)
    part = shape((288, 256))
    def combine(*operands):
        return kernel_call(
            combine_kernel,
            (part, part, shape((2, 128, 256))),
            "vvvvva"[: len(operands)],
            flops=300_000_000,
            nbytes=2_000_000,
        )(*operands)

    own_part, near_part, rows = combine(keep, other, theirs, pick, gate)
    far_mine = kernel_call(join_kernel, shape((2 * HALF, 2 * WIDTH + 128)), "vva")(
        got[1], got[2], gate
    )
    far_other = swap(far_mine, "tensor", 1)
    chunk = kernel_call(
        far_chunk_kernel,
        chunk_outs(),
        "vvvhh",
        scratch=[pltpu.VMEM((256, 2048), BF16), pltpu.VMEM((256, 128), BF16)]
        + weight_scratch()
        + [pltpu.SemaphoreType.DMA((2,))]
        + chunk_scratch(),
        flops=4_000_000_000,
        nbytes=10_000_000,
    )(far_mine, far_other, pair_all, up_weight, down_weight)
    fkeep, fhere, faway, flast, fcross, fact, fgrad, fpre, fgram, fpick, fgate = chunk
    fother, ftheirs = sums_over_tensor(fkeep, fhere, faway, flast, after=(theirs,))
    near_got = swap(near_part, "expert", 1)
    grad_down, grad_up, weights_done = kernel_call(
        weights_kernel,
        (shape((2, 512, 1024)), shape((2, 1024, 512)), shape((8, 128), F32)),
        "vvvvvvvv",
        flops=3_000_000_000,
        nbytes=8_000_000,
    )(act, grad, cross, pre, fact, fgrad, fcross, fpre)
    part2, part3, frows = combine(
        fkeep, fother, ftheirs, fpick, fgate, weights_done
    )
    got2, got3 = swap(part2, "expert", 2), swap(part3, "expert", 3)
    grad_pair = kernel_call(
        pair_kernel, shape((2, 256, 256)), "vvvv", flops=300_000_000, nbytes=2_000_000
    )(gram, rows, fgram, frows)
    mixed, grad_input = kernel_call(
        final_kernel,
        (shape((128, 256)), shape((128, 256))),
        "vvvvv",
        scratch=[pltpu.VMEM((1024, 128), F32)],
        flops=100_000_000,
        nbytes=1_000_000,
    )(own, own_part, near_got, got2, got3)
    return mixed, grad_input, grad_pair, grad_up, grad_down


def solution(mesh):
    placed = (
        P(("group", "expert"), None),
        P(("group", "expert"), None),
        P(("group", "expert"), None),
        P(("group", "expert"), None),
        P("expert", None, "tensor"),
        P("expert", None, "tensor"),
        P("expert", "tensor", None),
    )
    small = mesh.shape["expert"] == 4 and mesh.shape["tensor"] == 4
    return jax.shard_map(
        gathered_body if small else body,
        mesh=mesh,
        in_specs=placed,
        out_specs=(
            P(("group", "expert"), "tensor"),
            P(("group", "expert"), "tensor"),
            P(("group", "expert"), None, "tensor"),
            P(("group", "expert"), None, "tensor"),
            P(("group", "expert"), "tensor", None),
        ),
        check_vma=False,
    )
```

```python
import functools

import jax
import jax.numpy as jnp
from jax import lax
from jax.experimental import pallas as pl
from jax.experimental.pallas import tpu as pltpu
from jax.sharding import PartitionSpec as P

NF = 16
DE = 64


def dispatch_tables(routes, expert_total, capacity):
    row_count, pick_count = routes.shape
    flat_ids = routes.reshape(-1)
    onehot = (flat_ids[:, None] == jnp.arange(expert_total, dtype=jnp.int32)[None, :]).astype(
        jnp.int32
    )
    before = jnp.cumsum(onehot, axis=0) - onehot
    position = jnp.sum(before * onehot, axis=1)
    slot_index = flat_ids * capacity + position
    slot_count = expert_total * capacity
    tables = slot_index[:, None] == jnp.arange(slot_count, dtype=jnp.int32)[None, :]
    tables = tables.reshape(row_count, pick_count, slot_count)
    return jnp.transpose(tables, (1, 2, 0)).astype(jnp.bfloat16)


def body(inputs, cotangent, gate_values, routes, pair_weight, up_weight, down_weight):
    local_count = up_weight.shape[0]
    expert_count = lax.axis_size("expert")
    tensor_count = lax.axis_size("tensor")
    expert_total = local_count * expert_count
    row_count, pick_count = routes.shape
    feature_width = inputs.shape[1]
    capacity = 2 * row_count * pick_count // expert_total
    expert_rows = expert_count * capacity
    part_width = feature_width // tensor_count
    tensor_index = lax.axis_index("tensor")
    feature_start = tensor_index * part_width
    tables = dispatch_tables(routes, expert_total, capacity)
    any_table = jnp.sum(tables, axis=0)
    scaled = (gate_values[:, :, None] * cotangent[:, None, :].astype(jnp.float32)).astype(
        jnp.bfloat16
    )
    input_slice = lax.dynamic_slice_in_dim(inputs, feature_start, part_width, 1)
    cotangent_slice = lax.dynamic_slice_in_dim(cotangent, feature_start, part_width, 1)
    input_slots = jnp.dot(any_table, inputs, preferred_element_type=jnp.float32).astype(
        jnp.bfloat16
    )
    grad_slots = jnp.einsum(
        "ksr,rkd->sd", tables, scaled, preferred_element_type=jnp.float32
    ).astype(jnp.bfloat16)
    send_shape = (expert_count, local_count, capacity, feature_width)
    input_homes, grad_homes = (
        lax.all_to_all(
            input_slots.reshape(send_shape), "expert", split_axis=0, concat_axis=2, tiled=True
        ),
        lax.all_to_all(
            grad_slots.reshape(send_shape), "expert", split_axis=0, concat_axis=2, tiled=True
        ),
    )
    input_rows = input_homes.reshape(local_count, expert_rows, feature_width)
    grad_rows = grad_homes.reshape(local_count, expert_rows, feature_width)
    cells = jnp.transpose(input_rows.reshape(local_count, expert_rows, NF, DE), (0, 2, 3, 1))
    gram = jnp.einsum("eidr,ejdr->eijr", cells, cells, preferred_element_type=jnp.float32) / DE
    gram_flat = gram.reshape(local_count, NF * NF, expert_rows).astype(jnp.bfloat16)
    input_mine = lax.dynamic_slice_in_dim(input_rows, feature_start, part_width, 2)
    cross_sum = input_mine.astype(jnp.float32) + jnp.einsum(
        "epr,epd->erd", gram_flat, pair_weight, preferred_element_type=jnp.float32
    )
    cross_part = cross_sum.astype(jnp.bfloat16)
    cross_whole = lax.all_gather(cross_part, "tensor", axis=2, tiled=True)
    hidden_pre = jnp.einsum(
        "erd,edh->erh", cross_whole, up_weight, preferred_element_type=jnp.float32
    )
    hidden_act = jax.nn.silu(hidden_pre).astype(jnp.bfloat16)
    out_terms = jnp.einsum(
        "erh,ehd->erd", hidden_act, down_weight, preferred_element_type=jnp.float32
    )
    out_mine = lax.psum_scatter(
        out_terms.astype(jnp.bfloat16), "tensor", scatter_dimension=2, tiled=True
    )
    grad_act = jnp.einsum(
        "erd,ehd->erh", grad_rows, down_weight, preferred_element_type=jnp.float32
    )
    sigmoid_pre = jax.nn.sigmoid(hidden_pre)
    grad_pre = (grad_act * sigmoid_pre * (1.0 + hidden_pre * (1.0 - sigmoid_pre))).astype(
        jnp.bfloat16
    )
    grad_down = jnp.einsum(
        "erh,erd->ehd", hidden_act, grad_rows, preferred_element_type=jnp.float32
    ).astype(jnp.bfloat16)
    grad_up = jnp.einsum(
        "erd,erh->edh", cross_whole, grad_pre, preferred_element_type=jnp.float32
    ).astype(jnp.bfloat16)
    cross_terms = jnp.einsum(
        "erh,edh->erd", grad_pre, up_weight, preferred_element_type=jnp.float32
    )
    grad_cross = lax.psum_scatter(
        cross_terms.astype(jnp.bfloat16), "tensor", scatter_dimension=2, tiled=True
    )
    grad_pair = jnp.einsum(
        "epr,erd->epd", gram_flat, grad_cross, preferred_element_type=jnp.float32
    ).astype(jnp.bfloat16)
    pair_terms = jnp.einsum(
        "erd,epd->epr", grad_cross, pair_weight, preferred_element_type=jnp.float32
    )
    grad_gram = (
        lax.psum(pair_terms.astype(jnp.bfloat16), "tensor")
        .astype(jnp.float32)
        .reshape(local_count, NF, NF, expert_rows)
    )
    symmetric = grad_gram + jnp.swapaxes(grad_gram, 1, 2)
    field_count = part_width // DE
    symmetric_mine = lax.dynamic_slice_in_dim(symmetric, tensor_index * field_count, field_count, 1)
    gram_back = (
        jnp.einsum(
            "eijr,ejdr->eidr",
            symmetric_mine,
            cells.astype(jnp.float32),
            precision=lax.Precision.HIGHEST,
        )
        / DE
    )
    gram_back = jnp.transpose(gram_back, (0, 3, 1, 2)).reshape(local_count, expert_rows, part_width)
    grad_mine = (grad_cross.astype(jnp.float32) + gram_back).astype(jnp.bfloat16)
    back_shape = (1, local_count, expert_rows, part_width)
    out_back, grad_back = (
        lax.all_to_all(
            out_mine.reshape(back_shape), "expert", split_axis=2, concat_axis=0, tiled=True
        ),
        lax.all_to_all(
            grad_mine.reshape(back_shape), "expert", split_axis=2, concat_axis=0, tiled=True
        ),
    )
    out_back = out_back.reshape(expert_total * capacity, part_width)
    grad_back = grad_back.reshape(expert_total * capacity, part_width)
    picked = jnp.einsum("ksr,sd->rkd", tables, out_back, preferred_element_type=jnp.float32)
    mixed = (
        input_slice.astype(jnp.float32) + jnp.sum(gate_values[:, :, None] * picked, axis=1)
    ).astype(jnp.bfloat16)
    grad_input = (
        cotangent_slice.astype(jnp.float32)
        + jnp.dot(any_table.T, grad_back, preferred_element_type=jnp.float32)
    ).astype(jnp.bfloat16)
    return (mixed, grad_input, grad_pair, grad_up, grad_down)


F32 = jnp.float32
BF16 = jnp.bfloat16
NT = (((1,), (1,)), ((), ()))
TN = (((0,), (0,)), ((), ()))
WIDTH = 1024
HALF = 64


def mm(a, b, dims=None):
    if dims is None:
        return jnp.dot(a, b, preferred_element_type=F32)
    return lax.dot_general(a, b, dims, preferred_element_type=F32)


def kernel_call(kernel, out_shape, where, scratch=(), flops=0, nbytes=0, vmem=48):
    kinds = {"v": pltpu.VMEM, "a": pl.ANY, "h": pltpu.HBM}
    return pl.pallas_call(
        kernel,
        out_shape=out_shape,
        in_specs=[pl.BlockSpec(memory_space=kinds[w]) for w in where],
        scratch_shapes=list(scratch),
        compiler_params=pltpu.CompilerParams(vmem_limit_bytes=vmem * 1024 * 1024),
        cost_estimate=pl.CostEstimate(flops=flops, bytes_accessed=nbytes, transcendentals=0),
    )


def shape(dims, dtype=BF16):
    return jax.ShapeDtypeStruct(dims, dtype)


def load(pairs, sems):
    copies = [pltpu.make_async_copy(a, b, sems.at[n]) for n, (a, b) in enumerate(pairs)]
    for copy in copies:
        copy.start()
    return copies


def payload_kernel(x, c, gates_in, routes_in, pair_in, out_o, own_o, pair_o, gates, routes, sems):
    core = lax.rem(lax.axis_index("tensor"), 2)
    mine = pl.ds(pl.multiple_of(core * HALF, HALF), HALF)
    copies = load(
        [
            (gates_in, gates),
            (routes_in, routes),
            (x.at[mine, :], out_o.at[:, 0:WIDTH]),
            (c.at[mine, :], out_o.at[:, WIDTH : 2 * WIDTH]),
            (x, own_o.at[:, 0:WIDTH]),
            (c, own_o.at[:, WIDTH : 2 * WIDTH]),
            (pair_in, pair_o),
        ],
        sems,
    )
    copies[0].wait()
    copies[1].wait()
    high = gates[...].astype(BF16).astype(F32)
    low = gates[...] - high
    meta = jnp.concatenate(
        [routes[...].astype(F32), high, low, jnp.zeros((122, 128), F32)], axis=0
    )
    columns = meta.T
    own_o[:, 2 * WIDTH :] = columns.astype(BF16)
    out_o[:, 2 * WIDTH :] = jnp.where(core == 0, columns[0:HALF], columns[HALF:]).astype(BF16)
    for copy in copies[2:]:
        copy.wait()


def stage_kernel(pair_x, own, pair, pair_x_o, own_o, pair_o):
    pair_x_o[...] = pair_x[...]
    own_o[...] = own[...]
    pair_o[...] = pair[...]


def join_kernel(a, b, after, out_o):
    out_o[0:HALF, :] = a[...]
    out_o[HALF : 2 * HALF, :] = b[...]


def place_rows(whole, info, block, core, near, far):
    for at, piece in ((core, near), (1 - core, far)):
        rows = pl.ds(pl.multiple_of(block * 128 + at * HALF, HALF), HALF)
        whole[rows, :] = piece[:, 0 : 2 * WIDTH]
        info[rows, :] = piece[:, 2 * WIDTH :]


def towers(meta, whole, up, down, ready, pair, outs, scratch):
    keep, send_here, send_away, send_last, cross_o, act_o, grad_o, pre_o, gram_o, pick_o, gate_o = outs
    flipped, partial, half_gram, terms, rows, slope, outs_s, backs = scratch
    j = lax.axis_index("tensor")
    core = lax.rem(j, 2)
    xi = j // 2
    first = lax.axis_index("expert") * 2
    tokens = meta.shape[1]
    before = (
        lax.broadcasted_iota(jnp.int32, (tokens, tokens), 0)
        < lax.broadcasted_iota(jnp.int32, (tokens, tokens), 1)
    ).astype(F32).astype(BF16)
    a = lax.broadcasted_iota(jnp.int32, (256, 144), 0)
    n = lax.broadcasted_iota(jnp.int32, (256, 144), 1)
    low = jnp.minimum(a // 16, a % 16)
    high = jnp.maximum(a // 16, a % 16)
    spread = jnp.where(low * 16 - low * (low - 1) // 2 + high - low == n, 1.0, 0.0).astype(BF16)
    a = lax.broadcasted_iota(jnp.int32, (256, 256), 0)
    b = lax.broadcasted_iota(jnp.int32, (256, 256), 1)
    swapped = (a % 16) * 16 + a // 16
    both = (jnp.where(a == b, 1.0, 0.0) + jnp.where(swapped == b, 1.0, 0.0)).astype(BF16)
    slots = lax.broadcasted_iota(jnp.int32, (128, tokens), 0).astype(F32)
    both_e = range(2)
    for e in both_e:
        mine = (first + e).astype(F32)
        s0 = meta[0:1, :] == mine
        s1 = meta[1:2, :] == mine
        named = jnp.where(s0, 1.0, 0.0) + jnp.where(s1, 1.0, 0.0)
        gate = jnp.where(s0, meta[2:3, :], 0.0) + jnp.where(s1, meta[3:4, :], 0.0)
        place = mm(jnp.broadcast_to(named, (8, tokens)).astype(BF16), before)[0:1, :]
        place = jnp.where(named > 0.5, place, -1.0)
        hit = slots == place
        pick_o[e] = jnp.where(hit, 1.0, 0.0).astype(BF16)
        weight = jnp.sum(jnp.where(hit, gate, 0.0), axis=1, keepdims=True)
        gate_o[e] = jnp.broadcast_to(weight, (128, 128))
    for e in both_e:
        rows[e] = mm(pick_o[e], whole[:, 0:WIDTH])
    for e in both_e:
        flipped[e] = rows[e].T
    for e in both_e:
        grad = mm(pick_o[e], whole[:, WIDTH : 2 * WIDTH])
        grad_o[e] = (gate_o[e][:, 0:1] * grad).astype(BF16)
    for e in both_e:
        half_gram[e, 136:144, :] = jnp.zeros((8, 128), F32)
        at = 0
        for i in range(16):
            left = flipped[e, i * 64 : i * 64 + 64, :]
            for q in range(i, 16):
                prod = left * flipped[e, q * 64 : q * 64 + 64, :]
                partial[e, at * 8 : at * 8 + 8, :] = jnp.sum(prod.reshape(8, 8, 128), axis=0)
                at += 1
        for g in range(17):
            acc = partial[e, pl.ds(g * 64, 8, stride=8), :]
            for q in range(1, 8):
                acc = acc + partial[e, pl.ds(g * 64 + q, 8, stride=8), :]
            half_gram[e, g * 8 : g * 8 + 8, :] = acc * (1.0 / DE)
        gram_o[e] = mm(spread, half_gram[e].astype(BF16)).astype(BF16)
    for e in both_e:
        cross_o[e] = (rows[e] + mm(gram_o[e], pair[e], TN)).astype(BF16)
    for copy in ready:
        copy.wait()
    for e in both_e:
        slope[e] = mm(grad_o[e], down[e], NT)
    for e in both_e:
        pre = mm(cross_o[e], up[e])
        sig = jax.nn.sigmoid(pre)
        act_o[e] = (pre * sig).astype(BF16)
        pre_o[e] = (slope[e] * sig * (1.0 + pre * (1.0 - sig))).astype(BF16)
    for e in both_e:
        terms[e] = mm(pre_o[e], up[e], NT).astype(BF16)
    for e in both_e:
        outs_s[e] = mm(act_o[e], down[e]).astype(BF16)
    for e in both_e:
        back = mm(pair[e], terms[e], NT).astype(BF16)
        backs[e] = mm(both, back).astype(BF16)
    for xr in (1, 0):
        for part in (1, 0):
            block = 2 * (xi ^ xr) + (core ^ part)
            cols = pl.ds(pl.multiple_of(block * 256, 256), 256)
            if part == 0:
                low, high = keep.at[xr, 0:320], keep.at[xr, 320:576]
            elif xr == 0:
                low, high = send_here.at[0:320], send_here.at[320:576]
            else:
                low, high = send_away, send_last
            for e in both_e:
                mine = slice(e * 128, e * 128 + 128)
                low[mine, :] = terms[e, :, cols]
                high[mine, :] = outs_s[e, :, cols]
                rows64 = pl.ds(pl.multiple_of(block * 64, 64), 64)
                low[256:320, mine] = backs[e, rows64, :]


def read_meta(info):
    rows = info[...].astype(F32).T
    return jnp.concatenate([rows[0:2], rows[2:4] + rows[4:6]], axis=0)


def own_chunk_kernel(*refs):
    own, p0, near, far, p1, p2, p3, up_in, down_in = refs[:9]
    outs, pair_o = refs[9:20], refs[20]
    whole, info, up, down, sems = refs[21:26]
    j = lax.axis_index("tensor")
    copies = load([(up_in, up), (down_in, down)], sems)
    whole[0:128, :] = own[:, 0 : 2 * WIDTH]
    info[0:128, :] = own[:, 2 * WIDTH :]
    place_rows(whole, info, 1, lax.rem(j, 2), near, far)
    for k, piece in enumerate((p0, p1, p2, p3)):
        cols = pl.ds(pl.multiple_of((j ^ k) * 256, 256), 256)
        for e in range(2):
            pair_o[e, :, cols] = piece[e]
    towers(read_meta(info), whole, up, down, copies, pair_o, outs, refs[26:])


def far_chunk_kernel(*refs):
    near, far, pair, up_in, down_in = refs[:5]
    outs = refs[5:16]
    whole, info, up, down, sems = refs[16:21]
    core = lax.rem(lax.axis_index("tensor"), 2)
    copies = load([(up_in, up), (down_in, down)], sems)
    for r in range(2):
        rows = slice(r * HALF, r * HALF + HALF)
        place_rows(whole, info, r, core, near.at[rows, :], far.at[rows, :])
    towers(read_meta(info), whole, up, down, copies, pair, outs, refs[21:])


def weights_kernel(act0, grad0, cross0, pre0, act1, grad1, cross1, pre1, down_o, up_o, done_o):
    done_o[...] = jnp.zeros((8, 128), F32)

    def stack(a, b):
        return jnp.concatenate([a, b], axis=0)

    for e in range(2):
        down_o[e] = mm(stack(act0[e], act1[e]), stack(grad0[e], grad1[e]), TN).astype(BF16)
        up_o[e] = mm(stack(cross0[e], cross1[e]), stack(pre0[e], pre1[e]), TN).astype(BF16)


def add2(a, b):
    return (a.astype(F32) + b.astype(F32)).astype(BF16)


def combine_grads(both, picks, rows_o):
    grads = jnp.zeros((256, 256), F32)
    back = jnp.zeros((64, 256), F32)
    for e in range(2):
        rows = both[e * 128 : e * 128 + 128]
        rows_o[e] = rows
        grads = grads + mm(picks[e], rows, TN)
        back = back + mm(both[256:320, e * 128 : e * 128 + 128], picks[e])
    return grads.astype(BF16), back.astype(BF16)


def put_grads(dst, grads, back, p):
    rows = slice(p * 128, p * 128 + 128)
    dst[0:128, :] = grads[rows]
    dst[128:160, 0:128] = back[0:32, rows]
    dst[128:160, 128:256] = back[32:64, rows]


def combine_outs(both, picks, gates):
    mixed = jnp.zeros((256, 256), F32)
    for e in range(2):
        out = both[e * 128 : e * 128 + 128].astype(F32) * gates[e][:, 0:1]
        mixed = mixed + mm(picks[e], out.astype(BF16), TN)
    return mixed.astype(BF16)


def combine_kernel(mine, other, theirs, pick, gate, first_o, second_o, rows_o):
    both = add2(add2(mine[0], other[...]), theirs[...])
    grads, back = combine_grads(both[0:320], pick, rows_o)
    mixed = combine_outs(both[320:576], pick, gate)
    for p, dst in enumerate((first_o, second_o)):
        put_grads(dst, grads, back, p)
        dst[160:288, :] = mixed[p * 128 : p * 128 + 128]


def far_grads_kernel(mine, other, theirs, pick, after, first_o, second_o, rows_o):
    both = add2(add2(mine[0, 0:320], other[0:320]), theirs[...])
    grads, back = combine_grads(both, pick, rows_o)
    for p, dst in enumerate((first_o, second_o)):
        put_grads(dst, grads, back, p)


def far_outs_kernel(mine, other, theirs, pick, gate, first_o, second_o):
    both = add2(add2(mine[0, 320:576], other[320:576]), theirs[...])
    mixed = combine_outs(both, pick, gate)
    first_o[...] = mixed[0:128]
    second_o[...] = mixed[128:256]


def sum_kernel(a, b, out_o):
    out_o[...] = add2(a[...], b[...])


def pair_kernel(gram0, rows0, gram1, rows1, out_o):
    for e in range(2):
        out_o[e] = (mm(gram0[e], rows0[e]) + mm(gram1[e], rows1[e])).astype(BF16)


def final_kernel(own, g0, g1, far_grads, far_outs, mixed_o, grad_o, flipped):
    column = pl.multiple_of(lax.axis_index("tensor") * 256, 256)
    mixed = own[:, pl.ds(column, 256)].astype(F32) + far_outs[...].astype(F32)
    total = own[:, pl.ds(WIDTH + column, 256)].astype(F32)
    back = jnp.zeros((32, 256), F32)
    for g in (g0, g1, far_grads):
        total = total + g[0:128, :].astype(F32)
        back = back + g[128:160, :].astype(F32)
    for g in (g0, g1):
        mixed = mixed + g[160:288, :].astype(F32)
    mixed_o[...] = mixed.astype(BF16)
    flipped[...] = own[:, 0:WIDTH].astype(F32).T
    back = jnp.concatenate([back[:, 0:128], back[:, 128:256]], axis=0)
    pieces = []
    for i in range(4):
        acc = jnp.zeros((64, 128), F32)
        for q in range(16):
            acc = acc + back[i * 16 + q : i * 16 + q + 1, :] * flipped[q * 64 : q * 64 + 64, :]
        pieces.append(acc)
    gram_back = jnp.concatenate(pieces, axis=0) * (1.0 / DE)
    grad_o[...] = (total + gram_back.T).astype(BF16)


def swap(value, axis, mask):
    size = lax.axis_size(axis)
    return lax.ppermute(value, axis, [(i, i ^ mask) for i in range(size)])


def chunk_outs():
    return (
        shape((2, 576, 256)),
        shape((576, 256)),
        shape((320, 256)),
        shape((256, 256)),
        shape((2, 128, 1024)),
        shape((2, 128, 512)),
        shape((2, 128, 1024)),
        shape((2, 128, 512)),
        shape((2, 256, 128)),
        shape((2, 128, 256)),
        shape((2, 128, 128), F32),
    )


def chunk_scratch():
    return [
        pltpu.VMEM((2, 1024, 128), F32),
        pltpu.VMEM((2, 1088, 128), F32),
        pltpu.VMEM((2, 144, 128), F32),
        pltpu.VMEM((2, 128, 1024), BF16),
        pltpu.VMEM((2, 128, 1024), F32),
        pltpu.VMEM((2, 128, 512), F32),
        pltpu.VMEM((2, 128, 1024), BF16),
        pltpu.VMEM((2, 256, 128), BF16),
    ]


def weight_scratch():
    return [pltpu.VMEM((2, 1024, 512), BF16), pltpu.VMEM((2, 512, 1024), BF16)]


def away_kernel(keep, low, high, out_o):
    out_o[0:320, :] = add2(keep[1, 0:320], low[...])
    out_o[320:576, :] = add2(keep[1, 320:576], high[...])


def away_grads_kernel(keep, low, after, out_o):
    out_o[...] = add2(keep[1, 0:320], low[...])


def away_outs_kernel(keep, high, after, out_o):
    out_o[...] = add2(keep[1, 320:576], high[...])


def gathered_body(inputs, cotangent, gate_values, routes, pair_weight, up_weight, down_weight):
    gates, choices = gate_values.T, routes.T
    width = 2 * WIDTH + 128
    payload, own, pair_own = kernel_call(
        payload_kernel,
        (
            shape((HALF, width)),
            shape((2 * HALF, width)),
            shape((2, 256, 256)),
        ),
        "hhhhh",
        scratch=[
            pltpu.VMEM((2, 128), F32),
            pltpu.VMEM((2, 128), jnp.int32),
            pltpu.SemaphoreType.DMA((7,)),
        ],
        vmem=60,
    )(inputs, cotangent, gates, choices, pair_weight)
    got = [swap(payload, "expert", 1), swap(payload, "expert", 2)]
    got.append(swap(got[1], "expert", 1))
    both = shape((2, 256, 256))
    pair_x, own, pair_own = kernel_call(
        stage_kernel, (both, shape((2 * HALF, width)), both), "vvv"
    )(swap(pair_own, "tensor", 2), own, pair_own)
    pair_c = swap(pair_own, "tensor", 1)
    pair_d = swap(pair_x, "tensor", 1)
    near_other = swap(got[0], "tensor", 1)
    chunk = kernel_call(
        own_chunk_kernel,
        chunk_outs() + (shape((2, 256, 1024)),),
        "vvvvvvvhh",
        scratch=[
            pltpu.VMEM((256, 2048), BF16),
            pltpu.VMEM((256, 128), BF16),
        ]
        + weight_scratch()
        + [pltpu.SemaphoreType.DMA((2,))]
        + chunk_scratch(),
        flops=4_000_000_000,
        nbytes=10_000_000,
    )(
        own, pair_own, got[0], near_other,
        pair_c, pair_x, pair_d, up_weight, down_weight,
    )
    keep, here, away, last, cross, act, grad, pre, gram, pick, gate, pair_all = chunk
    away = kernel_call(away_kernel, shape((576, 256)), "vvv")(
        keep, swap(away, "tensor", 1), swap(last, "tensor", 1)
    )
    theirs = swap(away, "tensor", 2)
    other = swap(here, "tensor", 1)
    part = shape((288, 256))
    combine = kernel_call(
        combine_kernel,
        (part, part, shape((2, 128, 256))),
        "vvvvv",
        flops=300_000_000,
        nbytes=2_000_000,
    )
    own_part, near_part, rows = combine(keep, other, theirs, pick, gate)
    far_mine = kernel_call(join_kernel, shape((2 * HALF, 2 * WIDTH + 128)), "vva")(
        got[1], got[2], gate
    )
    far_other = swap(far_mine, "tensor", 1)
    chunk = kernel_call(
        far_chunk_kernel,
        chunk_outs(),
        "vvvhh",
        scratch=[pltpu.VMEM((256, 2048), BF16), pltpu.VMEM((256, 128), BF16)]
        + weight_scratch()
        + [pltpu.SemaphoreType.DMA((2,))]
        + chunk_scratch(),
        flops=4_000_000_000,
        nbytes=10_000_000,
    )(far_mine, far_other, pair_all, up_weight, down_weight)
    fkeep, fhere, faway, flast, fcross, fact, fgrad, fpre, fgram, fpick, fgate = chunk
    fother = swap(fhere, "tensor", 1)
    fgrads = kernel_call(away_grads_kernel, shape((320, 256)), "vva")(
        fkeep, swap(faway, "tensor", 1), theirs
    )
    fouts = kernel_call(away_outs_kernel, shape((256, 256)), "vva")(
        fkeep, swap(flast, "tensor", 1), fgrads
    )
    fgrads = swap(fgrads, "tensor", 2)
    fouts = swap(fouts, "tensor", 2)
    near_got = swap(near_part, "expert", 1)
    grad_down, grad_up, weights_done = kernel_call(
        weights_kernel,
        (shape((2, 512, 1024)), shape((2, 1024, 512)), shape((8, 128), F32)),
        "vvvvvvvv",
        flops=3_000_000_000,
        nbytes=8_000_000,
    )(act, grad, cross, pre, fact, fgrad, fcross, fpre)
    part = shape((160, 256))
    grads2, grads3, frows = kernel_call(
        far_grads_kernel, (part, part, shape((2, 128, 256))), "vvvva"
    )(fkeep, fother, fgrads, fpick, weights_done)
    grads2 = kernel_call(sum_kernel, part, "vv")(grads2, swap(grads3, "expert", 1))
    far_grads = swap(grads2, "expert", 2)
    part = shape((128, 256))
    outs2, outs3 = kernel_call(far_outs_kernel, (part, part), "vvvvv")(
        fkeep, fother, fouts, fpick, fgate
    )
    outs2 = kernel_call(sum_kernel, part, "vv")(outs2, swap(outs3, "expert", 1))
    far_outs = swap(outs2, "expert", 2)
    grad_pair = kernel_call(
        pair_kernel, shape((2, 256, 256)), "vvvv", flops=300_000_000, nbytes=2_000_000
    )(gram, rows, fgram, frows)
    mixed, grad_input = kernel_call(
        final_kernel,
        (shape((128, 256)), shape((128, 256))),
        "vvvvv",
        scratch=[pltpu.VMEM((1024, 128), F32)],
        flops=100_000_000,
        nbytes=1_000_000,
    )(own, own_part, near_got, far_grads, far_outs)
    return mixed, grad_input, grad_pair, grad_up, grad_down


def solution(mesh):
    placed = (
        P(("group", "expert"), None),
        P(("group", "expert"), None),
        P(("group", "expert"), None),
        P(("group", "expert"), None),
        P("expert", None, "tensor"),
        P("expert", None, "tensor"),
        P("expert", "tensor", None),
    )
    small = mesh.shape["expert"] == 4 and mesh.shape["tensor"] == 4
    return jax.shard_map(
        gathered_body if small else body,
        mesh=mesh,
        in_specs=placed,
        out_specs=(
            P(("group", "expert"), "tensor"),
            P(("group", "expert"), "tensor"),
            P(("group", "expert"), None, "tensor"),
            P(("group", "expert"), None, "tensor"),
            P(("group", "expert"), "tensor", None),
        ),
        check_vma=False,
    )
```

```python
import functools

import jax
import jax.numpy as jnp
from jax import lax
from jax.experimental import pallas as pl
from jax.experimental.pallas import tpu as pltpu
from jax.sharding import PartitionSpec as P

NF = 16
DE = 64


def dispatch_tables(routes, expert_total, capacity):
    row_count, pick_count = routes.shape
    flat_ids = routes.reshape(-1)
    onehot = (flat_ids[:, None] == jnp.arange(expert_total, dtype=jnp.int32)[None, :]).astype(
        jnp.int32
    )
    before = jnp.cumsum(onehot, axis=0) - onehot
    position = jnp.sum(before * onehot, axis=1)
    slot_index = flat_ids * capacity + position
    slot_count = expert_total * capacity
    tables = slot_index[:, None] == jnp.arange(slot_count, dtype=jnp.int32)[None, :]
    tables = tables.reshape(row_count, pick_count, slot_count)
    return jnp.transpose(tables, (1, 2, 0)).astype(jnp.bfloat16)


def body(inputs, cotangent, gate_values, routes, pair_weight, up_weight, down_weight):
    local_count = up_weight.shape[0]
    expert_count = lax.axis_size("expert")
    tensor_count = lax.axis_size("tensor")
    expert_total = local_count * expert_count
    row_count, pick_count = routes.shape
    feature_width = inputs.shape[1]
    capacity = 2 * row_count * pick_count // expert_total
    expert_rows = expert_count * capacity
    part_width = feature_width // tensor_count
    tensor_index = lax.axis_index("tensor")
    feature_start = tensor_index * part_width
    tables = dispatch_tables(routes, expert_total, capacity)
    any_table = jnp.sum(tables, axis=0)
    scaled = (gate_values[:, :, None] * cotangent[:, None, :].astype(jnp.float32)).astype(
        jnp.bfloat16
    )
    input_slice = lax.dynamic_slice_in_dim(inputs, feature_start, part_width, 1)
    cotangent_slice = lax.dynamic_slice_in_dim(cotangent, feature_start, part_width, 1)
    input_slots = jnp.dot(any_table, inputs, preferred_element_type=jnp.float32).astype(
        jnp.bfloat16
    )
    grad_slots = jnp.einsum(
        "ksr,rkd->sd", tables, scaled, preferred_element_type=jnp.float32
    ).astype(jnp.bfloat16)
    send_shape = (expert_count, local_count, capacity, feature_width)
    input_homes, grad_homes = (
        lax.all_to_all(
            input_slots.reshape(send_shape), "expert", split_axis=0, concat_axis=2, tiled=True
        ),
        lax.all_to_all(
            grad_slots.reshape(send_shape), "expert", split_axis=0, concat_axis=2, tiled=True
        ),
    )
    input_rows = input_homes.reshape(local_count, expert_rows, feature_width)
    grad_rows = grad_homes.reshape(local_count, expert_rows, feature_width)
    cells = jnp.transpose(input_rows.reshape(local_count, expert_rows, NF, DE), (0, 2, 3, 1))
    gram = jnp.einsum("eidr,ejdr->eijr", cells, cells, preferred_element_type=jnp.float32) / DE
    gram_flat = gram.reshape(local_count, NF * NF, expert_rows).astype(jnp.bfloat16)
    input_mine = lax.dynamic_slice_in_dim(input_rows, feature_start, part_width, 2)
    cross_sum = input_mine.astype(jnp.float32) + jnp.einsum(
        "epr,epd->erd", gram_flat, pair_weight, preferred_element_type=jnp.float32
    )
    cross_part = cross_sum.astype(jnp.bfloat16)
    cross_whole = lax.all_gather(cross_part, "tensor", axis=2, tiled=True)
    hidden_pre = jnp.einsum(
        "erd,edh->erh", cross_whole, up_weight, preferred_element_type=jnp.float32
    )
    hidden_act = jax.nn.silu(hidden_pre).astype(jnp.bfloat16)
    out_terms = jnp.einsum(
        "erh,ehd->erd", hidden_act, down_weight, preferred_element_type=jnp.float32
    )
    out_mine = lax.psum_scatter(
        out_terms.astype(jnp.bfloat16), "tensor", scatter_dimension=2, tiled=True
    )
    grad_act = jnp.einsum(
        "erd,ehd->erh", grad_rows, down_weight, preferred_element_type=jnp.float32
    )
    sigmoid_pre = jax.nn.sigmoid(hidden_pre)
    grad_pre = (grad_act * sigmoid_pre * (1.0 + hidden_pre * (1.0 - sigmoid_pre))).astype(
        jnp.bfloat16
    )
    grad_down = jnp.einsum(
        "erh,erd->ehd", hidden_act, grad_rows, preferred_element_type=jnp.float32
    ).astype(jnp.bfloat16)
    grad_up = jnp.einsum(
        "erd,erh->edh", cross_whole, grad_pre, preferred_element_type=jnp.float32
    ).astype(jnp.bfloat16)
    cross_terms = jnp.einsum(
        "erh,edh->erd", grad_pre, up_weight, preferred_element_type=jnp.float32
    )
    grad_cross = lax.psum_scatter(
        cross_terms.astype(jnp.bfloat16), "tensor", scatter_dimension=2, tiled=True
    )
    grad_pair = jnp.einsum(
        "epr,erd->epd", gram_flat, grad_cross, preferred_element_type=jnp.float32
    ).astype(jnp.bfloat16)
    pair_terms = jnp.einsum(
        "erd,epd->epr", grad_cross, pair_weight, preferred_element_type=jnp.float32
    )
    grad_gram = (
        lax.psum(pair_terms.astype(jnp.bfloat16), "tensor")
        .astype(jnp.float32)
        .reshape(local_count, NF, NF, expert_rows)
    )
    symmetric = grad_gram + jnp.swapaxes(grad_gram, 1, 2)
    field_count = part_width // DE
    symmetric_mine = lax.dynamic_slice_in_dim(symmetric, tensor_index * field_count, field_count, 1)
    gram_back = (
        jnp.einsum(
            "eijr,ejdr->eidr",
            symmetric_mine,
            cells.astype(jnp.float32),
            precision=lax.Precision.HIGHEST,
        )
        / DE
    )
    gram_back = jnp.transpose(gram_back, (0, 3, 1, 2)).reshape(local_count, expert_rows, part_width)
    grad_mine = (grad_cross.astype(jnp.float32) + gram_back).astype(jnp.bfloat16)
    back_shape = (1, local_count, expert_rows, part_width)
    out_back, grad_back = (
        lax.all_to_all(
            out_mine.reshape(back_shape), "expert", split_axis=2, concat_axis=0, tiled=True
        ),
        lax.all_to_all(
            grad_mine.reshape(back_shape), "expert", split_axis=2, concat_axis=0, tiled=True
        ),
    )
    out_back = out_back.reshape(expert_total * capacity, part_width)
    grad_back = grad_back.reshape(expert_total * capacity, part_width)
    picked = jnp.einsum("ksr,sd->rkd", tables, out_back, preferred_element_type=jnp.float32)
    mixed = (
        input_slice.astype(jnp.float32) + jnp.sum(gate_values[:, :, None] * picked, axis=1)
    ).astype(jnp.bfloat16)
    grad_input = (
        cotangent_slice.astype(jnp.float32)
        + jnp.dot(any_table.T, grad_back, preferred_element_type=jnp.float32)
    ).astype(jnp.bfloat16)
    return (mixed, grad_input, grad_pair, grad_up, grad_down)


F32 = jnp.float32
BF16 = jnp.bfloat16
NT = (((1,), (1,)), ((), ()))
TN = (((0,), (0,)), ((), ()))
WIDTH = 1024
HALF = 64


def mm(a, b, dims=None):
    if dims is None:
        return jnp.dot(a, b, preferred_element_type=F32)
    return lax.dot_general(a, b, dims, preferred_element_type=F32)


def kernel_call(kernel, out_shape, where, scratch=(), flops=0, nbytes=0, vmem=48):
    kinds = {"v": pltpu.VMEM, "a": pl.ANY, "h": pltpu.HBM}
    return pl.pallas_call(
        kernel,
        out_shape=out_shape,
        in_specs=[pl.BlockSpec(memory_space=kinds[w]) for w in where],
        scratch_shapes=list(scratch),
        compiler_params=pltpu.CompilerParams(vmem_limit_bytes=vmem * 1024 * 1024),
        cost_estimate=pl.CostEstimate(flops=flops, bytes_accessed=nbytes, transcendentals=0),
    )


def shape(dims, dtype=BF16):
    return jax.ShapeDtypeStruct(dims, dtype)


def load(pairs, sems):
    copies = [pltpu.make_async_copy(a, b, sems.at[n]) for n, (a, b) in enumerate(pairs)]
    for copy in copies:
        copy.start()
    return copies


def payload_kernel(x, c, gates_in, routes_in, pair_in, out_o, own_o, pair_o, gates, routes, sems):
    core = lax.rem(lax.axis_index("tensor"), 2)
    mine = pl.ds(pl.multiple_of(core * HALF, HALF), HALF)
    copies = load(
        [
            (gates_in, gates),
            (routes_in, routes),
            (x.at[mine, :], out_o.at[:, 0:WIDTH]),
            (c.at[mine, :], out_o.at[:, WIDTH : 2 * WIDTH]),
            (x, own_o.at[:, 0:WIDTH]),
            (c, own_o.at[:, WIDTH : 2 * WIDTH]),
            (pair_in, pair_o),
        ],
        sems,
    )
    copies[0].wait()
    copies[1].wait()
    high = gates[...].astype(BF16).astype(F32)
    low = gates[...] - high
    meta = jnp.concatenate(
        [routes[...].astype(F32), high, low, jnp.zeros((122, 128), F32)], axis=0
    )
    columns = meta.T
    own_o[:, 2 * WIDTH :] = columns.astype(BF16)
    out_o[:, 2 * WIDTH :] = jnp.where(core == 0, columns[0:HALF], columns[HALF:]).astype(BF16)
    for copy in copies[2:]:
        copy.wait()


def after_kernel(value, after, out_o):
    out_o[...] = value[...]


def stage_kernel(pair_x, own, pair, pair_x_o, own_o, pair_o):
    pair_x_o[...] = pair_x[...]
    own_o[...] = own[...]
    pair_o[...] = pair[...]


def join_kernel(a, b, after, out_o):
    out_o[0:HALF, :] = a[...]
    out_o[HALF : 2 * HALF, :] = b[...]


def place_rows(whole, info, block, core, near, far):
    for at, piece in ((core, near), (1 - core, far)):
        rows = pl.ds(pl.multiple_of(block * 128 + at * HALF, HALF), HALF)
        whole[rows, :] = piece[:, 0 : 2 * WIDTH]
        info[rows, :] = piece[:, 2 * WIDTH :]


def towers(meta, whole, up, down, ready, pair, outs, scratch):
    keep, send_here, send_away, send_last, cross_o, act_o, grad_o, pre_o, gram_o, pick_o, gate_o = outs
    flipped, partial, half_gram, terms, rows, slope, outs_s, backs = scratch
    j = lax.axis_index("tensor")
    core = lax.rem(j, 2)
    xi = j // 2
    first = lax.axis_index("expert") * 2
    tokens = meta.shape[1]
    before = (
        lax.broadcasted_iota(jnp.int32, (tokens, tokens), 0)
        < lax.broadcasted_iota(jnp.int32, (tokens, tokens), 1)
    ).astype(F32).astype(BF16)
    a = lax.broadcasted_iota(jnp.int32, (256, 144), 0)
    n = lax.broadcasted_iota(jnp.int32, (256, 144), 1)
    low = jnp.minimum(a // 16, a % 16)
    high = jnp.maximum(a // 16, a % 16)
    spread = jnp.where(low * 16 - low * (low - 1) // 2 + high - low == n, 1.0, 0.0).astype(BF16)
    a = lax.broadcasted_iota(jnp.int32, (256, 256), 0)
    b = lax.broadcasted_iota(jnp.int32, (256, 256), 1)
    swapped = (a % 16) * 16 + a // 16
    both = (jnp.where(a == b, 1.0, 0.0) + jnp.where(swapped == b, 1.0, 0.0)).astype(BF16)
    slots = lax.broadcasted_iota(jnp.int32, (128, tokens), 0).astype(F32)
    both_e = range(2)
    for e in both_e:
        mine = (first + e).astype(F32)
        s0 = meta[0:1, :] == mine
        s1 = meta[1:2, :] == mine
        named = jnp.where(s0, 1.0, 0.0) + jnp.where(s1, 1.0, 0.0)
        gate = jnp.where(s0, meta[2:3, :], 0.0) + jnp.where(s1, meta[3:4, :], 0.0)
        place = mm(jnp.broadcast_to(named, (8, tokens)).astype(BF16), before)[0:1, :]
        place = jnp.where(named > 0.5, place, -1.0)
        hit = slots == place
        pick_o[e] = jnp.where(hit, 1.0, 0.0).astype(BF16)
        weight = jnp.sum(jnp.where(hit, gate, 0.0), axis=1, keepdims=True)
        gate_o[e] = jnp.broadcast_to(weight, (128, 128))
    for e in both_e:
        rows[e] = mm(pick_o[e], whole[:, 0:WIDTH])
    for e in both_e:
        flipped[e] = rows[e].T
    for e in both_e:
        grad = mm(pick_o[e], whole[:, WIDTH : 2 * WIDTH])
        grad_o[e] = (gate_o[e][:, 0:1] * grad).astype(BF16)
    for e in both_e:
        half_gram[e, 136:144, :] = jnp.zeros((8, 128), F32)
        at = 0
        for i in range(16):
            left = flipped[e, i * 64 : i * 64 + 64, :]
            for q in range(i, 16):
                prod = left * flipped[e, q * 64 : q * 64 + 64, :]
                partial[e, at * 8 : at * 8 + 8, :] = jnp.sum(prod.reshape(8, 8, 128), axis=0)
                at += 1
        for g in range(17):
            acc = partial[e, pl.ds(g * 64, 8, stride=8), :]
            for q in range(1, 8):
                acc = acc + partial[e, pl.ds(g * 64 + q, 8, stride=8), :]
            half_gram[e, g * 8 : g * 8 + 8, :] = acc * (1.0 / DE)
        gram_o[e] = mm(spread, half_gram[e].astype(BF16)).astype(BF16)
    for e in both_e:
        cross_o[e] = (rows[e] + mm(gram_o[e], pair[e], TN)).astype(BF16)
    for copy in ready:
        copy.wait()
    for e in both_e:
        slope[e] = mm(grad_o[e], down[e], NT)
    for e in both_e:
        pre = mm(cross_o[e], up[e])
        sig = jax.nn.sigmoid(pre)
        act_o[e] = (pre * sig).astype(BF16)
        pre_o[e] = (slope[e] * sig * (1.0 + pre * (1.0 - sig))).astype(BF16)
    for e in both_e:
        terms[e] = mm(pre_o[e], up[e], NT).astype(BF16)
    for e in both_e:
        outs_s[e] = mm(act_o[e], down[e]).astype(BF16)
    for e in both_e:
        back = mm(pair[e], terms[e], NT).astype(BF16)
        backs[e] = mm(both, back).astype(BF16)
    for xr in (1, 0):
        for part in (1, 0):
            block = 2 * (xi ^ xr) + (core ^ part)
            cols = pl.ds(pl.multiple_of(block * 256, 256), 256)
            if part == 0:
                low, high = keep.at[xr, 0:320], keep.at[xr, 320:576]
            elif xr == 0:
                low, high = send_here.at[0:320], send_here.at[320:576]
            else:
                low, high = send_away, send_last
            for e in both_e:
                mine = slice(e * 128, e * 128 + 128)
                low[mine, :] = terms[e, :, cols]
                high[mine, :] = outs_s[e, :, cols]
                rows64 = pl.ds(pl.multiple_of(block * 64, 64), 64)
                low[256:320, mine] = backs[e, rows64, :]


def read_meta(info):
    rows = info[...].astype(F32).T
    return jnp.concatenate([rows[0:2], rows[2:4] + rows[4:6]], axis=0)


def own_chunk_kernel(*refs):
    own, p0, near, far, p1, p2, p3, up_in, down_in = refs[:9]
    outs, pair_o = refs[9:20], refs[20]
    whole, info, up, down, sems = refs[21:26]
    j = lax.axis_index("tensor")
    copies = load([(up_in, up), (down_in, down)], sems)
    whole[0:128, :] = own[:, 0 : 2 * WIDTH]
    info[0:128, :] = own[:, 2 * WIDTH :]
    place_rows(whole, info, 1, lax.rem(j, 2), near, far)
    for k, piece in enumerate((p0, p1, p2, p3)):
        cols = pl.ds(pl.multiple_of((j ^ k) * 256, 256), 256)
        for e in range(2):
            pair_o[e, :, cols] = piece[e]
    towers(read_meta(info), whole, up, down, copies, pair_o, outs, refs[26:])


def far_chunk_kernel(*refs):
    near, far, pair, up_in, down_in = refs[:5]
    outs = refs[5:16]
    whole, info, up, down, sems = refs[16:21]
    core = lax.rem(lax.axis_index("tensor"), 2)
    copies = load([(up_in, up), (down_in, down)], sems)
    for r in range(2):
        rows = slice(r * HALF, r * HALF + HALF)
        place_rows(whole, info, r, core, near.at[rows, :], far.at[rows, :])
    towers(read_meta(info), whole, up, down, copies, pair, outs, refs[21:])


def weights_kernel(act0, grad0, cross0, pre0, act1, grad1, cross1, pre1, down_o, up_o, done_o):
    done_o[...] = jnp.zeros((8, 128), F32)

    def stack(a, b):
        return jnp.concatenate([a, b], axis=0)

    for e in range(2):
        down_o[e] = mm(stack(act0[e], act1[e]), stack(grad0[e], grad1[e]), TN).astype(BF16)
        up_o[e] = mm(stack(cross0[e], cross1[e]), stack(pre0[e], pre1[e]), TN).astype(BF16)


def add2(a, b):
    return (a.astype(F32) + b.astype(F32)).astype(BF16)


def combine_grads(both, picks, rows_o):
    grads = jnp.zeros((256, 256), F32)
    back = jnp.zeros((64, 256), F32)
    for e in range(2):
        rows = both[e * 128 : e * 128 + 128]
        rows_o[e] = rows
        grads = grads + mm(picks[e], rows, TN)
        back = back + mm(both[256:320, e * 128 : e * 128 + 128], picks[e])
    return grads.astype(BF16), back.astype(BF16)


def put_grads(dst, grads, back, p):
    rows = slice(p * 128, p * 128 + 128)
    dst[0:128, :] = grads[rows]
    dst[128:160, 0:128] = back[0:32, rows]
    dst[128:160, 128:256] = back[32:64, rows]


def combine_outs(both, picks, gates):
    mixed = jnp.zeros((256, 256), F32)
    for e in range(2):
        out = both[e * 128 : e * 128 + 128].astype(F32) * gates[e][:, 0:1]
        mixed = mixed + mm(picks[e], out.astype(BF16), TN)
    return mixed.astype(BF16)


def combine_kernel(mine, other, theirs, pick, gate, after, first_o, second_o, rows_o):
    both = add2(add2(mine[0], other[...]), theirs[...])
    grads, back = combine_grads(both[0:320], pick, rows_o)
    mixed = combine_outs(both[320:576], pick, gate)
    for p, dst in enumerate((first_o, second_o)):
        put_grads(dst, grads, back, p)
        dst[160:288, :] = mixed[p * 128 : p * 128 + 128]


def far_grads_kernel(mine, other, theirs, pick, after, after2, first_o, second_o, rows_o):
    both = add2(add2(mine[0, 0:320], other[0:320]), theirs[...])
    grads, back = combine_grads(both, pick, rows_o)
    for p, dst in enumerate((first_o, second_o)):
        put_grads(dst, grads, back, p)


def far_outs_kernel(mine, other, theirs, pick, gate, first_o, second_o):
    both = add2(add2(mine[0, 320:576], other[320:576]), theirs[...])
    mixed = combine_outs(both, pick, gate)
    first_o[...] = mixed[0:128]
    second_o[...] = mixed[128:256]


def sum_kernel(a, b, out_o):
    out_o[...] = add2(a[...], b[...])


def pair_kernel(gram0, rows0, gram1, rows1, out_o):
    for e in range(2):
        out_o[e] = (mm(gram0[e], rows0[e]) + mm(gram1[e], rows1[e])).astype(BF16)


def final_kernel(own, g0, g1, far_grads, far_outs, mixed_o, grad_o, flipped):
    column = pl.multiple_of(lax.axis_index("tensor") * 256, 256)
    mixed = own[:, pl.ds(column, 256)].astype(F32) + far_outs[...].astype(F32)
    total = own[:, pl.ds(WIDTH + column, 256)].astype(F32)
    back = jnp.zeros((32, 256), F32)
    for g in (g0, g1, far_grads):
        total = total + g[0:128, :].astype(F32)
        back = back + g[128:160, :].astype(F32)
    for g in (g0, g1):
        mixed = mixed + g[160:288, :].astype(F32)
    mixed_o[...] = mixed.astype(BF16)
    flipped[...] = own[:, 0:WIDTH].astype(F32).T
    back = jnp.concatenate([back[:, 0:128], back[:, 128:256]], axis=0)
    pieces = []
    for i in range(4):
        acc = jnp.zeros((64, 128), F32)
        for q in range(16):
            acc = acc + back[i * 16 + q : i * 16 + q + 1, :] * flipped[q * 64 : q * 64 + 64, :]
        pieces.append(acc)
    gram_back = jnp.concatenate(pieces, axis=0) * (1.0 / DE)
    grad_o[...] = (total + gram_back.T).astype(BF16)


def swap(value, axis, mask):
    size = lax.axis_size(axis)
    return lax.ppermute(value, axis, [(i, i ^ mask) for i in range(size)])


def chunk_outs():
    return (
        shape((2, 576, 256)),
        shape((576, 256)),
        shape((320, 256)),
        shape((256, 256)),
        shape((2, 128, 1024)),
        shape((2, 128, 512)),
        shape((2, 128, 1024)),
        shape((2, 128, 512)),
        shape((2, 256, 128)),
        shape((2, 128, 256)),
        shape((2, 128, 128), F32),
    )


def chunk_scratch():
    return [
        pltpu.VMEM((2, 1024, 128), F32),
        pltpu.VMEM((2, 1088, 128), F32),
        pltpu.VMEM((2, 144, 128), F32),
        pltpu.VMEM((2, 128, 1024), BF16),
        pltpu.VMEM((2, 128, 1024), F32),
        pltpu.VMEM((2, 128, 512), F32),
        pltpu.VMEM((2, 128, 1024), BF16),
        pltpu.VMEM((2, 256, 128), BF16),
    ]


def weight_scratch():
    return [pltpu.VMEM((2, 1024, 512), BF16), pltpu.VMEM((2, 512, 1024), BF16)]


def away_kernel(keep, low, high, out_o):
    out_o[0:320, :] = add2(keep[1, 0:320], low[...])
    out_o[320:576, :] = add2(keep[1, 320:576], high[...])


def away_grads_kernel(keep, low, after, out_o):
    out_o[...] = add2(keep[1, 0:320], low[...])


def away_outs_kernel(keep, high, after, out_o):
    out_o[...] = add2(keep[1, 320:576], high[...])


def gathered_body(inputs, cotangent, gate_values, routes, pair_weight, up_weight, down_weight):
    gates, choices = gate_values.T, routes.T
    width = 2 * WIDTH + 128
    payload, own, pair_own = kernel_call(
        payload_kernel,
        (
            shape((HALF, width)),
            shape((2 * HALF, width)),
            shape((2, 256, 256)),
        ),
        "hhhhh",
        scratch=[
            pltpu.VMEM((2, 128), F32),
            pltpu.VMEM((2, 128), jnp.int32),
            pltpu.SemaphoreType.DMA((7,)),
        ],
        vmem=60,
    )(inputs, cotangent, gates, choices, pair_weight)
    got = [swap(payload, "expert", 1), swap(payload, "expert", 2)]
    got.append(swap(got[1], "expert", 1))
    both = shape((2, 256, 256))
    pair_x, own, pair_own = kernel_call(
        stage_kernel,
        (both, shape((2 * HALF, width)), both),
        "vvv",
    )(swap(pair_own, "tensor", 2), own, pair_own)
    pair_x = kernel_call(after_kernel, both, "va")(pair_x, got[1])
    pair_c = swap(pair_own, "tensor", 1)
    pair_d = swap(pair_x, "tensor", 1)
    near_other = swap(got[0], "tensor", 1)
    chunk = kernel_call(
        own_chunk_kernel,
        chunk_outs() + (shape((2, 256, 1024)),),
        "vvvvvvvhh",
        scratch=[
            pltpu.VMEM((256, 2048), BF16),
            pltpu.VMEM((256, 128), BF16),
        ]
        + weight_scratch()
        + [pltpu.SemaphoreType.DMA((2,))]
        + chunk_scratch(),
        flops=4_000_000_000,
        nbytes=10_000_000,
    )(
        own, pair_own, got[0], near_other,
        pair_c, pair_x, pair_d, up_weight, down_weight,
    )
    keep, here, away, last, cross, act, grad, pre, gram, pick, gate, pair_all = chunk
    away = kernel_call(away_kernel, shape((576, 256)), "vvv")(
        keep, swap(away, "tensor", 1), swap(last, "tensor", 1)
    )
    theirs = swap(away, "tensor", 2)
    other = swap(here, "tensor", 1)
    far_mine = kernel_call(join_kernel, shape((2 * HALF, 2 * WIDTH + 128)), "vva")(
        got[1], got[2], gate
    )
    far_other = swap(far_mine, "tensor", 1)
    chunk = kernel_call(
        far_chunk_kernel,
        chunk_outs(),
        "vvvhh",
        scratch=[pltpu.VMEM((256, 2048), BF16), pltpu.VMEM((256, 128), BF16)]
        + weight_scratch()
        + [pltpu.SemaphoreType.DMA((2,))]
        + chunk_scratch(),
        flops=4_000_000_000,
        nbytes=10_000_000,
    )(far_mine, far_other, pair_all, up_weight, down_weight)
    fkeep, fhere, faway, flast, fcross, fact, fgrad, fpre, fgram, fpick, fgate = chunk
    fother = swap(fhere, "tensor", 1)
    fgrads = kernel_call(away_grads_kernel, shape((320, 256)), "vva")(
        fkeep, swap(faway, "tensor", 1), theirs
    )
    fouts = kernel_call(away_outs_kernel, shape((256, 256)), "vva")(
        fkeep, swap(flast, "tensor", 1), fgrads
    )
    fgrads = swap(fgrads, "tensor", 2)
    part = shape((288, 256))
    own_part, near_part, rows = kernel_call(
        combine_kernel, (part, part, shape((2, 128, 256))), "vvvvva"
    )(keep, other, theirs, pick, gate, fouts)
    near_got = swap(near_part, "expert", 1)
    fouts = swap(fouts, "tensor", 2)
    grad_down, grad_up, weights_done = kernel_call(
        weights_kernel,
        (shape((2, 512, 1024)), shape((2, 1024, 512)), shape((8, 128), F32)),
        "vvvvvvvv",
        flops=3_000_000_000,
        nbytes=8_000_000,
    )(act, grad, cross, pre, fact, fgrad, fcross, fpre)
    part = shape((160, 256))
    grads2, grads3, frows = kernel_call(
        far_grads_kernel, (part, part, shape((2, 128, 256))), "vvvvaa"
    )(fkeep, fother, fgrads, fpick, weights_done, near_got)
    grads2 = kernel_call(sum_kernel, part, "vv")(grads2, swap(grads3, "expert", 1))
    far_grads = swap(grads2, "expert", 2)
    part = shape((128, 256))
    outs2, outs3 = kernel_call(far_outs_kernel, (part, part), "vvvvv")(
        fkeep, fother, fouts, fpick, fgate
    )
    outs2 = kernel_call(sum_kernel, part, "vv")(outs2, swap(outs3, "expert", 1))
    far_outs = swap(outs2, "expert", 2)
    grad_pair = kernel_call(
        pair_kernel, shape((2, 256, 256)), "vvvv", flops=300_000_000, nbytes=2_000_000
    )(gram, rows, fgram, frows)
    mixed, grad_input = kernel_call(
        final_kernel,
        (shape((128, 256)), shape((128, 256))),
        "vvvvv",
        scratch=[pltpu.VMEM((1024, 128), F32)],
        flops=100_000_000,
        nbytes=1_000_000,
    )(own, own_part, near_got, far_grads, far_outs)
    return mixed, grad_input, grad_pair, grad_up, grad_down


def solution(mesh):
    placed = (
        P(("group", "expert"), None),
        P(("group", "expert"), None),
        P(("group", "expert"), None),
        P(("group", "expert"), None),
        P("expert", None, "tensor"),
        P("expert", None, "tensor"),
        P("expert", "tensor", None),
    )
    small = mesh.shape["expert"] == 4 and mesh.shape["tensor"] == 4
    return jax.shard_map(
        gathered_body if small else body,
        mesh=mesh,
        in_specs=placed,
        out_specs=(
            P(("group", "expert"), "tensor"),
            P(("group", "expert"), "tensor"),
            P(("group", "expert"), None, "tensor"),
            P(("group", "expert"), None, "tensor"),
            P(("group", "expert"), "tensor", None),
        ),
        check_vma=False,
    )
```

```python
import functools

import jax
import jax.numpy as jnp
from jax import lax
from jax.experimental import pallas as pl
from jax.experimental.pallas import tpu as pltpu
from jax.sharding import PartitionSpec as P

NF = 16
DE = 64


def dispatch_tables(routes, expert_total, capacity):
    row_count, pick_count = routes.shape
    flat_ids = routes.reshape(-1)
    onehot = (flat_ids[:, None] == jnp.arange(expert_total, dtype=jnp.int32)[None, :]).astype(
        jnp.int32
    )
    before = jnp.cumsum(onehot, axis=0) - onehot
    position = jnp.sum(before * onehot, axis=1)
    slot_index = flat_ids * capacity + position
    slot_count = expert_total * capacity
    tables = slot_index[:, None] == jnp.arange(slot_count, dtype=jnp.int32)[None, :]
    tables = tables.reshape(row_count, pick_count, slot_count)
    return jnp.transpose(tables, (1, 2, 0)).astype(jnp.bfloat16)


def body(inputs, cotangent, gate_values, routes, pair_weight, up_weight, down_weight):
    local_count = up_weight.shape[0]
    expert_count = lax.axis_size("expert")
    tensor_count = lax.axis_size("tensor")
    expert_total = local_count * expert_count
    row_count, pick_count = routes.shape
    feature_width = inputs.shape[1]
    capacity = 2 * row_count * pick_count // expert_total
    expert_rows = expert_count * capacity
    part_width = feature_width // tensor_count
    tensor_index = lax.axis_index("tensor")
    feature_start = tensor_index * part_width
    tables = dispatch_tables(routes, expert_total, capacity)
    any_table = jnp.sum(tables, axis=0)
    scaled = (gate_values[:, :, None] * cotangent[:, None, :].astype(jnp.float32)).astype(
        jnp.bfloat16
    )
    input_slice = lax.dynamic_slice_in_dim(inputs, feature_start, part_width, 1)
    cotangent_slice = lax.dynamic_slice_in_dim(cotangent, feature_start, part_width, 1)
    input_slots = jnp.dot(any_table, inputs, preferred_element_type=jnp.float32).astype(
        jnp.bfloat16
    )
    grad_slots = jnp.einsum(
        "ksr,rkd->sd", tables, scaled, preferred_element_type=jnp.float32
    ).astype(jnp.bfloat16)
    send_shape = (expert_count, local_count, capacity, feature_width)
    input_homes, grad_homes = (
        lax.all_to_all(
            input_slots.reshape(send_shape), "expert", split_axis=0, concat_axis=2, tiled=True
        ),
        lax.all_to_all(
            grad_slots.reshape(send_shape), "expert", split_axis=0, concat_axis=2, tiled=True
        ),
    )
    input_rows = input_homes.reshape(local_count, expert_rows, feature_width)
    grad_rows = grad_homes.reshape(local_count, expert_rows, feature_width)
    cells = jnp.transpose(input_rows.reshape(local_count, expert_rows, NF, DE), (0, 2, 3, 1))
    gram = jnp.einsum("eidr,ejdr->eijr", cells, cells, preferred_element_type=jnp.float32) / DE
    gram_flat = gram.reshape(local_count, NF * NF, expert_rows).astype(jnp.bfloat16)
    input_mine = lax.dynamic_slice_in_dim(input_rows, feature_start, part_width, 2)
    cross_sum = input_mine.astype(jnp.float32) + jnp.einsum(
        "epr,epd->erd", gram_flat, pair_weight, preferred_element_type=jnp.float32
    )
    cross_part = cross_sum.astype(jnp.bfloat16)
    cross_whole = lax.all_gather(cross_part, "tensor", axis=2, tiled=True)
    hidden_pre = jnp.einsum(
        "erd,edh->erh", cross_whole, up_weight, preferred_element_type=jnp.float32
    )
    hidden_act = jax.nn.silu(hidden_pre).astype(jnp.bfloat16)
    out_terms = jnp.einsum(
        "erh,ehd->erd", hidden_act, down_weight, preferred_element_type=jnp.float32
    )
    out_mine = lax.psum_scatter(
        out_terms.astype(jnp.bfloat16), "tensor", scatter_dimension=2, tiled=True
    )
    grad_act = jnp.einsum(
        "erd,ehd->erh", grad_rows, down_weight, preferred_element_type=jnp.float32
    )
    sigmoid_pre = jax.nn.sigmoid(hidden_pre)
    grad_pre = (grad_act * sigmoid_pre * (1.0 + hidden_pre * (1.0 - sigmoid_pre))).astype(
        jnp.bfloat16
    )
    grad_down = jnp.einsum(
        "erh,erd->ehd", hidden_act, grad_rows, preferred_element_type=jnp.float32
    ).astype(jnp.bfloat16)
    grad_up = jnp.einsum(
        "erd,erh->edh", cross_whole, grad_pre, preferred_element_type=jnp.float32
    ).astype(jnp.bfloat16)
    cross_terms = jnp.einsum(
        "erh,edh->erd", grad_pre, up_weight, preferred_element_type=jnp.float32
    )
    grad_cross = lax.psum_scatter(
        cross_terms.astype(jnp.bfloat16), "tensor", scatter_dimension=2, tiled=True
    )
    grad_pair = jnp.einsum(
        "epr,erd->epd", gram_flat, grad_cross, preferred_element_type=jnp.float32
    ).astype(jnp.bfloat16)
    pair_terms = jnp.einsum(
        "erd,epd->epr", grad_cross, pair_weight, preferred_element_type=jnp.float32
    )
    grad_gram = (
        lax.psum(pair_terms.astype(jnp.bfloat16), "tensor")
        .astype(jnp.float32)
        .reshape(local_count, NF, NF, expert_rows)
    )
    symmetric = grad_gram + jnp.swapaxes(grad_gram, 1, 2)
    field_count = part_width // DE
    symmetric_mine = lax.dynamic_slice_in_dim(symmetric, tensor_index * field_count, field_count, 1)
    gram_back = (
        jnp.einsum(
            "eijr,ejdr->eidr",
            symmetric_mine,
            cells.astype(jnp.float32),
            precision=lax.Precision.HIGHEST,
        )
        / DE
    )
    gram_back = jnp.transpose(gram_back, (0, 3, 1, 2)).reshape(local_count, expert_rows, part_width)
    grad_mine = (grad_cross.astype(jnp.float32) + gram_back).astype(jnp.bfloat16)
    back_shape = (1, local_count, expert_rows, part_width)
    out_back, grad_back = (
        lax.all_to_all(
            out_mine.reshape(back_shape), "expert", split_axis=2, concat_axis=0, tiled=True
        ),
        lax.all_to_all(
            grad_mine.reshape(back_shape), "expert", split_axis=2, concat_axis=0, tiled=True
        ),
    )
    out_back = out_back.reshape(expert_total * capacity, part_width)
    grad_back = grad_back.reshape(expert_total * capacity, part_width)
    picked = jnp.einsum("ksr,sd->rkd", tables, out_back, preferred_element_type=jnp.float32)
    mixed = (
        input_slice.astype(jnp.float32) + jnp.sum(gate_values[:, :, None] * picked, axis=1)
    ).astype(jnp.bfloat16)
    grad_input = (
        cotangent_slice.astype(jnp.float32)
        + jnp.dot(any_table.T, grad_back, preferred_element_type=jnp.float32)
    ).astype(jnp.bfloat16)
    return (mixed, grad_input, grad_pair, grad_up, grad_down)


F32 = jnp.float32
BF16 = jnp.bfloat16
NT = (((1,), (1,)), ((), ()))
TN = (((0,), (0,)), ((), ()))
WIDTH = 1024
HALF = 64


def mm(a, b, dims=None):
    if dims is None:
        return jnp.dot(a, b, preferred_element_type=F32)
    return lax.dot_general(a, b, dims, preferred_element_type=F32)


def kernel_call(kernel, out_shape, where, scratch=(), flops=0, nbytes=0, vmem=48):
    kinds = {"v": pltpu.VMEM, "a": pl.ANY, "h": pltpu.HBM}
    return pl.pallas_call(
        kernel,
        out_shape=out_shape,
        in_specs=[pl.BlockSpec(memory_space=kinds[w]) for w in where],
        scratch_shapes=list(scratch),
        compiler_params=pltpu.CompilerParams(vmem_limit_bytes=vmem * 1024 * 1024),
        cost_estimate=pl.CostEstimate(flops=flops, bytes_accessed=nbytes, transcendentals=0),
    )


def shape(dims, dtype=BF16):
    return jax.ShapeDtypeStruct(dims, dtype)


def load(pairs, sems):
    copies = [pltpu.make_async_copy(a, b, sems.at[n]) for n, (a, b) in enumerate(pairs)]
    for copy in copies:
        copy.start()
    return copies


def payload_kernel(x, c, gates_in, routes_in, pair_in, out_o, own_o, pair_o, gates, routes, sems):
    core = lax.rem(lax.axis_index("tensor"), 2)
    mine = pl.ds(pl.multiple_of(core * HALF, HALF), HALF)
    copies = load(
        [
            (gates_in, gates),
            (routes_in, routes),
            (x.at[mine, :], out_o.at[:, 0:WIDTH]),
            (c.at[mine, :], out_o.at[:, WIDTH : 2 * WIDTH]),
            (x, own_o.at[:, 0:WIDTH]),
            (c, own_o.at[:, WIDTH : 2 * WIDTH]),
            (pair_in, pair_o),
        ],
        sems,
    )
    copies[0].wait()
    copies[1].wait()
    high = gates[...].astype(BF16).astype(F32)
    low = gates[...] - high
    meta = jnp.concatenate(
        [routes[...].astype(F32), high, low, jnp.zeros((122, 128), F32)], axis=0
    )
    columns = meta.T
    own_o[:, 2 * WIDTH :] = columns.astype(BF16)
    out_o[:, 2 * WIDTH :] = jnp.where(core == 0, columns[0:HALF], columns[HALF:]).astype(BF16)
    for copy in copies[2:]:
        copy.wait()


def after_kernel(value, after, out_o):
    out_o[...] = value[...]


def stage_kernel(own, pair, own_o, pair_o):
    own_o[...] = own[...]
    pair_o[...] = pair[...]


def join_kernel(a, b, after, out_o):
    out_o[0:HALF, :] = a[...]
    out_o[HALF : 2 * HALF, :] = b[...]


def place_rows(whole, info, block, core, near, far):
    for at, piece in ((core, near), (1 - core, far)):
        rows = pl.ds(pl.multiple_of(block * 128 + at * HALF, HALF), HALF)
        whole[rows, :] = piece[:, 0 : 2 * WIDTH]
        info[rows, :] = piece[:, 2 * WIDTH :]


def towers(meta, whole, up, down, ready, pair, outs, scratch):
    keep, send_here, send_away, send_last, cross_o, act_o, grad_o, pre_o, gram_o, pick_o, gate_o = outs
    flipped, partial, half_gram, terms, rows, slope, outs_s, backs = scratch
    j = lax.axis_index("tensor")
    core = lax.rem(j, 2)
    xi = j // 2
    first = lax.axis_index("expert") * 2
    tokens = meta.shape[1]
    before = (
        lax.broadcasted_iota(jnp.int32, (tokens, tokens), 0)
        < lax.broadcasted_iota(jnp.int32, (tokens, tokens), 1)
    ).astype(F32).astype(BF16)
    a = lax.broadcasted_iota(jnp.int32, (256, 144), 0)
    n = lax.broadcasted_iota(jnp.int32, (256, 144), 1)
    low = jnp.minimum(a // 16, a % 16)
    high = jnp.maximum(a // 16, a % 16)
    spread = jnp.where(low * 16 - low * (low - 1) // 2 + high - low == n, 1.0, 0.0).astype(BF16)
    a = lax.broadcasted_iota(jnp.int32, (256, 256), 0)
    b = lax.broadcasted_iota(jnp.int32, (256, 256), 1)
    swapped = (a % 16) * 16 + a // 16
    both = (jnp.where(a == b, 1.0, 0.0) + jnp.where(swapped == b, 1.0, 0.0)).astype(BF16)
    slots = lax.broadcasted_iota(jnp.int32, (128, tokens), 0).astype(F32)
    both_e = range(2)
    for e in both_e:
        mine = (first + e).astype(F32)
        s0 = meta[0:1, :] == mine
        s1 = meta[1:2, :] == mine
        named = jnp.where(s0, 1.0, 0.0) + jnp.where(s1, 1.0, 0.0)
        gate = jnp.where(s0, meta[2:3, :], 0.0) + jnp.where(s1, meta[3:4, :], 0.0)
        place = mm(jnp.broadcast_to(named, (8, tokens)).astype(BF16), before)[0:1, :]
        place = jnp.where(named > 0.5, place, -1.0)
        hit = slots == place
        pick_o[e] = jnp.where(hit, 1.0, 0.0).astype(BF16)
        weight = jnp.sum(jnp.where(hit, gate, 0.0), axis=1, keepdims=True)
        gate_o[e] = jnp.broadcast_to(weight, (128, 128))
    for e in both_e:
        rows[e] = mm(pick_o[e], whole[:, 0:WIDTH])
    for e in both_e:
        flipped[e] = rows[e].T
    for e in both_e:
        grad = mm(pick_o[e], whole[:, WIDTH : 2 * WIDTH])
        grad_o[e] = (gate_o[e][:, 0:1] * grad).astype(BF16)
    for e in both_e:
        half_gram[e, 136:144, :] = jnp.zeros((8, 128), F32)
        at = 0
        for i in range(16):
            left = flipped[e, i * 64 : i * 64 + 64, :]
            for q in range(i, 16):
                prod = left * flipped[e, q * 64 : q * 64 + 64, :]
                partial[e, at * 8 : at * 8 + 8, :] = jnp.sum(prod.reshape(8, 8, 128), axis=0)
                at += 1
        for g in range(17):
            acc = partial[e, pl.ds(g * 64, 8, stride=8), :]
            for q in range(1, 8):
                acc = acc + partial[e, pl.ds(g * 64 + q, 8, stride=8), :]
            half_gram[e, g * 8 : g * 8 + 8, :] = acc * (1.0 / DE)
        gram_o[e] = mm(spread, half_gram[e].astype(BF16)).astype(BF16)
    for e in both_e:
        cross_o[e] = (rows[e] + mm(gram_o[e], pair[e], TN)).astype(BF16)
    for copy in ready:
        copy.wait()
    for e in both_e:
        slope[e] = mm(grad_o[e], down[e], NT)
    for e in both_e:
        pre = mm(cross_o[e], up[e])
        sig = jax.nn.sigmoid(pre)
        act_o[e] = (pre * sig).astype(BF16)
        pre_o[e] = (slope[e] * sig * (1.0 + pre * (1.0 - sig))).astype(BF16)
    for e in both_e:
        terms[e] = mm(pre_o[e], up[e], NT).astype(BF16)
    for e in both_e:
        outs_s[e] = mm(act_o[e], down[e]).astype(BF16)
    for e in both_e:
        back = mm(pair[e], terms[e], NT).astype(BF16)
        backs[e] = mm(both, back).astype(BF16)
    for xr in (1, 0):
        for part in (1, 0):
            block = 2 * (xi ^ xr) + (core ^ part)
            cols = pl.ds(pl.multiple_of(block * 256, 256), 256)
            if part == 0:
                low, high = keep.at[xr, 0:320], keep.at[xr, 320:576]
            elif xr == 0:
                low, high = send_here.at[0:320], send_here.at[320:576]
            else:
                low, high = send_away, send_last
            for e in both_e:
                mine = slice(e * 128, e * 128 + 128)
                low[mine, :] = terms[e, :, cols]
                high[mine, :] = outs_s[e, :, cols]
                rows64 = pl.ds(pl.multiple_of(block * 64, 64), 64)
                low[256:320, mine] = backs[e, rows64, :]


def read_meta(info):
    rows = info[...].astype(F32).T
    return jnp.concatenate([rows[0:2], rows[2:4] + rows[4:6]], axis=0)


def own_chunk_kernel(*refs):
    own, p0, near, far, p1, p2, p3, up_in, down_in = refs[:9]
    outs, pair_o = refs[9:20], refs[20]
    whole, info, up, down, sems = refs[21:26]
    j = lax.axis_index("tensor")
    copies = load([(up_in, up), (down_in, down)], sems)
    whole[0:128, :] = own[:, 0 : 2 * WIDTH]
    info[0:128, :] = own[:, 2 * WIDTH :]
    place_rows(whole, info, 1, lax.rem(j, 2), near, far)
    for k, piece in enumerate((p0, p1, p2, p3)):
        cols = pl.ds(pl.multiple_of((j ^ k) * 256, 256), 256)
        for e in range(2):
            pair_o[e, :, cols] = piece[e]
    towers(read_meta(info), whole, up, down, copies, pair_o, outs, refs[26:])


def far_chunk_kernel(*refs):
    near, far, pair, up_in, down_in = refs[:5]
    outs = refs[5:16]
    whole, info, up, down, sems = refs[16:21]
    core = lax.rem(lax.axis_index("tensor"), 2)
    copies = load([(up_in, up), (down_in, down)], sems)
    for r in range(2):
        rows = slice(r * HALF, r * HALF + HALF)
        place_rows(whole, info, r, core, near.at[rows, :], far.at[rows, :])
    towers(read_meta(info), whole, up, down, copies, pair, outs, refs[21:])


def weights_kernel(act0, grad0, cross0, pre0, act1, grad1, cross1, pre1, down_o, up_o, done_o):
    done_o[...] = jnp.zeros((8, 128), F32)

    def stack(a, b):
        return jnp.concatenate([a, b], axis=0)

    for e in range(2):
        down_o[e] = mm(stack(act0[e], act1[e]), stack(grad0[e], grad1[e]), TN).astype(BF16)
        up_o[e] = mm(stack(cross0[e], cross1[e]), stack(pre0[e], pre1[e]), TN).astype(BF16)


def add2(a, b):
    return (a.astype(F32) + b.astype(F32)).astype(BF16)


def combine_grads(both, picks, rows_o):
    grads = jnp.zeros((256, 256), F32)
    back = jnp.zeros((64, 256), F32)
    for e in range(2):
        rows = both[e * 128 : e * 128 + 128]
        rows_o[e] = rows
        grads = grads + mm(picks[e], rows, TN)
        back = back + mm(both[256:320, e * 128 : e * 128 + 128], picks[e])
    return grads.astype(BF16), back.astype(BF16)


def put_grads(dst, grads, back, p):
    rows = slice(p * 128, p * 128 + 128)
    dst[0:128, :] = grads[rows]
    dst[128:160, 0:128] = back[0:32, rows]
    dst[128:160, 128:256] = back[32:64, rows]


def combine_outs(both, picks, gates):
    mixed = jnp.zeros((256, 256), F32)
    for e in range(2):
        out = both[e * 128 : e * 128 + 128].astype(F32) * gates[e][:, 0:1]
        mixed = mixed + mm(picks[e], out.astype(BF16), TN)
    return mixed.astype(BF16)


def combine_kernel(mine, other, theirs, pick, gate, after, first_o, second_o, rows_o):
    both = add2(add2(mine[0], other[...]), theirs[...])
    grads, back = combine_grads(both[0:320], pick, rows_o)
    mixed = combine_outs(both[320:576], pick, gate)
    for p, dst in enumerate((first_o, second_o)):
        put_grads(dst, grads, back, p)
        dst[160:288, :] = mixed[p * 128 : p * 128 + 128]


def far_grads_kernel(mine, other, theirs, pick, after, first_o, second_o, rows_o):
    both = add2(add2(mine[0, 0:320], other[0:320]), theirs[...])
    grads, back = combine_grads(both, pick, rows_o)
    for p, dst in enumerate((first_o, second_o)):
        put_grads(dst, grads, back, p)


def far_outs_kernel(mine, other, theirs, pick, gate, after, first_o, second_o):
    both = add2(add2(mine[0, 320:576], other[320:576]), theirs[...])
    mixed = combine_outs(both, pick, gate)
    first_o[...] = mixed[0:128]
    second_o[...] = mixed[128:256]


def sum_kernel(a, b, out_o):
    out_o[...] = add2(a[...], b[...])


def pair_kernel(gram0, rows0, gram1, rows1, out_o):
    for e in range(2):
        out_o[e] = (mm(gram0[e], rows0[e]) + mm(gram1[e], rows1[e])).astype(BF16)


def final_kernel(own, g0, g1, far_grads, far_outs, mixed_o, grad_o, flipped):
    column = pl.multiple_of(lax.axis_index("tensor") * 256, 256)
    mixed = own[:, pl.ds(column, 256)].astype(F32) + far_outs[...].astype(F32)
    total = own[:, pl.ds(WIDTH + column, 256)].astype(F32)
    back = jnp.zeros((32, 256), F32)
    for g in (g0, g1, far_grads):
        total = total + g[0:128, :].astype(F32)
        back = back + g[128:160, :].astype(F32)
    for g in (g0, g1):
        mixed = mixed + g[160:288, :].astype(F32)
    mixed_o[...] = mixed.astype(BF16)
    flipped[...] = own[:, 0:WIDTH].astype(F32).T
    back = jnp.concatenate([back[:, 0:128], back[:, 128:256]], axis=0)
    pieces = []
    for i in range(4):
        acc = jnp.zeros((64, 128), F32)
        for q in range(16):
            acc = acc + back[i * 16 + q : i * 16 + q + 1, :] * flipped[q * 64 : q * 64 + 64, :]
        pieces.append(acc)
    gram_back = jnp.concatenate(pieces, axis=0) * (1.0 / DE)
    grad_o[...] = (total + gram_back.T).astype(BF16)


def swap(value, axis, mask):
    size = lax.axis_size(axis)
    return lax.ppermute(value, axis, [(i, i ^ mask) for i in range(size)])


def chunk_outs():
    return (
        shape((2, 576, 256)),
        shape((576, 256)),
        shape((320, 256)),
        shape((256, 256)),
        shape((2, 128, 1024)),
        shape((2, 128, 512)),
        shape((2, 128, 1024)),
        shape((2, 128, 512)),
        shape((2, 256, 128)),
        shape((2, 128, 256)),
        shape((2, 128, 128), F32),
    )


def chunk_scratch():
    return [
        pltpu.VMEM((2, 1024, 128), F32),
        pltpu.VMEM((2, 1088, 128), F32),
        pltpu.VMEM((2, 144, 128), F32),
        pltpu.VMEM((2, 128, 1024), BF16),
        pltpu.VMEM((2, 128, 1024), F32),
        pltpu.VMEM((2, 128, 512), F32),
        pltpu.VMEM((2, 128, 1024), BF16),
        pltpu.VMEM((2, 256, 128), BF16),
    ]


def weight_scratch():
    return [pltpu.VMEM((2, 1024, 512), BF16), pltpu.VMEM((2, 512, 1024), BF16)]


def away_kernel(keep, low, high, out_o):
    out_o[0:320, :] = add2(keep[1, 0:320], low[...])
    out_o[320:576, :] = add2(keep[1, 320:576], high[...])


def away_grads_kernel(keep, low, after, out_o):
    out_o[...] = add2(keep[1, 0:320], low[...])


def away_outs_kernel(keep, high, after, out_o):
    out_o[...] = add2(keep[1, 320:576], high[...])


def gathered_body(inputs, cotangent, gate_values, routes, pair_weight, up_weight, down_weight):
    gates, choices = gate_values.T, routes.T
    width = 2 * WIDTH + 128
    payload, own, pair_own = kernel_call(
        payload_kernel,
        (
            shape((HALF, width)),
            shape((2 * HALF, width)),
            shape((2, 256, 256)),
        ),
        "hhhhh",
        scratch=[
            pltpu.VMEM((2, 128), F32),
            pltpu.VMEM((2, 128), jnp.int32),
            pltpu.SemaphoreType.DMA((7,)),
        ],
        vmem=60,
    )(inputs, cotangent, gates, choices, pair_weight)
    got = [swap(payload, "expert", 1), swap(payload, "expert", 2)]
    got.append(swap(got[1], "expert", 1))
    both = shape((2, 256, 256))
    own, pair_own = kernel_call(
        stage_kernel, (shape((2 * HALF, width)), both), "vv"
    )(own, pair_own)
    pair_x = swap(pair_own, "tensor", 2)
    pair_x = kernel_call(after_kernel, both, "va")(pair_x, got[1])
    pair_c = swap(pair_own, "tensor", 1)
    pair_d = swap(pair_x, "tensor", 1)
    near_other = swap(got[0], "tensor", 1)
    chunk = kernel_call(
        own_chunk_kernel,
        chunk_outs() + (shape((2, 256, 1024)),),
        "vvvvvvvhh",
        scratch=[
            pltpu.VMEM((256, 2048), BF16),
            pltpu.VMEM((256, 128), BF16),
        ]
        + weight_scratch()
        + [pltpu.SemaphoreType.DMA((2,))]
        + chunk_scratch(),
        flops=4_000_000_000,
        nbytes=10_000_000,
    )(
        own, pair_own, got[0], near_other,
        pair_c, pair_x, pair_d, up_weight, down_weight,
    )
    keep, here, away, last, cross, act, grad, pre, gram, pick, gate, pair_all = chunk
    away = kernel_call(away_kernel, shape((576, 256)), "vvv")(
        keep, swap(away, "tensor", 1), swap(last, "tensor", 1)
    )
    theirs = swap(away, "tensor", 2)
    other = swap(here, "tensor", 1)
    far_mine = kernel_call(join_kernel, shape((2 * HALF, 2 * WIDTH + 128)), "vva")(
        got[1], got[2], gate
    )
    far_other = swap(far_mine, "tensor", 1)
    chunk = kernel_call(
        far_chunk_kernel,
        chunk_outs(),
        "vvvhh",
        scratch=[pltpu.VMEM((256, 2048), BF16), pltpu.VMEM((256, 128), BF16)]
        + weight_scratch()
        + [pltpu.SemaphoreType.DMA((2,))]
        + chunk_scratch(),
        flops=4_000_000_000,
        nbytes=10_000_000,
    )(far_mine, far_other, pair_all, up_weight, down_weight)
    fkeep, fhere, faway, flast, fcross, fact, fgrad, fpre, fgram, fpick, fgate = chunk
    fother = swap(fhere, "tensor", 1)
    fgrads = kernel_call(away_grads_kernel, shape((320, 256)), "vva")(
        fkeep, swap(faway, "tensor", 1), theirs
    )
    fouts = kernel_call(away_outs_kernel, shape((256, 256)), "vva")(
        fkeep, swap(flast, "tensor", 1), fgrads
    )
    fgrads = swap(fgrads, "tensor", 2)
    part = shape((288, 256))
    own_part, near_part, rows = kernel_call(
        combine_kernel, (part, part, shape((2, 128, 256))), "vvvvva"
    )(keep, other, theirs, pick, gate, fouts)
    near_got = swap(near_part, "expert", 1)
    fouts = swap(fouts, "tensor", 2)
    grad_down, grad_up, weights_done = kernel_call(
        weights_kernel,
        (shape((2, 512, 1024)), shape((2, 1024, 512)), shape((8, 128), F32)),
        "vvvvvvvv",
        flops=3_000_000_000,
        nbytes=8_000_000,
    )(act, grad, cross, pre, fact, fgrad, fcross, fpre)
    part = shape((160, 256))
    grads2, grads3, frows = kernel_call(
        far_grads_kernel, (part, part, shape((2, 128, 256))), "vvvva"
    )(fkeep, fother, fgrads, fpick, weights_done)
    grads2 = kernel_call(sum_kernel, part, "vv")(grads2, swap(grads3, "expert", 1))
    far_grads = swap(grads2, "expert", 2)
    part = shape((128, 256))
    outs2, outs3 = kernel_call(far_outs_kernel, (part, part), "vvvvva")(
        fkeep, fother, fouts, fpick, fgate, near_got
    )
    outs2 = kernel_call(sum_kernel, part, "vv")(outs2, swap(outs3, "expert", 1))
    far_outs = swap(outs2, "expert", 2)
    grad_pair = kernel_call(
        pair_kernel, shape((2, 256, 256)), "vvvv", flops=300_000_000, nbytes=2_000_000
    )(gram, rows, fgram, frows)
    mixed, grad_input = kernel_call(
        final_kernel,
        (shape((128, 256)), shape((128, 256))),
        "vvvvv",
        scratch=[pltpu.VMEM((1024, 128), F32)],
        flops=100_000_000,
        nbytes=1_000_000,
    )(own, own_part, near_got, far_grads, far_outs)
    return mixed, grad_input, grad_pair, grad_up, grad_down


def solution(mesh):
    placed = (
        P(("group", "expert"), None),
        P(("group", "expert"), None),
        P(("group", "expert"), None),
        P(("group", "expert"), None),
        P("expert", None, "tensor"),
        P("expert", None, "tensor"),
        P("expert", "tensor", None),
    )
    small = mesh.shape["expert"] == 4 and mesh.shape["tensor"] == 4
    return jax.shard_map(
        gathered_body if small else body,
        mesh=mesh,
        in_specs=placed,
        out_specs=(
            P(("group", "expert"), "tensor"),
            P(("group", "expert"), "tensor"),
            P(("group", "expert"), None, "tensor"),
            P(("group", "expert"), None, "tensor"),
            P(("group", "expert"), "tensor", None),
        ),
        check_vma=False,
    )
```

```python
import functools

import jax
import jax.numpy as jnp
from jax import lax
from jax.experimental import pallas as pl
from jax.experimental.pallas import tpu as pltpu
from jax.sharding import PartitionSpec as P

NF = 16
DE = 64


def dispatch_tables(routes, expert_total, capacity):
    row_count, pick_count = routes.shape
    flat_ids = routes.reshape(-1)
    onehot = (flat_ids[:, None] == jnp.arange(expert_total, dtype=jnp.int32)[None, :]).astype(
        jnp.int32
    )
    before = jnp.cumsum(onehot, axis=0) - onehot
    position = jnp.sum(before * onehot, axis=1)
    slot_index = flat_ids * capacity + position
    slot_count = expert_total * capacity
    tables = slot_index[:, None] == jnp.arange(slot_count, dtype=jnp.int32)[None, :]
    tables = tables.reshape(row_count, pick_count, slot_count)
    return jnp.transpose(tables, (1, 2, 0)).astype(jnp.bfloat16)


def body(inputs, cotangent, gate_values, routes, pair_weight, up_weight, down_weight):
    local_count = up_weight.shape[0]
    expert_count = lax.axis_size("expert")
    tensor_count = lax.axis_size("tensor")
    expert_total = local_count * expert_count
    row_count, pick_count = routes.shape
    feature_width = inputs.shape[1]
    capacity = 2 * row_count * pick_count // expert_total
    expert_rows = expert_count * capacity
    part_width = feature_width // tensor_count
    tensor_index = lax.axis_index("tensor")
    feature_start = tensor_index * part_width
    tables = dispatch_tables(routes, expert_total, capacity)
    any_table = jnp.sum(tables, axis=0)
    scaled = (gate_values[:, :, None] * cotangent[:, None, :].astype(jnp.float32)).astype(
        jnp.bfloat16
    )
    input_slice = lax.dynamic_slice_in_dim(inputs, feature_start, part_width, 1)
    cotangent_slice = lax.dynamic_slice_in_dim(cotangent, feature_start, part_width, 1)
    input_slots = jnp.dot(any_table, inputs, preferred_element_type=jnp.float32).astype(
        jnp.bfloat16
    )
    grad_slots = jnp.einsum(
        "ksr,rkd->sd", tables, scaled, preferred_element_type=jnp.float32
    ).astype(jnp.bfloat16)
    send_shape = (expert_count, local_count, capacity, feature_width)
    input_homes, grad_homes = (
        lax.all_to_all(
            input_slots.reshape(send_shape), "expert", split_axis=0, concat_axis=2, tiled=True
        ),
        lax.all_to_all(
            grad_slots.reshape(send_shape), "expert", split_axis=0, concat_axis=2, tiled=True
        ),
    )
    input_rows = input_homes.reshape(local_count, expert_rows, feature_width)
    grad_rows = grad_homes.reshape(local_count, expert_rows, feature_width)
    cells = jnp.transpose(input_rows.reshape(local_count, expert_rows, NF, DE), (0, 2, 3, 1))
    gram = jnp.einsum("eidr,ejdr->eijr", cells, cells, preferred_element_type=jnp.float32) / DE
    gram_flat = gram.reshape(local_count, NF * NF, expert_rows).astype(jnp.bfloat16)
    input_mine = lax.dynamic_slice_in_dim(input_rows, feature_start, part_width, 2)
    cross_sum = input_mine.astype(jnp.float32) + jnp.einsum(
        "epr,epd->erd", gram_flat, pair_weight, preferred_element_type=jnp.float32
    )
    cross_part = cross_sum.astype(jnp.bfloat16)
    cross_whole = lax.all_gather(cross_part, "tensor", axis=2, tiled=True)
    hidden_pre = jnp.einsum(
        "erd,edh->erh", cross_whole, up_weight, preferred_element_type=jnp.float32
    )
    hidden_act = jax.nn.silu(hidden_pre).astype(jnp.bfloat16)
    out_terms = jnp.einsum(
        "erh,ehd->erd", hidden_act, down_weight, preferred_element_type=jnp.float32
    )
    out_mine = lax.psum_scatter(
        out_terms.astype(jnp.bfloat16), "tensor", scatter_dimension=2, tiled=True
    )
    grad_act = jnp.einsum(
        "erd,ehd->erh", grad_rows, down_weight, preferred_element_type=jnp.float32
    )
    sigmoid_pre = jax.nn.sigmoid(hidden_pre)
    grad_pre = (grad_act * sigmoid_pre * (1.0 + hidden_pre * (1.0 - sigmoid_pre))).astype(
        jnp.bfloat16
    )
    grad_down = jnp.einsum(
        "erh,erd->ehd", hidden_act, grad_rows, preferred_element_type=jnp.float32
    ).astype(jnp.bfloat16)
    grad_up = jnp.einsum(
        "erd,erh->edh", cross_whole, grad_pre, preferred_element_type=jnp.float32
    ).astype(jnp.bfloat16)
    cross_terms = jnp.einsum(
        "erh,edh->erd", grad_pre, up_weight, preferred_element_type=jnp.float32
    )
    grad_cross = lax.psum_scatter(
        cross_terms.astype(jnp.bfloat16), "tensor", scatter_dimension=2, tiled=True
    )
    grad_pair = jnp.einsum(
        "epr,erd->epd", gram_flat, grad_cross, preferred_element_type=jnp.float32
    ).astype(jnp.bfloat16)
    pair_terms = jnp.einsum(
        "erd,epd->epr", grad_cross, pair_weight, preferred_element_type=jnp.float32
    )
    grad_gram = (
        lax.psum(pair_terms.astype(jnp.bfloat16), "tensor")
        .astype(jnp.float32)
        .reshape(local_count, NF, NF, expert_rows)
    )
    symmetric = grad_gram + jnp.swapaxes(grad_gram, 1, 2)
    field_count = part_width // DE
    symmetric_mine = lax.dynamic_slice_in_dim(symmetric, tensor_index * field_count, field_count, 1)
    gram_back = (
        jnp.einsum(
            "eijr,ejdr->eidr",
            symmetric_mine,
            cells.astype(jnp.float32),
            precision=lax.Precision.HIGHEST,
        )
        / DE
    )
    gram_back = jnp.transpose(gram_back, (0, 3, 1, 2)).reshape(local_count, expert_rows, part_width)
    grad_mine = (grad_cross.astype(jnp.float32) + gram_back).astype(jnp.bfloat16)
    back_shape = (1, local_count, expert_rows, part_width)
    out_back, grad_back = (
        lax.all_to_all(
            out_mine.reshape(back_shape), "expert", split_axis=2, concat_axis=0, tiled=True
        ),
        lax.all_to_all(
            grad_mine.reshape(back_shape), "expert", split_axis=2, concat_axis=0, tiled=True
        ),
    )
    out_back = out_back.reshape(expert_total * capacity, part_width)
    grad_back = grad_back.reshape(expert_total * capacity, part_width)
    picked = jnp.einsum("ksr,sd->rkd", tables, out_back, preferred_element_type=jnp.float32)
    mixed = (
        input_slice.astype(jnp.float32) + jnp.sum(gate_values[:, :, None] * picked, axis=1)
    ).astype(jnp.bfloat16)
    grad_input = (
        cotangent_slice.astype(jnp.float32)
        + jnp.dot(any_table.T, grad_back, preferred_element_type=jnp.float32)
    ).astype(jnp.bfloat16)
    return (mixed, grad_input, grad_pair, grad_up, grad_down)


F32 = jnp.float32
BF16 = jnp.bfloat16
NT = (((1,), (1,)), ((), ()))
TN = (((0,), (0,)), ((), ()))
WIDTH = 1024
HALF = 64


def mm(a, b, dims=None):
    if dims is None:
        return jnp.dot(a, b, preferred_element_type=F32)
    return lax.dot_general(a, b, dims, preferred_element_type=F32)


def kernel_call(kernel, out_shape, where, scratch=(), flops=0, nbytes=0, vmem=48):
    kinds = {"v": pltpu.VMEM, "a": pl.ANY, "h": pltpu.HBM}
    return pl.pallas_call(
        kernel,
        out_shape=out_shape,
        in_specs=[pl.BlockSpec(memory_space=kinds[w]) for w in where],
        scratch_shapes=list(scratch),
        compiler_params=pltpu.CompilerParams(vmem_limit_bytes=vmem * 1024 * 1024),
        cost_estimate=pl.CostEstimate(flops=flops, bytes_accessed=nbytes, transcendentals=0),
    )


def shape(dims, dtype=BF16):
    return jax.ShapeDtypeStruct(dims, dtype)


def load(pairs, sems):
    copies = [pltpu.make_async_copy(a, b, sems.at[n]) for n, (a, b) in enumerate(pairs)]
    for copy in copies:
        copy.start()
    return copies


def payload_kernel(x, c, gates_in, routes_in, pair_in, out_o, own_o, pair_o, gates, routes, sems):
    core = lax.rem(lax.axis_index("tensor"), 2)
    mine = pl.ds(pl.multiple_of(core * HALF, HALF), HALF)
    copies = load(
        [
            (gates_in, gates),
            (routes_in, routes),
            (x.at[mine, :], out_o.at[:, 0:WIDTH]),
            (c.at[mine, :], out_o.at[:, WIDTH : 2 * WIDTH]),
            (x, own_o.at[:, 0:WIDTH]),
            (c, own_o.at[:, WIDTH : 2 * WIDTH]),
            (pair_in, pair_o),
        ],
        sems,
    )
    copies[0].wait()
    copies[1].wait()
    high = gates[...].astype(BF16).astype(F32)
    low = gates[...] - high
    meta = jnp.concatenate(
        [routes[...].astype(F32), high, low, jnp.zeros((122, 128), F32)], axis=0
    )
    columns = meta.T
    own_o[:, 2 * WIDTH :] = columns.astype(BF16)
    out_o[:, 2 * WIDTH :] = jnp.where(core == 0, columns[0:HALF], columns[HALF:]).astype(BF16)
    for copy in copies[2:]:
        copy.wait()


def after_kernel(value, after, out_o):
    out_o[...] = value[...]


def stage_kernel(own, pair, own_o, pair_o):
    own_o[...] = own[...]
    pair_o[...] = pair[...]


def join_kernel(a, b, after, out_o):
    out_o[0:HALF, :] = a[...]
    out_o[HALF : 2 * HALF, :] = b[...]


def place_rows(whole, info, block, core, near, far):
    for at, piece in ((core, near), (1 - core, far)):
        rows = pl.ds(pl.multiple_of(block * 128 + at * HALF, HALF), HALF)
        whole[rows, :] = piece[:, 0 : 2 * WIDTH]
        info[rows, :] = piece[:, 2 * WIDTH :]


def towers(meta, whole, up, down, ready, pair, outs, scratch):
    keep, send_here, send_away, send_last, cross_o, act_o, grad_o, pre_o, gram_o, pick_o, gate_o = outs
    flipped, partial, half_gram, terms, rows, slope, outs_s, backs = scratch
    j = lax.axis_index("tensor")
    core = lax.rem(j, 2)
    xi = j // 2
    first = lax.axis_index("expert") * 2
    tokens = meta.shape[1]
    before = (
        lax.broadcasted_iota(jnp.int32, (tokens, tokens), 0)
        < lax.broadcasted_iota(jnp.int32, (tokens, tokens), 1)
    ).astype(F32).astype(BF16)
    a = lax.broadcasted_iota(jnp.int32, (256, 144), 0)
    n = lax.broadcasted_iota(jnp.int32, (256, 144), 1)
    low = jnp.minimum(a // 16, a % 16)
    high = jnp.maximum(a // 16, a % 16)
    spread = jnp.where(low * 16 - low * (low - 1) // 2 + high - low == n, 1.0, 0.0).astype(BF16)
    a = lax.broadcasted_iota(jnp.int32, (256, 256), 0)
    b = lax.broadcasted_iota(jnp.int32, (256, 256), 1)
    swapped = (a % 16) * 16 + a // 16
    both = (jnp.where(a == b, 1.0, 0.0) + jnp.where(swapped == b, 1.0, 0.0)).astype(BF16)
    slots = lax.broadcasted_iota(jnp.int32, (128, tokens), 0).astype(F32)
    both_e = range(2)
    for e in both_e:
        mine = (first + e).astype(F32)
        s0 = meta[0:1, :] == mine
        s1 = meta[1:2, :] == mine
        named = jnp.where(s0, 1.0, 0.0) + jnp.where(s1, 1.0, 0.0)
        gate = jnp.where(s0, meta[2:3, :], 0.0) + jnp.where(s1, meta[3:4, :], 0.0)
        place = mm(jnp.broadcast_to(named, (8, tokens)).astype(BF16), before)[0:1, :]
        place = jnp.where(named > 0.5, place, -1.0)
        hit = slots == place
        pick_o[e] = jnp.where(hit, 1.0, 0.0).astype(BF16)
        weight = jnp.sum(jnp.where(hit, gate, 0.0), axis=1, keepdims=True)
        gate_o[e] = jnp.broadcast_to(weight, (128, 128))
    for e in both_e:
        rows[e] = mm(pick_o[e], whole[:, 0:WIDTH])
    for e in both_e:
        flipped[e] = rows[e].T
    for e in both_e:
        grad = mm(pick_o[e], whole[:, WIDTH : 2 * WIDTH])
        grad_o[e] = (gate_o[e][:, 0:1] * grad).astype(BF16)
    for e in both_e:
        half_gram[e, 136:144, :] = jnp.zeros((8, 128), F32)
        at = 0
        for i in range(16):
            left = flipped[e, i * 64 : i * 64 + 64, :]
            for q in range(i, 16):
                prod = left * flipped[e, q * 64 : q * 64 + 64, :]
                partial[e, at * 8 : at * 8 + 8, :] = jnp.sum(prod.reshape(8, 8, 128), axis=0)
                at += 1
        for g in range(17):
            acc = partial[e, pl.ds(g * 64, 8, stride=8), :]
            for q in range(1, 8):
                acc = acc + partial[e, pl.ds(g * 64 + q, 8, stride=8), :]
            half_gram[e, g * 8 : g * 8 + 8, :] = acc * (1.0 / DE)
        gram_o[e] = mm(spread, half_gram[e].astype(BF16)).astype(BF16)
    for e in both_e:
        cross_o[e] = (rows[e] + mm(gram_o[e], pair[e], TN)).astype(BF16)
    for copy in ready:
        copy.wait()
    for e in both_e:
        slope[e] = mm(grad_o[e], down[e], NT)
    for e in both_e:
        pre = mm(cross_o[e], up[e])
        sig = jax.nn.sigmoid(pre)
        act_o[e] = (pre * sig).astype(BF16)
        pre_o[e] = (slope[e] * sig * (1.0 + pre * (1.0 - sig))).astype(BF16)
    for e in both_e:
        terms[e] = mm(pre_o[e], up[e], NT).astype(BF16)
    for e in both_e:
        outs_s[e] = mm(act_o[e], down[e]).astype(BF16)
    for e in both_e:
        back = mm(pair[e], terms[e], NT).astype(BF16)
        backs[e] = mm(both, back).astype(BF16)
    for xr in (1, 0):
        for part in (1, 0):
            block = 2 * (xi ^ xr) + (core ^ part)
            cols = pl.ds(pl.multiple_of(block * 256, 256), 256)
            if part == 0:
                low, high = keep.at[xr, 0:320], keep.at[xr, 320:576]
            elif xr == 0:
                low, high = send_here.at[0:320], send_here.at[320:576]
            else:
                low, high = send_away, send_last
            for e in both_e:
                mine = slice(e * 128, e * 128 + 128)
                low[mine, :] = terms[e, :, cols]
                high[mine, :] = outs_s[e, :, cols]
                rows64 = pl.ds(pl.multiple_of(block * 64, 64), 64)
                low[256:320, mine] = backs[e, rows64, :]


def read_meta(info):
    rows = info[...].astype(F32).T
    return jnp.concatenate([rows[0:2], rows[2:4] + rows[4:6]], axis=0)


def own_chunk_kernel(*refs):
    own, p0, near, far, p1, p2, p3, up_in, down_in = refs[:9]
    outs, pair_o = refs[9:20], refs[20]
    whole, info, up, down, sems = refs[21:26]
    j = lax.axis_index("tensor")
    copies = load([(up_in, up), (down_in, down)], sems)
    whole[0:128, :] = own[:, 0 : 2 * WIDTH]
    info[0:128, :] = own[:, 2 * WIDTH :]
    place_rows(whole, info, 1, lax.rem(j, 2), near, far)
    for k, piece in enumerate((p0, p1, p2, p3)):
        cols = pl.ds(pl.multiple_of((j ^ k) * 256, 256), 256)
        for e in range(2):
            pair_o[e, :, cols] = piece[e]
    towers(read_meta(info), whole, up, down, copies, pair_o, outs, refs[26:])


def far_chunk_kernel(*refs):
    near, far, pair, up_in, down_in = refs[:5]
    outs = refs[5:16]
    whole, info, up, down, sems = refs[16:21]
    core = lax.rem(lax.axis_index("tensor"), 2)
    copies = load([(up_in, up), (down_in, down)], sems)
    for r in range(2):
        rows = slice(r * HALF, r * HALF + HALF)
        place_rows(whole, info, r, core, near.at[rows, :], far.at[rows, :])
    towers(read_meta(info), whole, up, down, copies, pair, outs, refs[21:])


def weights_kernel(act0, grad0, cross0, pre0, act1, grad1, cross1, pre1, down_o, up_o, done_o):
    done_o[...] = jnp.zeros((8, 128), F32)

    def stack(a, b):
        return jnp.concatenate([a, b], axis=0)

    for e in range(2):
        down_o[e] = mm(stack(act0[e], act1[e]), stack(grad0[e], grad1[e]), TN).astype(BF16)
        up_o[e] = mm(stack(cross0[e], cross1[e]), stack(pre0[e], pre1[e]), TN).astype(BF16)


def add2(a, b):
    return (a.astype(F32) + b.astype(F32)).astype(BF16)


def combine_grads(both, picks, rows_o):
    grads = jnp.zeros((256, 256), F32)
    back = jnp.zeros((64, 256), F32)
    for e in range(2):
        rows = both[e * 128 : e * 128 + 128]
        rows_o[e] = rows
        grads = grads + mm(picks[e], rows, TN)
        back = back + mm(both[256:320, e * 128 : e * 128 + 128], picks[e])
    return grads.astype(BF16), back.astype(BF16)


def put_grads(dst, grads, back, p):
    rows = slice(p * 128, p * 128 + 128)
    dst[0:128, :] = grads[rows]
    dst[128:160, 0:128] = back[0:32, rows]
    dst[128:160, 128:256] = back[32:64, rows]


def combine_outs(both, picks, gates):
    mixed = jnp.zeros((256, 256), F32)
    for e in range(2):
        out = both[e * 128 : e * 128 + 128].astype(F32) * gates[e][:, 0:1]
        mixed = mixed + mm(picks[e], out.astype(BF16), TN)
    return mixed.astype(BF16)


def combine_kernel(mine, other, theirs, pick, gate, after, first_o, second_o, rows_o):
    both = add2(add2(mine[0], other[...]), theirs[...])
    grads, back = combine_grads(both[0:320], pick, rows_o)
    mixed = combine_outs(both[320:576], pick, gate)
    for p, dst in enumerate((first_o, second_o)):
        put_grads(dst, grads, back, p)
        dst[160:288, :] = mixed[p * 128 : p * 128 + 128]


def far_grads_kernel(mine, other, theirs, pick, after, first_o, second_o, rows_o):
    both = add2(add2(mine[0, 0:320], other[0:320]), theirs[...])
    grads, back = combine_grads(both, pick, rows_o)
    for p, dst in enumerate((first_o, second_o)):
        put_grads(dst, grads, back, p)


def far_outs_kernel(mine, other, theirs, pick, gate, after, first_o, second_o):
    both = add2(add2(mine[0, 320:576], other[320:576]), theirs[...])
    mixed = combine_outs(both, pick, gate)
    first_o[...] = mixed[0:128]
    second_o[...] = mixed[128:256]


def sum_kernel(a, b, out_o):
    out_o[...] = add2(a[...], b[...])


def pair_kernel(gram0, rows0, gram1, rows1, out_o):
    for e in range(2):
        out_o[e] = (mm(gram0[e], rows0[e]) + mm(gram1[e], rows1[e])).astype(BF16)


def final_kernel(own, g0, g1, far_grads, far_outs, mixed_o, grad_o, flipped):
    column = pl.multiple_of(lax.axis_index("tensor") * 256, 256)
    mixed = own[:, pl.ds(column, 256)].astype(F32) + far_outs[...].astype(F32)
    total = own[:, pl.ds(WIDTH + column, 256)].astype(F32)
    back = jnp.zeros((32, 256), F32)
    for g in (g0, g1, far_grads):
        total = total + g[0:128, :].astype(F32)
        back = back + g[128:160, :].astype(F32)
    for g in (g0, g1):
        mixed = mixed + g[160:288, :].astype(F32)
    mixed_o[...] = mixed.astype(BF16)
    flipped[...] = own[:, 0:WIDTH].astype(F32).T
    back = jnp.concatenate([back[:, 0:128], back[:, 128:256]], axis=0)
    pieces = []
    for i in range(4):
        acc = jnp.zeros((64, 128), F32)
        for q in range(16):
            acc = acc + back[i * 16 + q : i * 16 + q + 1, :] * flipped[q * 64 : q * 64 + 64, :]
        pieces.append(acc)
    gram_back = jnp.concatenate(pieces, axis=0) * (1.0 / DE)
    grad_o[...] = (total + gram_back.T).astype(BF16)


def swap(value, axis, mask):
    size = lax.axis_size(axis)
    return lax.ppermute(value, axis, [(i, i ^ mask) for i in range(size)])


def chunk_outs():
    return (
        shape((2, 576, 256)),
        shape((576, 256)),
        shape((320, 256)),
        shape((256, 256)),
        shape((2, 128, 1024)),
        shape((2, 128, 512)),
        shape((2, 128, 1024)),
        shape((2, 128, 512)),
        shape((2, 256, 128)),
        shape((2, 128, 256)),
        shape((2, 128, 128), F32),
    )


def chunk_scratch():
    return [
        pltpu.VMEM((2, 1024, 128), F32),
        pltpu.VMEM((2, 1088, 128), F32),
        pltpu.VMEM((2, 144, 128), F32),
        pltpu.VMEM((2, 128, 1024), BF16),
        pltpu.VMEM((2, 128, 1024), F32),
        pltpu.VMEM((2, 128, 512), F32),
        pltpu.VMEM((2, 128, 1024), BF16),
        pltpu.VMEM((2, 256, 128), BF16),
    ]


def weight_scratch():
    return [pltpu.VMEM((2, 1024, 512), BF16), pltpu.VMEM((2, 512, 1024), BF16)]


def away_kernel(keep, low, high, out_o):
    out_o[0:320, :] = add2(keep[1, 0:320], low[...])
    out_o[320:576, :] = add2(keep[1, 320:576], high[...])


def away_grads_kernel(keep, low, out_o):
    out_o[...] = add2(keep[1, 0:320], low[...])


def away_outs_kernel(keep, high, after, after2, out_o):
    out_o[...] = add2(keep[1, 320:576], high[...])


def gathered_body(inputs, cotangent, gate_values, routes, pair_weight, up_weight, down_weight):
    gates, choices = gate_values.T, routes.T
    width = 2 * WIDTH + 128
    payload, own, pair_own = kernel_call(
        payload_kernel,
        (
            shape((HALF, width)),
            shape((2 * HALF, width)),
            shape((2, 256, 256)),
        ),
        "hhhhh",
        scratch=[
            pltpu.VMEM((2, 128), F32),
            pltpu.VMEM((2, 128), jnp.int32),
            pltpu.SemaphoreType.DMA((7,)),
        ],
        vmem=60,
    )(inputs, cotangent, gates, choices, pair_weight)
    got = [swap(payload, "expert", 1), swap(payload, "expert", 2)]
    got.append(swap(got[1], "expert", 1))
    both = shape((2, 256, 256))
    own, pair_own = kernel_call(
        stage_kernel, (shape((2 * HALF, width)), both), "vv"
    )(own, pair_own)
    pair_x = swap(pair_own, "tensor", 2)
    pair_x = kernel_call(after_kernel, both, "va", flops=30_000_000)(pair_x, got[1])
    pair_c = swap(pair_own, "tensor", 1)
    pair_d = swap(pair_x, "tensor", 1)
    near = kernel_call(after_kernel, shape((HALF, width)), "va")(got[0], got[1])
    near_other = swap(near, "tensor", 1)
    chunk = kernel_call(
        own_chunk_kernel,
        chunk_outs() + (shape((2, 256, 1024)),),
        "vvvvvvvhh",
        scratch=[
            pltpu.VMEM((256, 2048), BF16),
            pltpu.VMEM((256, 128), BF16),
        ]
        + weight_scratch()
        + [pltpu.SemaphoreType.DMA((2,))]
        + chunk_scratch(),
        flops=4_000_000_000,
        nbytes=10_000_000,
    )(
        own, pair_own, got[0], near_other,
        pair_c, pair_x, pair_d, up_weight, down_weight,
    )
    keep, here, away, last, cross, act, grad, pre, gram, pick, gate, pair_all = chunk
    away = kernel_call(away_kernel, shape((576, 256)), "vvv")(
        keep, swap(away, "tensor", 1), swap(last, "tensor", 1)
    )
    theirs = swap(away, "tensor", 2)
    other = swap(here, "tensor", 1)
    far_mine = kernel_call(join_kernel, shape((2 * HALF, 2 * WIDTH + 128)), "vva")(
        got[1], got[2], gate
    )
    far_other = swap(far_mine, "tensor", 1)
    chunk = kernel_call(
        far_chunk_kernel,
        chunk_outs(),
        "vvvhh",
        scratch=[pltpu.VMEM((256, 2048), BF16), pltpu.VMEM((256, 128), BF16)]
        + weight_scratch()
        + [pltpu.SemaphoreType.DMA((2,))]
        + chunk_scratch(),
        flops=4_000_000_000,
        nbytes=10_000_000,
    )(far_mine, far_other, pair_all, up_weight, down_weight)
    fkeep, fhere, faway, flast, fcross, fact, fgrad, fpre, fgram, fpick, fgate = chunk
    fother = swap(fhere, "tensor", 1)
    fgrads = kernel_call(away_grads_kernel, shape((320, 256)), "vv")(
        fkeep, swap(faway, "tensor", 1)
    )
    fouts = kernel_call(away_outs_kernel, shape((256, 256)), "vvaa")(
        fkeep, swap(flast, "tensor", 1), fgrads, theirs
    )
    fgrads = swap(fgrads, "tensor", 2)
    part = shape((288, 256))
    own_part, near_part, rows = kernel_call(
        combine_kernel, (part, part, shape((2, 128, 256))), "vvvvva"
    )(keep, other, theirs, pick, gate, fouts)
    near_got = swap(near_part, "expert", 1)
    fouts = swap(fouts, "tensor", 2)
    grad_down, grad_up, weights_done = kernel_call(
        weights_kernel,
        (shape((2, 512, 1024)), shape((2, 1024, 512)), shape((8, 128), F32)),
        "vvvvvvvv",
        flops=3_000_000_000,
        nbytes=8_000_000,
    )(act, grad, cross, pre, fact, fgrad, fcross, fpre)
    part = shape((160, 256))
    grads2, grads3, frows = kernel_call(
        far_grads_kernel, (part, part, shape((2, 128, 256))), "vvvva"
    )(fkeep, fother, fgrads, fpick, weights_done)
    grads2 = kernel_call(sum_kernel, part, "vv")(grads2, swap(grads3, "expert", 1))
    far_grads = swap(grads2, "expert", 2)
    part = shape((128, 256))
    outs2, outs3 = kernel_call(far_outs_kernel, (part, part), "vvvvva")(
        fkeep, fother, fouts, fpick, fgate, near_got
    )
    outs2 = kernel_call(sum_kernel, part, "vv")(outs2, swap(outs3, "expert", 1))
    far_outs = swap(outs2, "expert", 2)
    grad_pair = kernel_call(
        pair_kernel, shape((2, 256, 256)), "vvvv", flops=300_000_000, nbytes=2_000_000
    )(gram, rows, fgram, frows)
    mixed, grad_input = kernel_call(
        final_kernel,
        (shape((128, 256)), shape((128, 256))),
        "vvvvv",
        scratch=[pltpu.VMEM((1024, 128), F32)],
        flops=100_000_000,
        nbytes=1_000_000,
    )(own, own_part, near_got, far_grads, far_outs)
    return mixed, grad_input, grad_pair, grad_up, grad_down


def solution(mesh):
    placed = (
        P(("group", "expert"), None),
        P(("group", "expert"), None),
        P(("group", "expert"), None),
        P(("group", "expert"), None),
        P("expert", None, "tensor"),
        P("expert", None, "tensor"),
        P("expert", "tensor", None),
    )
    small = mesh.shape["expert"] == 4 and mesh.shape["tensor"] == 4
    return jax.shard_map(
        gathered_body if small else body,
        mesh=mesh,
        in_specs=placed,
        out_specs=(
            P(("group", "expert"), "tensor"),
            P(("group", "expert"), "tensor"),
            P(("group", "expert"), None, "tensor"),
            P(("group", "expert"), None, "tensor"),
            P(("group", "expert"), "tensor", None),
        ),
        check_vma=False,
    )
```

```python
import functools

import jax
import jax.numpy as jnp
from jax import lax
from jax.experimental import pallas as pl
from jax.experimental.pallas import tpu as pltpu
from jax.sharding import PartitionSpec as P

NF = 16
DE = 64


def dispatch_tables(routes, expert_total, capacity):
    row_count, pick_count = routes.shape
    flat_ids = routes.reshape(-1)
    onehot = (flat_ids[:, None] == jnp.arange(expert_total, dtype=jnp.int32)[None, :]).astype(
        jnp.int32
    )
    before = jnp.cumsum(onehot, axis=0) - onehot
    position = jnp.sum(before * onehot, axis=1)
    slot_index = flat_ids * capacity + position
    slot_count = expert_total * capacity
    tables = slot_index[:, None] == jnp.arange(slot_count, dtype=jnp.int32)[None, :]
    tables = tables.reshape(row_count, pick_count, slot_count)
    return jnp.transpose(tables, (1, 2, 0)).astype(jnp.bfloat16)


def body(inputs, cotangent, gate_values, routes, pair_weight, up_weight, down_weight):
    local_count = up_weight.shape[0]
    expert_count = lax.axis_size("expert")
    tensor_count = lax.axis_size("tensor")
    expert_total = local_count * expert_count
    row_count, pick_count = routes.shape
    feature_width = inputs.shape[1]
    capacity = 2 * row_count * pick_count // expert_total
    expert_rows = expert_count * capacity
    part_width = feature_width // tensor_count
    tensor_index = lax.axis_index("tensor")
    feature_start = tensor_index * part_width
    tables = dispatch_tables(routes, expert_total, capacity)
    any_table = jnp.sum(tables, axis=0)
    scaled = (gate_values[:, :, None] * cotangent[:, None, :].astype(jnp.float32)).astype(
        jnp.bfloat16
    )
    input_slice = lax.dynamic_slice_in_dim(inputs, feature_start, part_width, 1)
    cotangent_slice = lax.dynamic_slice_in_dim(cotangent, feature_start, part_width, 1)
    input_slots = jnp.dot(any_table, inputs, preferred_element_type=jnp.float32).astype(
        jnp.bfloat16
    )
    grad_slots = jnp.einsum(
        "ksr,rkd->sd", tables, scaled, preferred_element_type=jnp.float32
    ).astype(jnp.bfloat16)
    send_shape = (expert_count, local_count, capacity, feature_width)
    input_homes, grad_homes = (
        lax.all_to_all(
            input_slots.reshape(send_shape), "expert", split_axis=0, concat_axis=2, tiled=True
        ),
        lax.all_to_all(
            grad_slots.reshape(send_shape), "expert", split_axis=0, concat_axis=2, tiled=True
        ),
    )
    input_rows = input_homes.reshape(local_count, expert_rows, feature_width)
    grad_rows = grad_homes.reshape(local_count, expert_rows, feature_width)
    cells = jnp.transpose(input_rows.reshape(local_count, expert_rows, NF, DE), (0, 2, 3, 1))
    gram = jnp.einsum("eidr,ejdr->eijr", cells, cells, preferred_element_type=jnp.float32) / DE
    gram_flat = gram.reshape(local_count, NF * NF, expert_rows).astype(jnp.bfloat16)
    input_mine = lax.dynamic_slice_in_dim(input_rows, feature_start, part_width, 2)
    cross_sum = input_mine.astype(jnp.float32) + jnp.einsum(
        "epr,epd->erd", gram_flat, pair_weight, preferred_element_type=jnp.float32
    )
    cross_part = cross_sum.astype(jnp.bfloat16)
    cross_whole = lax.all_gather(cross_part, "tensor", axis=2, tiled=True)
    hidden_pre = jnp.einsum(
        "erd,edh->erh", cross_whole, up_weight, preferred_element_type=jnp.float32
    )
    hidden_act = jax.nn.silu(hidden_pre).astype(jnp.bfloat16)
    out_terms = jnp.einsum(
        "erh,ehd->erd", hidden_act, down_weight, preferred_element_type=jnp.float32
    )
    out_mine = lax.psum_scatter(
        out_terms.astype(jnp.bfloat16), "tensor", scatter_dimension=2, tiled=True
    )
    grad_act = jnp.einsum(
        "erd,ehd->erh", grad_rows, down_weight, preferred_element_type=jnp.float32
    )
    sigmoid_pre = jax.nn.sigmoid(hidden_pre)
    grad_pre = (grad_act * sigmoid_pre * (1.0 + hidden_pre * (1.0 - sigmoid_pre))).astype(
        jnp.bfloat16
    )
    grad_down = jnp.einsum(
        "erh,erd->ehd", hidden_act, grad_rows, preferred_element_type=jnp.float32
    ).astype(jnp.bfloat16)
    grad_up = jnp.einsum(
        "erd,erh->edh", cross_whole, grad_pre, preferred_element_type=jnp.float32
    ).astype(jnp.bfloat16)
    cross_terms = jnp.einsum(
        "erh,edh->erd", grad_pre, up_weight, preferred_element_type=jnp.float32
    )
    grad_cross = lax.psum_scatter(
        cross_terms.astype(jnp.bfloat16), "tensor", scatter_dimension=2, tiled=True
    )
    grad_pair = jnp.einsum(
        "epr,erd->epd", gram_flat, grad_cross, preferred_element_type=jnp.float32
    ).astype(jnp.bfloat16)
    pair_terms = jnp.einsum(
        "erd,epd->epr", grad_cross, pair_weight, preferred_element_type=jnp.float32
    )
    grad_gram = (
        lax.psum(pair_terms.astype(jnp.bfloat16), "tensor")
        .astype(jnp.float32)
        .reshape(local_count, NF, NF, expert_rows)
    )
    symmetric = grad_gram + jnp.swapaxes(grad_gram, 1, 2)
    field_count = part_width // DE
    symmetric_mine = lax.dynamic_slice_in_dim(symmetric, tensor_index * field_count, field_count, 1)
    gram_back = (
        jnp.einsum(
            "eijr,ejdr->eidr",
            symmetric_mine,
            cells.astype(jnp.float32),
            precision=lax.Precision.HIGHEST,
        )
        / DE
    )
    gram_back = jnp.transpose(gram_back, (0, 3, 1, 2)).reshape(local_count, expert_rows, part_width)
    grad_mine = (grad_cross.astype(jnp.float32) + gram_back).astype(jnp.bfloat16)
    back_shape = (1, local_count, expert_rows, part_width)
    out_back, grad_back = (
        lax.all_to_all(
            out_mine.reshape(back_shape), "expert", split_axis=2, concat_axis=0, tiled=True
        ),
        lax.all_to_all(
            grad_mine.reshape(back_shape), "expert", split_axis=2, concat_axis=0, tiled=True
        ),
    )
    out_back = out_back.reshape(expert_total * capacity, part_width)
    grad_back = grad_back.reshape(expert_total * capacity, part_width)
    picked = jnp.einsum("ksr,sd->rkd", tables, out_back, preferred_element_type=jnp.float32)
    mixed = (
        input_slice.astype(jnp.float32) + jnp.sum(gate_values[:, :, None] * picked, axis=1)
    ).astype(jnp.bfloat16)
    grad_input = (
        cotangent_slice.astype(jnp.float32)
        + jnp.dot(any_table.T, grad_back, preferred_element_type=jnp.float32)
    ).astype(jnp.bfloat16)
    return (mixed, grad_input, grad_pair, grad_up, grad_down)


F32 = jnp.float32
BF16 = jnp.bfloat16
NT = (((1,), (1,)), ((), ()))
TN = (((0,), (0,)), ((), ()))
WIDTH = 1024
HALF = 64


def mm(a, b, dims=None):
    if dims is None:
        return jnp.dot(a, b, preferred_element_type=F32)
    return lax.dot_general(a, b, dims, preferred_element_type=F32)


def kernel_call(kernel, out_shape, where, scratch=(), flops=0, nbytes=0, vmem=48):
    kinds = {"v": pltpu.VMEM, "a": pl.ANY, "h": pltpu.HBM}
    return pl.pallas_call(
        kernel,
        out_shape=out_shape,
        in_specs=[pl.BlockSpec(memory_space=kinds[w]) for w in where],
        scratch_shapes=list(scratch),
        compiler_params=pltpu.CompilerParams(vmem_limit_bytes=vmem * 1024 * 1024),
        cost_estimate=pl.CostEstimate(flops=flops, bytes_accessed=nbytes, transcendentals=0),
    )


def shape(dims, dtype=BF16):
    return jax.ShapeDtypeStruct(dims, dtype)


def load(pairs, sems):
    copies = [pltpu.make_async_copy(a, b, sems.at[n]) for n, (a, b) in enumerate(pairs)]
    for copy in copies:
        copy.start()
    return copies


def payload_kernel(x, c, gates_in, routes_in, pair_in, out_o, own_o, pair_o, gates, routes, sems):
    core = lax.rem(lax.axis_index("tensor"), 2)
    mine = pl.ds(pl.multiple_of(core * HALF, HALF), HALF)
    copies = load(
        [
            (gates_in, gates),
            (routes_in, routes),
            (x.at[mine, :], out_o.at[:, 0:WIDTH]),
            (c.at[mine, :], out_o.at[:, WIDTH : 2 * WIDTH]),
            (x, own_o.at[:, 0:WIDTH]),
            (c, own_o.at[:, WIDTH : 2 * WIDTH]),
            (pair_in, pair_o),
        ],
        sems,
    )
    copies[0].wait()
    copies[1].wait()
    high = gates[...].astype(BF16).astype(F32)
    low = gates[...] - high
    meta = jnp.concatenate(
        [routes[...].astype(F32), high, low, jnp.zeros((122, 128), F32)], axis=0
    )
    columns = meta.T
    own_o[:, 2 * WIDTH :] = columns.astype(BF16)
    out_o[:, 2 * WIDTH :] = jnp.where(core == 0, columns[0:HALF], columns[HALF:]).astype(BF16)
    for copy in copies[2:]:
        copy.wait()


def after_kernel(value, after, out_o):
    out_o[...] = value[...]


def stage_kernel(own, pair, own_o, pair_o):
    own_o[...] = own[...]
    pair_o[...] = pair[...]


def join_kernel(a, b, after, out_o):
    out_o[0:HALF, :] = a[...]
    out_o[HALF : 2 * HALF, :] = b[...]


def place_rows(whole, info, block, core, near, far):
    for at, piece in ((core, near), (1 - core, far)):
        rows = pl.ds(pl.multiple_of(block * 128 + at * HALF, HALF), HALF)
        whole[rows, :] = piece[:, 0 : 2 * WIDTH]
        info[rows, :] = piece[:, 2 * WIDTH :]


def towers(meta, whole, up, down, ready, pair, outs, scratch):
    keep, send_here, send_away, send_last, cross_o, act_o, grad_o, pre_o, gram_o, pick_o, gate_o = outs
    flipped, partial, half_gram, terms, rows, slope, outs_s, backs = scratch
    j = lax.axis_index("tensor")
    core = lax.rem(j, 2)
    xi = j // 2
    first = lax.axis_index("expert") * 2
    tokens = meta.shape[1]
    before = (
        lax.broadcasted_iota(jnp.int32, (tokens, tokens), 0)
        < lax.broadcasted_iota(jnp.int32, (tokens, tokens), 1)
    ).astype(F32).astype(BF16)
    a = lax.broadcasted_iota(jnp.int32, (256, 144), 0)
    n = lax.broadcasted_iota(jnp.int32, (256, 144), 1)
    low = jnp.minimum(a // 16, a % 16)
    high = jnp.maximum(a // 16, a % 16)
    spread = jnp.where(low * 16 - low * (low - 1) // 2 + high - low == n, 1.0, 0.0).astype(BF16)
    a = lax.broadcasted_iota(jnp.int32, (256, 256), 0)
    b = lax.broadcasted_iota(jnp.int32, (256, 256), 1)
    swapped = (a % 16) * 16 + a // 16
    both = (jnp.where(a == b, 1.0, 0.0) + jnp.where(swapped == b, 1.0, 0.0)).astype(BF16)
    slots = lax.broadcasted_iota(jnp.int32, (128, tokens), 0).astype(F32)
    both_e = range(2)
    for e in both_e:
        mine = (first + e).astype(F32)
        s0 = meta[0:1, :] == mine
        s1 = meta[1:2, :] == mine
        named = jnp.where(s0, 1.0, 0.0) + jnp.where(s1, 1.0, 0.0)
        gate = jnp.where(s0, meta[2:3, :], 0.0) + jnp.where(s1, meta[3:4, :], 0.0)
        place = mm(jnp.broadcast_to(named, (8, tokens)).astype(BF16), before)[0:1, :]
        place = jnp.where(named > 0.5, place, -1.0)
        hit = slots == place
        pick_o[e] = jnp.where(hit, 1.0, 0.0).astype(BF16)
        weight = jnp.sum(jnp.where(hit, gate, 0.0), axis=1, keepdims=True)
        gate_o[e] = jnp.broadcast_to(weight, (128, 128))
    for e in both_e:
        rows[e] = mm(pick_o[e], whole[:, 0:WIDTH])
    for e in both_e:
        flipped[e] = rows[e].T
    for e in both_e:
        grad = mm(pick_o[e], whole[:, WIDTH : 2 * WIDTH])
        grad_o[e] = (gate_o[e][:, 0:1] * grad).astype(BF16)
    for e in both_e:
        half_gram[e, 136:144, :] = jnp.zeros((8, 128), F32)
        at = 0
        for i in range(16):
            left = flipped[e, i * 64 : i * 64 + 64, :]
            for q in range(i, 16):
                prod = left * flipped[e, q * 64 : q * 64 + 64, :]
                partial[e, at * 8 : at * 8 + 8, :] = jnp.sum(prod.reshape(8, 8, 128), axis=0)
                at += 1
        for g in range(17):
            acc = partial[e, pl.ds(g * 64, 8, stride=8), :]
            for q in range(1, 8):
                acc = acc + partial[e, pl.ds(g * 64 + q, 8, stride=8), :]
            half_gram[e, g * 8 : g * 8 + 8, :] = acc * (1.0 / DE)
        gram_o[e] = mm(spread, half_gram[e].astype(BF16)).astype(BF16)
    for e in both_e:
        cross_o[e] = (rows[e] + mm(gram_o[e], pair[e], TN)).astype(BF16)
    for copy in ready:
        copy.wait()
    for e in both_e:
        slope[e] = mm(grad_o[e], down[e], NT)
    for e in both_e:
        pre = mm(cross_o[e], up[e])
        sig = jax.nn.sigmoid(pre)
        act_o[e] = (pre * sig).astype(BF16)
        pre_o[e] = (slope[e] * sig * (1.0 + pre * (1.0 - sig))).astype(BF16)
    for e in both_e:
        terms[e] = mm(pre_o[e], up[e], NT).astype(BF16)
    for e in both_e:
        outs_s[e] = mm(act_o[e], down[e]).astype(BF16)
    for e in both_e:
        back = mm(pair[e], terms[e], NT).astype(BF16)
        backs[e] = mm(both, back).astype(BF16)
    for xr in (1, 0):
        for part in (1, 0):
            block = 2 * (xi ^ xr) + (core ^ part)
            cols = pl.ds(pl.multiple_of(block * 256, 256), 256)
            if part == 0:
                low, high = keep.at[xr, 0:320], keep.at[xr, 320:576]
            elif xr == 0:
                low, high = send_here.at[0:320], send_here.at[320:576]
            else:
                low, high = send_away, send_last
            for e in both_e:
                mine = slice(e * 128, e * 128 + 128)
                low[mine, :] = terms[e, :, cols]
                high[mine, :] = outs_s[e, :, cols]
                rows64 = pl.ds(pl.multiple_of(block * 64, 64), 64)
                low[256:320, mine] = backs[e, rows64, :]


def read_meta(info):
    rows = info[...].astype(F32).T
    return jnp.concatenate([rows[0:2], rows[2:4] + rows[4:6]], axis=0)


def own_chunk_kernel(*refs):
    own, p0, near, far, p1, p2, p3, up_in, down_in = refs[:9]
    outs, pair_o = refs[9:20], refs[20]
    whole, info, up, down, sems = refs[21:26]
    j = lax.axis_index("tensor")
    copies = load([(up_in, up), (down_in, down)], sems)
    whole[0:128, :] = own[:, 0 : 2 * WIDTH]
    info[0:128, :] = own[:, 2 * WIDTH :]
    place_rows(whole, info, 1, lax.rem(j, 2), near, far)
    for k, piece in enumerate((p0, p1, p2, p3)):
        cols = pl.ds(pl.multiple_of((j ^ k) * 256, 256), 256)
        for e in range(2):
            pair_o[e, :, cols] = piece[e]
    towers(read_meta(info), whole, up, down, copies, pair_o, outs, refs[26:])


def far_chunk_kernel(*refs):
    near, far, pair, up_in, down_in = refs[:5]
    outs = refs[5:16]
    whole, info, up, down, sems = refs[16:21]
    core = lax.rem(lax.axis_index("tensor"), 2)
    copies = load([(up_in, up), (down_in, down)], sems)
    for r in range(2):
        rows = slice(r * HALF, r * HALF + HALF)
        place_rows(whole, info, r, core, near.at[rows, :], far.at[rows, :])
    towers(read_meta(info), whole, up, down, copies, pair, outs, refs[21:])


def stack(a, b):
    return jnp.concatenate([a, b], axis=0)


def down_kernel(act0, grad0, act1, grad1, down_o, done_o):
    done_o[...] = jnp.zeros((8, 128), F32)
    for e in range(2):
        down_o[e] = mm(stack(act0[e], act1[e]), stack(grad0[e], grad1[e]), TN).astype(BF16)


def up_kernel(cross0, pre0, cross1, pre1, up_o):
    for e in range(2):
        up_o[e] = mm(stack(cross0[e], cross1[e]), stack(pre0[e], pre1[e]), TN).astype(BF16)


def add2(a, b):
    return (a.astype(F32) + b.astype(F32)).astype(BF16)


def combine_grads(both, picks, rows_o):
    grads = jnp.zeros((256, 256), F32)
    back = jnp.zeros((64, 256), F32)
    for e in range(2):
        rows = both[e * 128 : e * 128 + 128]
        rows_o[e] = rows
        grads = grads + mm(picks[e], rows, TN)
        back = back + mm(both[256:320, e * 128 : e * 128 + 128], picks[e])
    return grads.astype(BF16), back.astype(BF16)


def put_grads(dst, grads, back, p):
    rows = slice(p * 128, p * 128 + 128)
    dst[0:128, :] = grads[rows]
    dst[128:160, 0:128] = back[0:32, rows]
    dst[128:160, 128:256] = back[32:64, rows]


def combine_outs(both, picks, gates):
    mixed = jnp.zeros((256, 256), F32)
    for e in range(2):
        out = both[e * 128 : e * 128 + 128].astype(F32) * gates[e][:, 0:1]
        mixed = mixed + mm(picks[e], out.astype(BF16), TN)
    return mixed.astype(BF16)


def combine_kernel(mine, other, theirs, pick, gate, after, first_o, second_o, rows_o):
    both = add2(add2(mine[0], other[...]), theirs[...])
    grads, back = combine_grads(both[0:320], pick, rows_o)
    mixed = combine_outs(both[320:576], pick, gate)
    for p, dst in enumerate((first_o, second_o)):
        put_grads(dst, grads, back, p)
        dst[160:288, :] = mixed[p * 128 : p * 128 + 128]


def far_grads_kernel(mine, other, theirs, pick, after, first_o, second_o, rows_o):
    both = add2(add2(mine[0, 0:320], other[0:320]), theirs[...])
    grads, back = combine_grads(both, pick, rows_o)
    for p, dst in enumerate((first_o, second_o)):
        put_grads(dst, grads, back, p)


def far_outs_kernel(mine, other, theirs, pick, gate, after, first_o, second_o):
    both = add2(add2(mine[0, 320:576], other[320:576]), theirs[...])
    mixed = combine_outs(both, pick, gate)
    first_o[...] = mixed[0:128]
    second_o[...] = mixed[128:256]


def sum_kernel(a, b, *rest):
    rest[-1][...] = add2(a[...], b[...])


def pair_kernel(gram0, rows0, gram1, rows1, out_o):
    for e in range(2):
        out_o[e] = (mm(gram0[e], rows0[e]) + mm(gram1[e], rows1[e])).astype(BF16)


def final_kernel(own, g0, g1, far_grads, far_outs, mixed_o, grad_o, flipped):
    column = pl.multiple_of(lax.axis_index("tensor") * 256, 256)
    mixed = own[:, pl.ds(column, 256)].astype(F32) + far_outs[...].astype(F32)
    total = own[:, pl.ds(WIDTH + column, 256)].astype(F32)
    back = jnp.zeros((32, 256), F32)
    for g in (g0, g1, far_grads):
        total = total + g[0:128, :].astype(F32)
        back = back + g[128:160, :].astype(F32)
    for g in (g0, g1):
        mixed = mixed + g[160:288, :].astype(F32)
    mixed_o[...] = mixed.astype(BF16)
    flipped[...] = own[:, 0:WIDTH].astype(F32).T
    back = jnp.concatenate([back[:, 0:128], back[:, 128:256]], axis=0)
    pieces = []
    for i in range(4):
        acc = jnp.zeros((64, 128), F32)
        for q in range(16):
            acc = acc + back[i * 16 + q : i * 16 + q + 1, :] * flipped[q * 64 : q * 64 + 64, :]
        pieces.append(acc)
    gram_back = jnp.concatenate(pieces, axis=0) * (1.0 / DE)
    grad_o[...] = (total + gram_back.T).astype(BF16)


def swap(value, axis, mask):
    size = lax.axis_size(axis)
    return lax.ppermute(value, axis, [(i, i ^ mask) for i in range(size)])


def chunk_outs():
    return (
        shape((2, 576, 256)),
        shape((576, 256)),
        shape((320, 256)),
        shape((256, 256)),
        shape((2, 128, 1024)),
        shape((2, 128, 512)),
        shape((2, 128, 1024)),
        shape((2, 128, 512)),
        shape((2, 256, 128)),
        shape((2, 128, 256)),
        shape((2, 128, 128), F32),
    )


def chunk_scratch():
    return [
        pltpu.VMEM((2, 1024, 128), F32),
        pltpu.VMEM((2, 1088, 128), F32),
        pltpu.VMEM((2, 144, 128), F32),
        pltpu.VMEM((2, 128, 1024), BF16),
        pltpu.VMEM((2, 128, 1024), F32),
        pltpu.VMEM((2, 128, 512), F32),
        pltpu.VMEM((2, 128, 1024), BF16),
        pltpu.VMEM((2, 256, 128), BF16),
    ]


def weight_scratch():
    return [pltpu.VMEM((2, 1024, 512), BF16), pltpu.VMEM((2, 512, 1024), BF16)]


def away_kernel(keep, low, high, out_o):
    out_o[0:320, :] = add2(keep[1, 0:320], low[...])
    out_o[320:576, :] = add2(keep[1, 320:576], high[...])


def away_grads_kernel(keep, low, out_o):
    out_o[...] = add2(keep[1, 0:320], low[...])


def away_outs_kernel(keep, high, after, after2, out_o):
    out_o[...] = add2(keep[1, 320:576], high[...])


def gathered_body(inputs, cotangent, gate_values, routes, pair_weight, up_weight, down_weight):
    gates, choices = gate_values.T, routes.T
    width = 2 * WIDTH + 128
    payload, own, pair_own = kernel_call(
        payload_kernel,
        (
            shape((HALF, width)),
            shape((2 * HALF, width)),
            shape((2, 256, 256)),
        ),
        "hhhhh",
        scratch=[
            pltpu.VMEM((2, 128), F32),
            pltpu.VMEM((2, 128), jnp.int32),
            pltpu.SemaphoreType.DMA((7,)),
        ],
        vmem=60,
    )(inputs, cotangent, gates, choices, pair_weight)
    got = [swap(payload, "expert", 1), swap(payload, "expert", 2)]
    got.append(swap(got[1], "expert", 1))
    both = shape((2, 256, 256))
    own, pair_own = kernel_call(
        stage_kernel, (shape((2 * HALF, width)), both), "vv"
    )(own, pair_own)
    pair_x = swap(pair_own, "tensor", 2)
    pair_x = kernel_call(after_kernel, both, "va", flops=30_000_000)(pair_x, got[1])
    pair_c = swap(pair_own, "tensor", 1)
    pair_d = swap(pair_x, "tensor", 1)
    near_other = swap(got[0], "tensor", 1)
    chunk = kernel_call(
        own_chunk_kernel,
        chunk_outs() + (shape((2, 256, 1024)),),
        "vvvvvvvhh",
        scratch=[
            pltpu.VMEM((256, 2048), BF16),
            pltpu.VMEM((256, 128), BF16),
        ]
        + weight_scratch()
        + [pltpu.SemaphoreType.DMA((2,))]
        + chunk_scratch(),
        flops=4_000_000_000,
        nbytes=10_000_000,
    )(
        own, pair_own, got[0], near_other,
        pair_c, pair_x, pair_d, up_weight, down_weight,
    )
    keep, here, away, last, cross, act, grad, pre, gram, pick, gate, pair_all = chunk
    away = kernel_call(away_kernel, shape((576, 256)), "vvv")(
        keep, swap(away, "tensor", 1), swap(last, "tensor", 1)
    )
    theirs = swap(away, "tensor", 2)
    other = swap(here, "tensor", 1)
    far_mine = kernel_call(join_kernel, shape((2 * HALF, 2 * WIDTH + 128)), "vva")(
        got[1], got[2], gate
    )
    far_other = swap(far_mine, "tensor", 1)
    chunk = kernel_call(
        far_chunk_kernel,
        chunk_outs(),
        "vvvhh",
        scratch=[pltpu.VMEM((256, 2048), BF16), pltpu.VMEM((256, 128), BF16)]
        + weight_scratch()
        + [pltpu.SemaphoreType.DMA((2,))]
        + chunk_scratch(),
        flops=4_000_000_000,
        nbytes=10_000_000,
    )(far_mine, far_other, pair_all, up_weight, down_weight)
    fkeep, fhere, faway, flast, fcross, fact, fgrad, fpre, fgram, fpick, fgate = chunk
    fother = swap(fhere, "tensor", 1)
    fgrads = kernel_call(away_grads_kernel, shape((320, 256)), "vv")(
        fkeep, swap(faway, "tensor", 1)
    )
    fouts = kernel_call(away_outs_kernel, shape((256, 256)), "vvaa")(
        fkeep, swap(flast, "tensor", 1), fgrads, theirs
    )
    fgrads = swap(fgrads, "tensor", 2)
    part = shape((288, 256))
    own_part, near_part, rows = kernel_call(
        combine_kernel, (part, part, shape((2, 128, 256))), "vvvvva"
    )(keep, other, theirs, pick, gate, fouts)
    near_got = swap(near_part, "expert", 1)
    fouts = swap(fouts, "tensor", 2)
    grad_down, down_done = kernel_call(
        down_kernel,
        (shape((2, 512, 1024)), shape((8, 128), F32)),
        "vvvv",
        flops=1_500_000_000,
        nbytes=4_000_000,
    )(act, grad, fact, fgrad)
    grad_up = kernel_call(
        up_kernel,
        shape((2, 1024, 512)),
        "vvvv",
        flops=1_500_000_000,
        nbytes=4_000_000,
    )(cross, pre, fcross, fpre)
    part = shape((160, 256))
    grads2, grads3, frows = kernel_call(
        far_grads_kernel, (part, part, shape((2, 128, 256))), "vvvva"
    )(fkeep, fother, fgrads, fpick, down_done)
    grads2 = kernel_call(sum_kernel, part, "vv")(grads2, swap(grads3, "expert", 1))
    far_grads = swap(grads2, "expert", 2)
    part = shape((128, 256))
    outs2, outs3 = kernel_call(far_outs_kernel, (part, part), "vvvvva")(
        fkeep, fother, fouts, fpick, fgate, near_got
    )
    outs2 = kernel_call(sum_kernel, part, "vva")(outs2, swap(outs3, "expert", 1), grads2)
    far_outs = swap(outs2, "expert", 2)
    grad_pair = kernel_call(
        pair_kernel, shape((2, 256, 256)), "vvvv", flops=300_000_000, nbytes=2_000_000
    )(gram, rows, fgram, frows)
    mixed, grad_input = kernel_call(
        final_kernel,
        (shape((128, 256)), shape((128, 256))),
        "vvvvv",
        scratch=[pltpu.VMEM((1024, 128), F32)],
        flops=100_000_000,
        nbytes=1_000_000,
    )(own, own_part, near_got, far_grads, far_outs)
    return mixed, grad_input, grad_pair, grad_up, grad_down


def solution(mesh):
    placed = (
        P(("group", "expert"), None),
        P(("group", "expert"), None),
        P(("group", "expert"), None),
        P(("group", "expert"), None),
        P("expert", None, "tensor"),
        P("expert", None, "tensor"),
        P("expert", "tensor", None),
    )
    small = mesh.shape["expert"] == 4 and mesh.shape["tensor"] == 4
    return jax.shard_map(
        gathered_body if small else body,
        mesh=mesh,
        in_specs=placed,
        out_specs=(
            P(("group", "expert"), "tensor"),
            P(("group", "expert"), "tensor"),
            P(("group", "expert"), None, "tensor"),
            P(("group", "expert"), None, "tensor"),
            P(("group", "expert"), "tensor", None),
        ),
        check_vma=False,
    )
```

```python
import functools

import jax
import jax.numpy as jnp
from jax import lax
from jax.experimental import pallas as pl
from jax.experimental.pallas import tpu as pltpu
from jax.sharding import PartitionSpec as P

NF = 16
DE = 64


def dispatch_tables(routes, expert_total, capacity):
    row_count, pick_count = routes.shape
    flat_ids = routes.reshape(-1)
    onehot = (flat_ids[:, None] == jnp.arange(expert_total, dtype=jnp.int32)[None, :]).astype(
        jnp.int32
    )
    before = jnp.cumsum(onehot, axis=0) - onehot
    position = jnp.sum(before * onehot, axis=1)
    slot_index = flat_ids * capacity + position
    slot_count = expert_total * capacity
    tables = slot_index[:, None] == jnp.arange(slot_count, dtype=jnp.int32)[None, :]
    tables = tables.reshape(row_count, pick_count, slot_count)
    return jnp.transpose(tables, (1, 2, 0)).astype(jnp.bfloat16)


def body(inputs, cotangent, gate_values, routes, pair_weight, up_weight, down_weight):
    local_count = up_weight.shape[0]
    expert_count = lax.axis_size("expert")
    tensor_count = lax.axis_size("tensor")
    expert_total = local_count * expert_count
    row_count, pick_count = routes.shape
    feature_width = inputs.shape[1]
    capacity = 2 * row_count * pick_count // expert_total
    expert_rows = expert_count * capacity
    part_width = feature_width // tensor_count
    tensor_index = lax.axis_index("tensor")
    feature_start = tensor_index * part_width
    tables = dispatch_tables(routes, expert_total, capacity)
    any_table = jnp.sum(tables, axis=0)
    scaled = (gate_values[:, :, None] * cotangent[:, None, :].astype(jnp.float32)).astype(
        jnp.bfloat16
    )
    input_slice = lax.dynamic_slice_in_dim(inputs, feature_start, part_width, 1)
    cotangent_slice = lax.dynamic_slice_in_dim(cotangent, feature_start, part_width, 1)
    input_slots = jnp.dot(any_table, inputs, preferred_element_type=jnp.float32).astype(
        jnp.bfloat16
    )
    grad_slots = jnp.einsum(
        "ksr,rkd->sd", tables, scaled, preferred_element_type=jnp.float32
    ).astype(jnp.bfloat16)
    send_shape = (expert_count, local_count, capacity, feature_width)
    input_homes, grad_homes = (
        lax.all_to_all(
            input_slots.reshape(send_shape), "expert", split_axis=0, concat_axis=2, tiled=True
        ),
        lax.all_to_all(
            grad_slots.reshape(send_shape), "expert", split_axis=0, concat_axis=2, tiled=True
        ),
    )
    input_rows = input_homes.reshape(local_count, expert_rows, feature_width)
    grad_rows = grad_homes.reshape(local_count, expert_rows, feature_width)
    cells = jnp.transpose(input_rows.reshape(local_count, expert_rows, NF, DE), (0, 2, 3, 1))
    gram = jnp.einsum("eidr,ejdr->eijr", cells, cells, preferred_element_type=jnp.float32) / DE
    gram_flat = gram.reshape(local_count, NF * NF, expert_rows).astype(jnp.bfloat16)
    input_mine = lax.dynamic_slice_in_dim(input_rows, feature_start, part_width, 2)
    cross_sum = input_mine.astype(jnp.float32) + jnp.einsum(
        "epr,epd->erd", gram_flat, pair_weight, preferred_element_type=jnp.float32
    )
    cross_part = cross_sum.astype(jnp.bfloat16)
    cross_whole = lax.all_gather(cross_part, "tensor", axis=2, tiled=True)
    hidden_pre = jnp.einsum(
        "erd,edh->erh", cross_whole, up_weight, preferred_element_type=jnp.float32
    )
    hidden_act = jax.nn.silu(hidden_pre).astype(jnp.bfloat16)
    out_terms = jnp.einsum(
        "erh,ehd->erd", hidden_act, down_weight, preferred_element_type=jnp.float32
    )
    out_mine = lax.psum_scatter(
        out_terms.astype(jnp.bfloat16), "tensor", scatter_dimension=2, tiled=True
    )
    grad_act = jnp.einsum(
        "erd,ehd->erh", grad_rows, down_weight, preferred_element_type=jnp.float32
    )
    sigmoid_pre = jax.nn.sigmoid(hidden_pre)
    grad_pre = (grad_act * sigmoid_pre * (1.0 + hidden_pre * (1.0 - sigmoid_pre))).astype(
        jnp.bfloat16
    )
    grad_down = jnp.einsum(
        "erh,erd->ehd", hidden_act, grad_rows, preferred_element_type=jnp.float32
    ).astype(jnp.bfloat16)
    grad_up = jnp.einsum(
        "erd,erh->edh", cross_whole, grad_pre, preferred_element_type=jnp.float32
    ).astype(jnp.bfloat16)
    cross_terms = jnp.einsum(
        "erh,edh->erd", grad_pre, up_weight, preferred_element_type=jnp.float32
    )
    grad_cross = lax.psum_scatter(
        cross_terms.astype(jnp.bfloat16), "tensor", scatter_dimension=2, tiled=True
    )
    grad_pair = jnp.einsum(
        "epr,erd->epd", gram_flat, grad_cross, preferred_element_type=jnp.float32
    ).astype(jnp.bfloat16)
    pair_terms = jnp.einsum(
        "erd,epd->epr", grad_cross, pair_weight, preferred_element_type=jnp.float32
    )
    grad_gram = (
        lax.psum(pair_terms.astype(jnp.bfloat16), "tensor")
        .astype(jnp.float32)
        .reshape(local_count, NF, NF, expert_rows)
    )
    symmetric = grad_gram + jnp.swapaxes(grad_gram, 1, 2)
    field_count = part_width // DE
    symmetric_mine = lax.dynamic_slice_in_dim(symmetric, tensor_index * field_count, field_count, 1)
    gram_back = (
        jnp.einsum(
            "eijr,ejdr->eidr",
            symmetric_mine,
            cells.astype(jnp.float32),
            precision=lax.Precision.HIGHEST,
        )
        / DE
    )
    gram_back = jnp.transpose(gram_back, (0, 3, 1, 2)).reshape(local_count, expert_rows, part_width)
    grad_mine = (grad_cross.astype(jnp.float32) + gram_back).astype(jnp.bfloat16)
    back_shape = (1, local_count, expert_rows, part_width)
    out_back, grad_back = (
        lax.all_to_all(
            out_mine.reshape(back_shape), "expert", split_axis=2, concat_axis=0, tiled=True
        ),
        lax.all_to_all(
            grad_mine.reshape(back_shape), "expert", split_axis=2, concat_axis=0, tiled=True
        ),
    )
    out_back = out_back.reshape(expert_total * capacity, part_width)
    grad_back = grad_back.reshape(expert_total * capacity, part_width)
    picked = jnp.einsum("ksr,sd->rkd", tables, out_back, preferred_element_type=jnp.float32)
    mixed = (
        input_slice.astype(jnp.float32) + jnp.sum(gate_values[:, :, None] * picked, axis=1)
    ).astype(jnp.bfloat16)
    grad_input = (
        cotangent_slice.astype(jnp.float32)
        + jnp.dot(any_table.T, grad_back, preferred_element_type=jnp.float32)
    ).astype(jnp.bfloat16)
    return (mixed, grad_input, grad_pair, grad_up, grad_down)


F32 = jnp.float32
BF16 = jnp.bfloat16
NT = (((1,), (1,)), ((), ()))
TN = (((0,), (0,)), ((), ()))
WIDTH = 1024
HALF = 64


def mm(a, b, dims=None):
    if dims is None:
        return jnp.dot(a, b, preferred_element_type=F32)
    return lax.dot_general(a, b, dims, preferred_element_type=F32)


def kernel_call(kernel, out_shape, where, scratch=(), flops=0, nbytes=0, vmem=48):
    kinds = {"v": pltpu.VMEM, "a": pl.ANY, "h": pltpu.HBM}
    return pl.pallas_call(
        kernel,
        out_shape=out_shape,
        in_specs=[pl.BlockSpec(memory_space=kinds[w]) for w in where],
        scratch_shapes=list(scratch),
        compiler_params=pltpu.CompilerParams(vmem_limit_bytes=vmem * 1024 * 1024),
        cost_estimate=pl.CostEstimate(flops=flops, bytes_accessed=nbytes, transcendentals=0),
    )


def shape(dims, dtype=BF16):
    return jax.ShapeDtypeStruct(dims, dtype)


def load(pairs, sems):
    copies = [pltpu.make_async_copy(a, b, sems.at[n]) for n, (a, b) in enumerate(pairs)]
    for copy in copies:
        copy.start()
    return copies


def payload_kernel(x, c, gates_in, routes_in, out_o, meta_o, gates, routes, sems):
    core = lax.rem(lax.axis_index("tensor"), 2)
    mine = pl.ds(pl.multiple_of(core * HALF, HALF), HALF)
    copies = load(
        [
            (gates_in, gates),
            (routes_in, routes),
            (x.at[mine, :], out_o.at[:, 0:WIDTH]),
            (c.at[mine, :], out_o.at[:, WIDTH : 2 * WIDTH]),
        ],
        sems,
    )
    copies[0].wait()
    copies[1].wait()
    high = gates[...].astype(BF16).astype(F32)
    low = gates[...] - high
    meta = jnp.concatenate(
        [routes[...].astype(F32), high, low, jnp.zeros((122, 128), F32)], axis=0
    )
    columns = meta.T
    meta_o[...] = columns.astype(BF16)
    out_o[:, 2 * WIDTH :] = jnp.where(core == 0, columns[0:HALF], columns[HALF:]).astype(BF16)
    for copy in copies[2:]:
        copy.wait()


def after_kernel(value, after, out_o):
    out_o[...] = value[...]


def stage_kernel(x, c, meta, pair, own_o, pair_o):
    own_o[:, 0:WIDTH] = x[...]
    own_o[:, WIDTH : 2 * WIDTH] = c[...]
    own_o[:, 2 * WIDTH :] = meta[...]
    pair_o[...] = pair[...]


def join_kernel(a, b, after, out_o):
    out_o[0:HALF, :] = a[...]
    out_o[HALF : 2 * HALF, :] = b[...]


def place_rows(whole, info, block, core, near, far):
    for at, piece in ((core, near), (1 - core, far)):
        rows = pl.ds(pl.multiple_of(block * 128 + at * HALF, HALF), HALF)
        whole[rows, :] = piece[:, 0 : 2 * WIDTH]
        info[rows, :] = piece[:, 2 * WIDTH :]


def towers(meta, whole, up, down, ready, pair, outs, scratch):
    keep, send_here, send_away, send_last, cross_o, act_o, grad_o, pre_o, gram_o, pick_o, gate_o = outs
    flipped, partial, half_gram, terms, rows, slope, outs_s, backs = scratch
    j = lax.axis_index("tensor")
    core = lax.rem(j, 2)
    xi = j // 2
    first = lax.axis_index("expert") * 2
    tokens = meta.shape[1]
    before = (
        lax.broadcasted_iota(jnp.int32, (tokens, tokens), 0)
        < lax.broadcasted_iota(jnp.int32, (tokens, tokens), 1)
    ).astype(F32).astype(BF16)
    a = lax.broadcasted_iota(jnp.int32, (256, 144), 0)
    n = lax.broadcasted_iota(jnp.int32, (256, 144), 1)
    low = jnp.minimum(a // 16, a % 16)
    high = jnp.maximum(a // 16, a % 16)
    spread = jnp.where(low * 16 - low * (low - 1) // 2 + high - low == n, 1.0, 0.0).astype(BF16)
    a = lax.broadcasted_iota(jnp.int32, (256, 256), 0)
    b = lax.broadcasted_iota(jnp.int32, (256, 256), 1)
    swapped = (a % 16) * 16 + a // 16
    both = (jnp.where(a == b, 1.0, 0.0) + jnp.where(swapped == b, 1.0, 0.0)).astype(BF16)
    slots = lax.broadcasted_iota(jnp.int32, (128, tokens), 0).astype(F32)
    both_e = range(2)
    for e in both_e:
        mine = (first + e).astype(F32)
        s0 = meta[0:1, :] == mine
        s1 = meta[1:2, :] == mine
        named = jnp.where(s0, 1.0, 0.0) + jnp.where(s1, 1.0, 0.0)
        gate = jnp.where(s0, meta[2:3, :], 0.0) + jnp.where(s1, meta[3:4, :], 0.0)
        place = mm(jnp.broadcast_to(named, (8, tokens)).astype(BF16), before)[0:1, :]
        place = jnp.where(named > 0.5, place, -1.0)
        hit = slots == place
        pick_o[e] = jnp.where(hit, 1.0, 0.0).astype(BF16)
        weight = jnp.sum(jnp.where(hit, gate, 0.0), axis=1, keepdims=True)
        gate_o[e] = jnp.broadcast_to(weight, (128, 128))
    for e in both_e:
        rows[e] = mm(pick_o[e], whole[:, 0:WIDTH])
    for e in both_e:
        flipped[e] = rows[e].T
    for e in both_e:
        grad = mm(pick_o[e], whole[:, WIDTH : 2 * WIDTH])
        grad_o[e] = (gate_o[e][:, 0:1] * grad).astype(BF16)
    for e in both_e:
        half_gram[e, 136:144, :] = jnp.zeros((8, 128), F32)
        at = 0
        for i in range(16):
            left = flipped[e, i * 64 : i * 64 + 64, :]
            for q in range(i, 16):
                prod = left * flipped[e, q * 64 : q * 64 + 64, :]
                partial[e, at * 8 : at * 8 + 8, :] = jnp.sum(prod.reshape(8, 8, 128), axis=0)
                at += 1
        for g in range(17):
            acc = partial[e, pl.ds(g * 64, 8, stride=8), :]
            for q in range(1, 8):
                acc = acc + partial[e, pl.ds(g * 64 + q, 8, stride=8), :]
            half_gram[e, g * 8 : g * 8 + 8, :] = acc * (1.0 / DE)
        gram_o[e] = mm(spread, half_gram[e].astype(BF16)).astype(BF16)
    for e in both_e:
        cross_o[e] = (rows[e] + mm(gram_o[e], pair[e], TN)).astype(BF16)
    for copy in ready:
        copy.wait()
    for e in both_e:
        slope[e] = mm(grad_o[e], down[e], NT)
    for e in both_e:
        pre = mm(cross_o[e], up[e])
        sig = jax.nn.sigmoid(pre)
        act_o[e] = (pre * sig).astype(BF16)
        pre_o[e] = (slope[e] * sig * (1.0 + pre * (1.0 - sig))).astype(BF16)
    for e in both_e:
        terms[e] = mm(pre_o[e], up[e], NT).astype(BF16)
    for e in both_e:
        outs_s[e] = mm(act_o[e], down[e]).astype(BF16)
    for e in both_e:
        back = mm(pair[e], terms[e], NT).astype(BF16)
        backs[e] = mm(both, back).astype(BF16)
    for xr in (1, 0):
        for part in (1, 0):
            block = 2 * (xi ^ xr) + (core ^ part)
            cols = pl.ds(pl.multiple_of(block * 256, 256), 256)
            if part == 0:
                low, high = keep.at[xr, 0:320], keep.at[xr, 320:576]
            elif xr == 0:
                low, high = send_here.at[0:320], send_here.at[320:576]
            else:
                low, high = send_away, send_last
            for e in both_e:
                mine = slice(e * 128, e * 128 + 128)
                low[mine, :] = terms[e, :, cols]
                high[mine, :] = outs_s[e, :, cols]
                rows64 = pl.ds(pl.multiple_of(block * 64, 64), 64)
                low[256:320, mine] = backs[e, rows64, :]


def read_meta(info):
    rows = info[...].astype(F32).T
    return jnp.concatenate([rows[0:2], rows[2:4] + rows[4:6]], axis=0)


def place_pairs(pair, pieces):
    j = lax.axis_index("tensor")
    for k, piece in enumerate(pieces):
        cols = pl.ds(pl.multiple_of((j ^ k) * 256, 256), 256)
        for e in range(2):
            pair[e, :, cols] = piece[e]


def own_chunk_kernel(*refs):
    own, near, far, p0, p1, p2, p3, up_in, down_in = refs[:9]
    outs = refs[9:20]
    whole, info, pair, up, down, sems = refs[20:26]
    core = lax.rem(lax.axis_index("tensor"), 2)
    copies = load([(up_in, up), (down_in, down)], sems)
    whole[0:128, :] = own[:, 0 : 2 * WIDTH]
    info[0:128, :] = own[:, 2 * WIDTH :]
    place_rows(whole, info, 1, core, near, far)
    place_pairs(pair, (p0, p1, p2, p3))
    towers(read_meta(info), whole, up, down, copies, pair, outs, refs[26:])


def far_chunk_kernel(*refs):
    near, far, p0, p1, p2, p3, up_in, down_in = refs[:8]
    outs = refs[8:19]
    whole, info, pair, up, down, sems = refs[19:25]
    core = lax.rem(lax.axis_index("tensor"), 2)
    copies = load([(up_in, up), (down_in, down)], sems)
    for r in range(2):
        rows = slice(r * HALF, r * HALF + HALF)
        place_rows(whole, info, r, core, near.at[rows, :], far.at[rows, :])
    place_pairs(pair, (p0, p1, p2, p3))
    towers(read_meta(info), whole, up, down, copies, pair, outs, refs[25:])


def weights_kernel(act0, grad0, cross0, pre0, act1, grad1, cross1, pre1, down_o, up_o, done_o):
    done_o[...] = jnp.zeros((8, 128), F32)

    def stack(a, b):
        return jnp.concatenate([a, b], axis=0)

    for e in range(2):
        down_o[e] = mm(stack(act0[e], act1[e]), stack(grad0[e], grad1[e]), TN).astype(BF16)
        up_o[e] = mm(stack(cross0[e], cross1[e]), stack(pre0[e], pre1[e]), TN).astype(BF16)


def add2(a, b):
    return (a.astype(F32) + b.astype(F32)).astype(BF16)


def combine_grads(both, picks, rows_o):
    grads = jnp.zeros((256, 256), F32)
    back = jnp.zeros((64, 256), F32)
    for e in range(2):
        rows = both[e * 128 : e * 128 + 128]
        rows_o[e] = rows
        grads = grads + mm(picks[e], rows, TN)
        back = back + mm(both[256:320, e * 128 : e * 128 + 128], picks[e])
    return grads.astype(BF16), back.astype(BF16)


def put_grads(dst, grads, back, p):
    rows = slice(p * 128, p * 128 + 128)
    dst[0:128, :] = grads[rows]
    dst[128:160, 0:128] = back[0:32, rows]
    dst[128:160, 128:256] = back[32:64, rows]


def combine_outs(both, picks, gates):
    mixed = jnp.zeros((256, 256), F32)
    for e in range(2):
        out = both[e * 128 : e * 128 + 128].astype(F32) * gates[e][:, 0:1]
        mixed = mixed + mm(picks[e], out.astype(BF16), TN)
    return mixed.astype(BF16)


def combine_kernel(mine, other, theirs, pick, gate, after, first_o, second_o, rows_o):
    both = add2(add2(mine[0], other[...]), theirs[...])
    grads, back = combine_grads(both[0:320], pick, rows_o)
    mixed = combine_outs(both[320:576], pick, gate)
    for p, dst in enumerate((first_o, second_o)):
        put_grads(dst, grads, back, p)
        dst[160:288, :] = mixed[p * 128 : p * 128 + 128]


def far_grads_kernel(mine, other, theirs, pick, after, first_o, second_o, rows_o):
    both = add2(add2(mine[0, 0:320], other[0:320]), theirs[...])
    grads, back = combine_grads(both, pick, rows_o)
    for p, dst in enumerate((first_o, second_o)):
        put_grads(dst, grads, back, p)


def far_outs_kernel(mine, other, theirs, pick, gate, after, first_o, second_o):
    both = add2(add2(mine[0, 320:576], other[320:576]), theirs[...])
    mixed = combine_outs(both, pick, gate)
    first_o[...] = mixed[0:128]
    second_o[...] = mixed[128:256]


def sum_kernel(a, b, out_o):
    out_o[...] = add2(a[...], b[...])


def pair_kernel(gram0, rows0, gram1, rows1, out_o):
    for e in range(2):
        out_o[e] = (mm(gram0[e], rows0[e]) + mm(gram1[e], rows1[e])).astype(BF16)


def final_kernel(own, g0, g1, far_grads, far_outs, mixed_o, grad_o, flipped):
    column = pl.multiple_of(lax.axis_index("tensor") * 256, 256)
    mixed = own[:, pl.ds(column, 256)].astype(F32) + far_outs[...].astype(F32)
    total = own[:, pl.ds(WIDTH + column, 256)].astype(F32)
    back = jnp.zeros((32, 256), F32)
    for g in (g0, g1, far_grads):
        total = total + g[0:128, :].astype(F32)
        back = back + g[128:160, :].astype(F32)
    for g in (g0, g1):
        mixed = mixed + g[160:288, :].astype(F32)
    mixed_o[...] = mixed.astype(BF16)
    flipped[...] = own[:, 0:WIDTH].astype(F32).T
    back = jnp.concatenate([back[:, 0:128], back[:, 128:256]], axis=0)
    pieces = []
    for i in range(4):
        acc = jnp.zeros((64, 128), F32)
        for q in range(16):
            acc = acc + back[i * 16 + q : i * 16 + q + 1, :] * flipped[q * 64 : q * 64 + 64, :]
        pieces.append(acc)
    gram_back = jnp.concatenate(pieces, axis=0) * (1.0 / DE)
    grad_o[...] = (total + gram_back.T).astype(BF16)


def swap(value, axis, mask):
    size = lax.axis_size(axis)
    return lax.ppermute(value, axis, [(i, i ^ mask) for i in range(size)])


def chunk_outs():
    return (
        shape((2, 576, 256)),
        shape((576, 256)),
        shape((320, 256)),
        shape((256, 256)),
        shape((2, 128, 1024)),
        shape((2, 128, 512)),
        shape((2, 128, 1024)),
        shape((2, 128, 512)),
        shape((2, 256, 128)),
        shape((2, 128, 256)),
        shape((2, 128, 128), F32),
    )


def chunk_scratch():
    return [
        pltpu.VMEM((2, 1024, 128), F32),
        pltpu.VMEM((2, 1088, 128), F32),
        pltpu.VMEM((2, 144, 128), F32),
        pltpu.VMEM((2, 128, 1024), BF16),
        pltpu.VMEM((2, 128, 1024), F32),
        pltpu.VMEM((2, 128, 512), F32),
        pltpu.VMEM((2, 128, 1024), BF16),
        pltpu.VMEM((2, 256, 128), BF16),
    ]


def weight_scratch():
    return [pltpu.VMEM((2, 1024, 512), BF16), pltpu.VMEM((2, 512, 1024), BF16)]


def away_kernel(keep, low, high, out_o):
    out_o[0:320, :] = add2(keep[1, 0:320], low[...])
    out_o[320:576, :] = add2(keep[1, 320:576], high[...])


def away_grads_kernel(keep, low, out_o):
    out_o[...] = add2(keep[1, 0:320], low[...])


def away_outs_kernel(keep, high, after, after2, out_o):
    out_o[...] = add2(keep[1, 320:576], high[...])


def gathered_body(inputs, cotangent, gate_values, routes, pair_weight, up_weight, down_weight):
    gates, choices = gate_values.T, routes.T
    width = 2 * WIDTH + 128
    payload, meta = kernel_call(
        payload_kernel,
        (shape((HALF, width)), shape((2 * HALF, 128))),
        "hhhh",
        scratch=[
            pltpu.VMEM((2, 128), F32),
            pltpu.VMEM((2, 128), jnp.int32),
            pltpu.SemaphoreType.DMA((4,)),
        ],
        vmem=60,
    )(inputs, cotangent, gates, choices)
    got = [swap(payload, "expert", 1), swap(payload, "expert", 2)]
    got.append(swap(got[1], "expert", 1))
    both = shape((2, 256, 256))
    own, pair_own = kernel_call(
        stage_kernel, (shape((2 * HALF, width)), both), "vvvv"
    )(inputs, cotangent, meta, pair_weight)
    pair_x = swap(pair_own, "tensor", 2)
    pair_x = kernel_call(after_kernel, both, "va", flops=30_000_000)(pair_x, got[1])
    pair_c = swap(pair_own, "tensor", 1)
    pair_d = swap(pair_x, "tensor", 1)
    near_other = swap(got[0], "tensor", 1)
    pairs = (pair_own, pair_c, pair_x, pair_d)
    chunk_spaces = [
        pltpu.VMEM((256, 2048), BF16),
        pltpu.VMEM((256, 128), BF16),
        pltpu.VMEM((2, 256, 1024), BF16),
        *weight_scratch(),
        pltpu.SemaphoreType.DMA((2,)),
        *chunk_scratch(),
    ]
    chunk = kernel_call(
        own_chunk_kernel,
        chunk_outs(),
        "vvvvvvvhh",
        scratch=chunk_spaces,
        flops=4_000_000_000,
        nbytes=10_000_000,
    )(own, got[0], near_other, *pairs, up_weight, down_weight)
    keep, here, away, last, cross, act, grad, pre, gram, pick, gate = chunk
    away = kernel_call(away_kernel, shape((576, 256)), "vvv")(
        keep, swap(away, "tensor", 1), swap(last, "tensor", 1)
    )
    theirs = swap(away, "tensor", 2)
    other = swap(here, "tensor", 1)
    far_mine = kernel_call(join_kernel, shape((2 * HALF, 2 * WIDTH + 128)), "vva")(
        got[1], got[2], gate
    )
    far_other = swap(far_mine, "tensor", 1)
    chunk = kernel_call(
        far_chunk_kernel,
        chunk_outs(),
        "vvvvvvhh",
        scratch=chunk_spaces,
        flops=4_000_000_000,
        nbytes=10_000_000,
    )(far_mine, far_other, *pairs, up_weight, down_weight)
    fkeep, fhere, faway, flast, fcross, fact, fgrad, fpre, fgram, fpick, fgate = chunk
    fother = swap(fhere, "tensor", 1)
    fgrads = kernel_call(away_grads_kernel, shape((320, 256)), "vv")(
        fkeep, swap(faway, "tensor", 1)
    )
    fouts = kernel_call(away_outs_kernel, shape((256, 256)), "vvaa")(
        fkeep, swap(flast, "tensor", 1), fgrads, theirs
    )
    fgrads = swap(fgrads, "tensor", 2)
    part = shape((288, 256))
    own_part, near_part, rows = kernel_call(
        combine_kernel, (part, part, shape((2, 128, 256))), "vvvvva"
    )(keep, other, theirs, pick, gate, fouts)
    near_got = swap(near_part, "expert", 1)
    fouts = swap(fouts, "tensor", 2)
    grad_down, grad_up, weights_done = kernel_call(
        weights_kernel,
        (shape((2, 512, 1024)), shape((2, 1024, 512)), shape((8, 128), F32)),
        "vvvvvvvv",
        flops=3_000_000_000,
        nbytes=8_000_000,
    )(act, grad, cross, pre, fact, fgrad, fcross, fpre)
    part = shape((160, 256))
    grads2, grads3, frows = kernel_call(
        far_grads_kernel, (part, part, shape((2, 128, 256))), "vvvva"
    )(fkeep, fother, fgrads, fpick, weights_done)
    grads2 = kernel_call(sum_kernel, part, "vv")(grads2, swap(grads3, "expert", 1))
    far_grads = swap(grads2, "expert", 2)
    part = shape((128, 256))
    outs2, outs3 = kernel_call(far_outs_kernel, (part, part), "vvvvva")(
        fkeep, fother, fouts, fpick, fgate, near_got
    )
    outs2 = kernel_call(sum_kernel, part, "vv")(outs2, swap(outs3, "expert", 1))
    far_outs = swap(outs2, "expert", 2)
    grad_pair = kernel_call(
        pair_kernel, shape((2, 256, 256)), "vvvv", flops=300_000_000, nbytes=2_000_000
    )(gram, rows, fgram, frows)
    mixed, grad_input = kernel_call(
        final_kernel,
        (shape((128, 256)), shape((128, 256))),
        "vvvvv",
        scratch=[pltpu.VMEM((1024, 128), F32)],
        flops=100_000_000,
        nbytes=1_000_000,
    )(own, own_part, near_got, far_grads, far_outs)
    return mixed, grad_input, grad_pair, grad_up, grad_down


def solution(mesh):
    placed = (
        P(("group", "expert"), None),
        P(("group", "expert"), None),
        P(("group", "expert"), None),
        P(("group", "expert"), None),
        P("expert", None, "tensor"),
        P("expert", None, "tensor"),
        P("expert", "tensor", None),
    )
    small = mesh.shape["expert"] == 4 and mesh.shape["tensor"] == 4
    return jax.shard_map(
        gathered_body if small else body,
        mesh=mesh,
        in_specs=placed,
        out_specs=(
            P(("group", "expert"), "tensor"),
            P(("group", "expert"), "tensor"),
            P(("group", "expert"), None, "tensor"),
            P(("group", "expert"), None, "tensor"),
            P(("group", "expert"), "tensor", None),
        ),
        check_vma=False,
    )
```

```python
import functools

import jax
import jax.numpy as jnp
from jax import lax
from jax.experimental import pallas as pl
from jax.experimental.pallas import tpu as pltpu
from jax.sharding import PartitionSpec as P

NF = 16
DE = 64


def dispatch_tables(routes, expert_total, capacity):
    row_count, pick_count = routes.shape
    flat_ids = routes.reshape(-1)
    onehot = (flat_ids[:, None] == jnp.arange(expert_total, dtype=jnp.int32)[None, :]).astype(
        jnp.int32
    )
    before = jnp.cumsum(onehot, axis=0) - onehot
    position = jnp.sum(before * onehot, axis=1)
    slot_index = flat_ids * capacity + position
    slot_count = expert_total * capacity
    tables = slot_index[:, None] == jnp.arange(slot_count, dtype=jnp.int32)[None, :]
    tables = tables.reshape(row_count, pick_count, slot_count)
    return jnp.transpose(tables, (1, 2, 0)).astype(jnp.bfloat16)


def body(inputs, cotangent, gate_values, routes, pair_weight, up_weight, down_weight):
    local_count = up_weight.shape[0]
    expert_count = lax.axis_size("expert")
    tensor_count = lax.axis_size("tensor")
    expert_total = local_count * expert_count
    row_count, pick_count = routes.shape
    feature_width = inputs.shape[1]
    capacity = 2 * row_count * pick_count // expert_total
    expert_rows = expert_count * capacity
    part_width = feature_width // tensor_count
    tensor_index = lax.axis_index("tensor")
    feature_start = tensor_index * part_width
    tables = dispatch_tables(routes, expert_total, capacity)
    any_table = jnp.sum(tables, axis=0)
    scaled = (gate_values[:, :, None] * cotangent[:, None, :].astype(jnp.float32)).astype(
        jnp.bfloat16
    )
    input_slice = lax.dynamic_slice_in_dim(inputs, feature_start, part_width, 1)
    cotangent_slice = lax.dynamic_slice_in_dim(cotangent, feature_start, part_width, 1)
    input_slots = jnp.dot(any_table, inputs, preferred_element_type=jnp.float32).astype(
        jnp.bfloat16
    )
    grad_slots = jnp.einsum(
        "ksr,rkd->sd", tables, scaled, preferred_element_type=jnp.float32
    ).astype(jnp.bfloat16)
    send_shape = (expert_count, local_count, capacity, feature_width)
    input_homes, grad_homes = (
        lax.all_to_all(
            input_slots.reshape(send_shape), "expert", split_axis=0, concat_axis=2, tiled=True
        ),
        lax.all_to_all(
            grad_slots.reshape(send_shape), "expert", split_axis=0, concat_axis=2, tiled=True
        ),
    )
    input_rows = input_homes.reshape(local_count, expert_rows, feature_width)
    grad_rows = grad_homes.reshape(local_count, expert_rows, feature_width)
    cells = jnp.transpose(input_rows.reshape(local_count, expert_rows, NF, DE), (0, 2, 3, 1))
    gram = jnp.einsum("eidr,ejdr->eijr", cells, cells, preferred_element_type=jnp.float32) / DE
    gram_flat = gram.reshape(local_count, NF * NF, expert_rows).astype(jnp.bfloat16)
    input_mine = lax.dynamic_slice_in_dim(input_rows, feature_start, part_width, 2)
    cross_sum = input_mine.astype(jnp.float32) + jnp.einsum(
        "epr,epd->erd", gram_flat, pair_weight, preferred_element_type=jnp.float32
    )
    cross_part = cross_sum.astype(jnp.bfloat16)
    cross_whole = lax.all_gather(cross_part, "tensor", axis=2, tiled=True)
    hidden_pre = jnp.einsum(
        "erd,edh->erh", cross_whole, up_weight, preferred_element_type=jnp.float32
    )
    hidden_act = jax.nn.silu(hidden_pre).astype(jnp.bfloat16)
    out_terms = jnp.einsum(
        "erh,ehd->erd", hidden_act, down_weight, preferred_element_type=jnp.float32
    )
    out_mine = lax.psum_scatter(
        out_terms.astype(jnp.bfloat16), "tensor", scatter_dimension=2, tiled=True
    )
    grad_act = jnp.einsum(
        "erd,ehd->erh", grad_rows, down_weight, preferred_element_type=jnp.float32
    )
    sigmoid_pre = jax.nn.sigmoid(hidden_pre)
    grad_pre = (grad_act * sigmoid_pre * (1.0 + hidden_pre * (1.0 - sigmoid_pre))).astype(
        jnp.bfloat16
    )
    grad_down = jnp.einsum(
        "erh,erd->ehd", hidden_act, grad_rows, preferred_element_type=jnp.float32
    ).astype(jnp.bfloat16)
    grad_up = jnp.einsum(
        "erd,erh->edh", cross_whole, grad_pre, preferred_element_type=jnp.float32
    ).astype(jnp.bfloat16)
    cross_terms = jnp.einsum(
        "erh,edh->erd", grad_pre, up_weight, preferred_element_type=jnp.float32
    )
    grad_cross = lax.psum_scatter(
        cross_terms.astype(jnp.bfloat16), "tensor", scatter_dimension=2, tiled=True
    )
    grad_pair = jnp.einsum(
        "epr,erd->epd", gram_flat, grad_cross, preferred_element_type=jnp.float32
    ).astype(jnp.bfloat16)
    pair_terms = jnp.einsum(
        "erd,epd->epr", grad_cross, pair_weight, preferred_element_type=jnp.float32
    )
    grad_gram = (
        lax.psum(pair_terms.astype(jnp.bfloat16), "tensor")
        .astype(jnp.float32)
        .reshape(local_count, NF, NF, expert_rows)
    )
    symmetric = grad_gram + jnp.swapaxes(grad_gram, 1, 2)
    field_count = part_width // DE
    symmetric_mine = lax.dynamic_slice_in_dim(symmetric, tensor_index * field_count, field_count, 1)
    gram_back = (
        jnp.einsum(
            "eijr,ejdr->eidr",
            symmetric_mine,
            cells.astype(jnp.float32),
            precision=lax.Precision.HIGHEST,
        )
        / DE
    )
    gram_back = jnp.transpose(gram_back, (0, 3, 1, 2)).reshape(local_count, expert_rows, part_width)
    grad_mine = (grad_cross.astype(jnp.float32) + gram_back).astype(jnp.bfloat16)
    back_shape = (1, local_count, expert_rows, part_width)
    out_back, grad_back = (
        lax.all_to_all(
            out_mine.reshape(back_shape), "expert", split_axis=2, concat_axis=0, tiled=True
        ),
        lax.all_to_all(
            grad_mine.reshape(back_shape), "expert", split_axis=2, concat_axis=0, tiled=True
        ),
    )
    out_back = out_back.reshape(expert_total * capacity, part_width)
    grad_back = grad_back.reshape(expert_total * capacity, part_width)
    picked = jnp.einsum("ksr,sd->rkd", tables, out_back, preferred_element_type=jnp.float32)
    mixed = (
        input_slice.astype(jnp.float32) + jnp.sum(gate_values[:, :, None] * picked, axis=1)
    ).astype(jnp.bfloat16)
    grad_input = (
        cotangent_slice.astype(jnp.float32)
        + jnp.dot(any_table.T, grad_back, preferred_element_type=jnp.float32)
    ).astype(jnp.bfloat16)
    return (mixed, grad_input, grad_pair, grad_up, grad_down)


F32 = jnp.float32
BF16 = jnp.bfloat16
NT = (((1,), (1,)), ((), ()))
TN = (((0,), (0,)), ((), ()))
WIDTH = 1024
HALF = 64


def mm(a, b, dims=None):
    if dims is None:
        return jnp.dot(a, b, preferred_element_type=F32)
    return lax.dot_general(a, b, dims, preferred_element_type=F32)


def kernel_call(kernel, out_shape, where, scratch=(), flops=0, nbytes=0, vmem=48):
    kinds = {"v": pltpu.VMEM, "a": pl.ANY, "h": pltpu.HBM}
    return pl.pallas_call(
        kernel,
        out_shape=out_shape,
        in_specs=[pl.BlockSpec(memory_space=kinds[w]) for w in where],
        scratch_shapes=list(scratch),
        compiler_params=pltpu.CompilerParams(vmem_limit_bytes=vmem * 1024 * 1024),
        cost_estimate=pl.CostEstimate(flops=flops, bytes_accessed=nbytes, transcendentals=0),
    )


def shape(dims, dtype=BF16):
    return jax.ShapeDtypeStruct(dims, dtype)


def load(pairs, sems):
    copies = [pltpu.make_async_copy(a, b, sems.at[n]) for n, (a, b) in enumerate(pairs)]
    for copy in copies:
        copy.start()
    return copies


def payload_kernel(x, c, gates_in, routes_in, out_o, meta_o, gates, routes, sems):
    core = lax.rem(lax.axis_index("tensor"), 2)
    mine = pl.ds(pl.multiple_of(core * HALF, HALF), HALF)
    copies = load(
        [
            (gates_in, gates),
            (routes_in, routes),
            (x.at[mine, :], out_o.at[:, 0:WIDTH]),
            (c.at[mine, :], out_o.at[:, WIDTH : 2 * WIDTH]),
        ],
        sems,
    )
    copies[0].wait()
    copies[1].wait()
    high = gates[...].astype(BF16).astype(F32)
    low = gates[...] - high
    meta = jnp.concatenate(
        [routes[...].astype(F32), high, low, jnp.zeros((122, 128), F32)], axis=0
    )
    columns = meta.T
    meta_o[...] = columns.astype(BF16)
    out_o[:, 2 * WIDTH :] = jnp.where(core == 0, columns[0:HALF], columns[HALF:]).astype(BF16)
    for copy in copies[2:]:
        copy.wait()


def after_kernel(value, after, out_o):
    out_o[...] = value[...]


def stage_kernel(x, c, meta, pair, own_o, pair_o):
    own_o[:, 0:WIDTH] = x[...]
    own_o[:, WIDTH : 2 * WIDTH] = c[...]
    own_o[:, 2 * WIDTH :] = meta[...]
    pair_o[...] = pair[...]


def join_kernel(a, b, after, out_o):
    out_o[0:HALF, :] = a[...]
    out_o[HALF : 2 * HALF, :] = b[...]


def place_rows(whole, info, block, core, near, far):
    for at, piece in ((core, near), (1 - core, far)):
        rows = pl.ds(pl.multiple_of(block * 128 + at * HALF, HALF), HALF)
        whole[rows, :] = piece[:, 0 : 2 * WIDTH]
        info[rows, :] = piece[:, 2 * WIDTH :]


def towers(meta, whole, up, down, ready, pair, outs, scratch):
    keep, send_here, send_away, send_last, cross_o, act_o, grad_o, pre_o, gram_o, pick_o, gate_o = outs
    flipped, partial, half_gram, terms, rows, slope, outs_s, backs = scratch
    j = lax.axis_index("tensor")
    core = lax.rem(j, 2)
    xi = j // 2
    first = lax.axis_index("expert") * 2
    tokens = meta.shape[1]
    before = (
        lax.broadcasted_iota(jnp.int32, (tokens, tokens), 0)
        < lax.broadcasted_iota(jnp.int32, (tokens, tokens), 1)
    ).astype(F32).astype(BF16)
    a = lax.broadcasted_iota(jnp.int32, (256, 144), 0)
    n = lax.broadcasted_iota(jnp.int32, (256, 144), 1)
    low = jnp.minimum(a // 16, a % 16)
    high = jnp.maximum(a // 16, a % 16)
    spread = jnp.where(low * 16 - low * (low - 1) // 2 + high - low == n, 1.0, 0.0).astype(BF16)
    a = lax.broadcasted_iota(jnp.int32, (256, 256), 0)
    b = lax.broadcasted_iota(jnp.int32, (256, 256), 1)
    swapped = (a % 16) * 16 + a // 16
    both = (jnp.where(a == b, 1.0, 0.0) + jnp.where(swapped == b, 1.0, 0.0)).astype(BF16)
    slots = lax.broadcasted_iota(jnp.int32, (128, tokens), 0).astype(F32)
    both_e = range(2)
    for e in both_e:
        mine = (first + e).astype(F32)
        s0 = meta[0:1, :] == mine
        s1 = meta[1:2, :] == mine
        named = jnp.where(s0, 1.0, 0.0) + jnp.where(s1, 1.0, 0.0)
        gate = jnp.where(s0, meta[2:3, :], 0.0) + jnp.where(s1, meta[3:4, :], 0.0)
        place = mm(jnp.broadcast_to(named, (8, tokens)).astype(BF16), before)[0:1, :]
        place = jnp.where(named > 0.5, place, -1.0)
        hit = slots == place
        pick_o[e] = jnp.where(hit, 1.0, 0.0).astype(BF16)
        weight = jnp.sum(jnp.where(hit, gate, 0.0), axis=1, keepdims=True)
        gate_o[e] = jnp.broadcast_to(weight, (128, 128))
    for e in both_e:
        rows[e] = mm(pick_o[e], whole[:, 0:WIDTH])
    for e in both_e:
        flipped[e] = rows[e].T
    for e in both_e:
        grad = mm(pick_o[e], whole[:, WIDTH : 2 * WIDTH])
        grad_o[e] = (gate_o[e][:, 0:1] * grad).astype(BF16)
    for e in both_e:
        half_gram[e, 136:144, :] = jnp.zeros((8, 128), F32)
        at = 0
        for i in range(16):
            left = flipped[e, i * 64 : i * 64 + 64, :]
            for q in range(i, 16):
                prod = left * flipped[e, q * 64 : q * 64 + 64, :]
                partial[e, at * 8 : at * 8 + 8, :] = jnp.sum(prod.reshape(8, 8, 128), axis=0)
                at += 1
        for g in range(17):
            acc = partial[e, pl.ds(g * 64, 8, stride=8), :]
            for q in range(1, 8):
                acc = acc + partial[e, pl.ds(g * 64 + q, 8, stride=8), :]
            half_gram[e, g * 8 : g * 8 + 8, :] = acc * (1.0 / DE)
        gram_o[e] = mm(spread, half_gram[e].astype(BF16)).astype(BF16)
    for copy in ready[2:]:
        copy.wait()
    for e in both_e:
        cross_o[e] = (rows[e] + mm(gram_o[e], pair[e], TN)).astype(BF16)
    for copy in ready[:2]:
        copy.wait()
    for e in both_e:
        slope[e] = mm(grad_o[e], down[e], NT)
    for e in both_e:
        pre = mm(cross_o[e], up[e])
        sig = jax.nn.sigmoid(pre)
        act_o[e] = (pre * sig).astype(BF16)
        pre_o[e] = (slope[e] * sig * (1.0 + pre * (1.0 - sig))).astype(BF16)
    for e in both_e:
        terms[e] = mm(pre_o[e], up[e], NT).astype(BF16)
    for e in both_e:
        outs_s[e] = mm(act_o[e], down[e]).astype(BF16)
    for e in both_e:
        back = mm(pair[e], terms[e], NT).astype(BF16)
        backs[e] = mm(both, back).astype(BF16)
    for xr in (1, 0):
        for part in (1, 0):
            block = 2 * (xi ^ xr) + (core ^ part)
            cols = pl.ds(pl.multiple_of(block * 256, 256), 256)
            if part == 0:
                low, high = keep.at[xr, 0:320], keep.at[xr, 320:576]
            elif xr == 0:
                low, high = send_here.at[0:320], send_here.at[320:576]
            else:
                low, high = send_away, send_last
            for e in both_e:
                mine = slice(e * 128, e * 128 + 128)
                low[mine, :] = terms[e, :, cols]
                high[mine, :] = outs_s[e, :, cols]
                rows64 = pl.ds(pl.multiple_of(block * 64, 64), 64)
                low[256:320, mine] = backs[e, rows64, :]


def read_meta(info):
    rows = info[...].astype(F32).T
    return jnp.concatenate([rows[0:2], rows[2:4] + rows[4:6]], axis=0)


def own_chunk_kernel(*refs):
    own, p0, near, far, p1, p2, p3, up_in, down_in = refs[:9]
    outs, pair_o = refs[9:20], refs[20]
    whole, info, up, down, sems = refs[21:26]
    j = lax.axis_index("tensor")
    pairs = []
    for k, piece in enumerate((p0, p1, p2, p3)):
        cols = pl.ds(pl.multiple_of((j ^ k) * 256, 256), 256)
        pairs.append((piece, pair_o.at[:, :, cols]))
    copies = load([(up_in, up), (down_in, down), *pairs], sems)
    whole[0:128, :] = own[:, 0 : 2 * WIDTH]
    info[0:128, :] = own[:, 2 * WIDTH :]
    place_rows(whole, info, 1, lax.rem(j, 2), near, far)
    towers(read_meta(info), whole, up, down, copies, pair_o, outs, refs[26:])


def far_chunk_kernel(*refs):
    near, far, pair, up_in, down_in = refs[:5]
    outs = refs[5:16]
    whole, info, up, down, sems = refs[16:21]
    core = lax.rem(lax.axis_index("tensor"), 2)
    copies = load([(up_in, up), (down_in, down)], sems)
    for r in range(2):
        rows = slice(r * HALF, r * HALF + HALF)
        place_rows(whole, info, r, core, near.at[rows, :], far.at[rows, :])
    towers(read_meta(info), whole, up, down, copies, pair, outs, refs[21:])


def weights_kernel(act0, grad0, cross0, pre0, act1, grad1, cross1, pre1, down_o, up_o, done_o):
    done_o[...] = jnp.zeros((8, 128), F32)

    def stack(a, b):
        return jnp.concatenate([a, b], axis=0)

    for e in range(2):
        down_o[e] = mm(stack(act0[e], act1[e]), stack(grad0[e], grad1[e]), TN).astype(BF16)
        up_o[e] = mm(stack(cross0[e], cross1[e]), stack(pre0[e], pre1[e]), TN).astype(BF16)


def add2(a, b):
    return (a.astype(F32) + b.astype(F32)).astype(BF16)


def combine_grads(both, picks, rows_o):
    grads = jnp.zeros((256, 256), F32)
    back = jnp.zeros((64, 256), F32)
    for e in range(2):
        rows = both[e * 128 : e * 128 + 128]
        rows_o[e] = rows
        grads = grads + mm(picks[e], rows, TN)
        back = back + mm(both[256:320, e * 128 : e * 128 + 128], picks[e])
    return grads.astype(BF16), back.astype(BF16)


def put_grads(dst, grads, back, p):
    rows = slice(p * 128, p * 128 + 128)
    dst[0:128, :] = grads[rows]
    dst[128:160, 0:128] = back[0:32, rows]
    dst[128:160, 128:256] = back[32:64, rows]


def combine_outs(both, picks, gates):
    mixed = jnp.zeros((256, 256), F32)
    for e in range(2):
        out = both[e * 128 : e * 128 + 128].astype(F32) * gates[e][:, 0:1]
        mixed = mixed + mm(picks[e], out.astype(BF16), TN)
    return mixed.astype(BF16)


def combine_kernel(mine, other, theirs, pick, gate, after, first_o, second_o, rows_o):
    both = add2(add2(mine[0], other[...]), theirs[...])
    grads, back = combine_grads(both[0:320], pick, rows_o)
    mixed = combine_outs(both[320:576], pick, gate)
    for p, dst in enumerate((first_o, second_o)):
        put_grads(dst, grads, back, p)
        dst[160:288, :] = mixed[p * 128 : p * 128 + 128]


def far_grads_kernel(mine, other, theirs, pick, after, first_o, second_o, rows_o):
    both = add2(add2(mine[0, 0:320], other[0:320]), theirs[...])
    grads, back = combine_grads(both, pick, rows_o)
    for p, dst in enumerate((first_o, second_o)):
        put_grads(dst, grads, back, p)


def far_outs_kernel(mine, other, theirs, pick, gate, after, first_o, second_o):
    both = add2(add2(mine[0, 320:576], other[320:576]), theirs[...])
    mixed = combine_outs(both, pick, gate)
    first_o[...] = mixed[0:128]
    second_o[...] = mixed[128:256]


def sum_kernel(a, b, out_o):
    out_o[...] = add2(a[...], b[...])


def pair_kernel(gram0, rows0, gram1, rows1, out_o):
    for e in range(2):
        out_o[e] = (mm(gram0[e], rows0[e]) + mm(gram1[e], rows1[e])).astype(BF16)


def final_kernel(own, g0, g1, far_grads, far_outs, mixed_o, grad_o, flipped):
    column = pl.multiple_of(lax.axis_index("tensor") * 256, 256)
    mixed = own[:, pl.ds(column, 256)].astype(F32) + far_outs[...].astype(F32)
    total = own[:, pl.ds(WIDTH + column, 256)].astype(F32)
    back = jnp.zeros((32, 256), F32)
    for g in (g0, g1, far_grads):
        total = total + g[0:128, :].astype(F32)
        back = back + g[128:160, :].astype(F32)
    for g in (g0, g1):
        mixed = mixed + g[160:288, :].astype(F32)
    mixed_o[...] = mixed.astype(BF16)
    flipped[...] = own[:, 0:WIDTH].astype(F32).T
    back = jnp.concatenate([back[:, 0:128], back[:, 128:256]], axis=0)
    pieces = []
    for i in range(4):
        acc = jnp.zeros((64, 128), F32)
        for q in range(16):
            acc = acc + back[i * 16 + q : i * 16 + q + 1, :] * flipped[q * 64 : q * 64 + 64, :]
        pieces.append(acc)
    gram_back = jnp.concatenate(pieces, axis=0) * (1.0 / DE)
    grad_o[...] = (total + gram_back.T).astype(BF16)


def swap(value, axis, mask):
    size = lax.axis_size(axis)
    return lax.ppermute(value, axis, [(i, i ^ mask) for i in range(size)])


def chunk_outs():
    return (
        shape((2, 576, 256)),
        shape((576, 256)),
        shape((320, 256)),
        shape((256, 256)),
        shape((2, 128, 1024)),
        shape((2, 128, 512)),
        shape((2, 128, 1024)),
        shape((2, 128, 512)),
        shape((2, 256, 128)),
        shape((2, 128, 256)),
        shape((2, 128, 128), F32),
    )


def chunk_scratch():
    return [
        pltpu.VMEM((2, 1024, 128), F32),
        pltpu.VMEM((2, 1088, 128), F32),
        pltpu.VMEM((2, 144, 128), F32),
        pltpu.VMEM((2, 128, 1024), BF16),
        pltpu.VMEM((2, 128, 1024), F32),
        pltpu.VMEM((2, 128, 512), F32),
        pltpu.VMEM((2, 128, 1024), BF16),
        pltpu.VMEM((2, 256, 128), BF16),
    ]


def weight_scratch():
    return [pltpu.VMEM((2, 1024, 512), BF16), pltpu.VMEM((2, 512, 1024), BF16)]


def away_kernel(keep, low, high, out_o):
    out_o[0:320, :] = add2(keep[1, 0:320], low[...])
    out_o[320:576, :] = add2(keep[1, 320:576], high[...])


def away_grads_kernel(keep, low, out_o):
    out_o[...] = add2(keep[1, 0:320], low[...])


def away_outs_kernel(keep, high, after, after2, out_o):
    out_o[...] = add2(keep[1, 320:576], high[...])


def gathered_body(inputs, cotangent, gate_values, routes, pair_weight, up_weight, down_weight):
    gates, choices = gate_values.T, routes.T
    width = 2 * WIDTH + 128
    payload, meta = kernel_call(
        payload_kernel,
        (shape((HALF, width)), shape((2 * HALF, 128))),
        "hhhh",
        scratch=[
            pltpu.VMEM((2, 128), F32),
            pltpu.VMEM((2, 128), jnp.int32),
            pltpu.SemaphoreType.DMA((4,)),
        ],
        vmem=60,
    )(inputs, cotangent, gates, choices)
    got = [swap(payload, "expert", 1), swap(payload, "expert", 2)]
    got.append(swap(got[1], "expert", 1))
    both = shape((2, 256, 256))
    own, pair_own = kernel_call(
        stage_kernel, (shape((2 * HALF, width)), both), "vvvv"
    )(inputs, cotangent, meta, pair_weight)
    pair_x = swap(pair_own, "tensor", 2)
    pair_x = kernel_call(after_kernel, both, "va", flops=30_000_000)(pair_x, got[1])
    pair_c = swap(pair_own, "tensor", 1)
    pair_d = swap(pair_x, "tensor", 1)
    near_other = swap(got[0], "tensor", 1)
    chunk = kernel_call(
        own_chunk_kernel,
        chunk_outs() + (shape((2, 256, 1024)),),
        "vvvvvvvhh",
        scratch=[
            pltpu.VMEM((256, 2048), BF16),
            pltpu.VMEM((256, 128), BF16),
        ]
        + weight_scratch()
        + [pltpu.SemaphoreType.DMA((6,))]
        + chunk_scratch(),
        flops=4_000_000_000,
        nbytes=10_000_000,
    )(
        own, pair_own, got[0], near_other,
        pair_c, pair_x, pair_d, up_weight, down_weight,
    )
    keep, here, away, last, cross, act, grad, pre, gram, pick, gate, pair_all = chunk
    away = kernel_call(away_kernel, shape((576, 256)), "vvv")(
        keep, swap(away, "tensor", 1), swap(last, "tensor", 1)
    )
    theirs = swap(away, "tensor", 2)
    other = swap(here, "tensor", 1)
    far_mine = kernel_call(join_kernel, shape((2 * HALF, 2 * WIDTH + 128)), "vva")(
        got[1], got[2], away
    )
    far_other = swap(far_mine, "tensor", 1)
    chunk = kernel_call(
        far_chunk_kernel,
        chunk_outs(),
        "vvvhh",
        scratch=[pltpu.VMEM((256, 2048), BF16), pltpu.VMEM((256, 128), BF16)]
        + weight_scratch()
        + [pltpu.SemaphoreType.DMA((2,))]
        + chunk_scratch(),
        flops=4_000_000_000,
        nbytes=10_000_000,
    )(far_mine, far_other, pair_all, up_weight, down_weight)
    fkeep, fhere, faway, flast, fcross, fact, fgrad, fpre, fgram, fpick, fgate = chunk
    fother = swap(fhere, "tensor", 1)
    fgrads = kernel_call(away_grads_kernel, shape((320, 256)), "vv")(
        fkeep, swap(faway, "tensor", 1)
    )
    fouts = kernel_call(away_outs_kernel, shape((256, 256)), "vvaa")(
        fkeep, swap(flast, "tensor", 1), fgrads, theirs
    )
    fgrads = swap(fgrads, "tensor", 2)
    part = shape((288, 256))
    own_part, near_part, rows = kernel_call(
        combine_kernel, (part, part, shape((2, 128, 256))), "vvvvva"
    )(keep, other, theirs, pick, gate, fouts)
    near_got = swap(near_part, "expert", 1)
    fouts = swap(fouts, "tensor", 2)
    grad_down, grad_up, weights_done = kernel_call(
        weights_kernel,
        (shape((2, 512, 1024)), shape((2, 1024, 512)), shape((8, 128), F32)),
        "vvvvvvvv",
        flops=3_000_000_000,
        nbytes=8_000_000,
    )(act, grad, cross, pre, fact, fgrad, fcross, fpre)
    part = shape((160, 256))
    grads2, grads3, frows = kernel_call(
        far_grads_kernel, (part, part, shape((2, 128, 256))), "vvvva"
    )(fkeep, fother, fgrads, fpick, weights_done)
    grads2 = kernel_call(sum_kernel, part, "vv")(grads2, swap(grads3, "expert", 1))
    far_grads = swap(grads2, "expert", 2)
    part = shape((128, 256))
    outs2, outs3 = kernel_call(far_outs_kernel, (part, part), "vvvvva")(
        fkeep, fother, fouts, fpick, fgate, near_got
    )
    outs2 = kernel_call(sum_kernel, part, "vv")(outs2, swap(outs3, "expert", 1))
    far_outs = swap(outs2, "expert", 2)
    grad_pair = kernel_call(
        pair_kernel, shape((2, 256, 256)), "vvvv", flops=300_000_000, nbytes=2_000_000
    )(gram, rows, fgram, frows)
    mixed, grad_input = kernel_call(
        final_kernel,
        (shape((128, 256)), shape((128, 256))),
        "vvvvv",
        scratch=[pltpu.VMEM((1024, 128), F32)],
        flops=100_000_000,
        nbytes=1_000_000,
    )(own, own_part, near_got, far_grads, far_outs)
    return mixed, grad_input, grad_pair, grad_up, grad_down


def solution(mesh):
    placed = (
        P(("group", "expert"), None),
        P(("group", "expert"), None),
        P(("group", "expert"), None),
        P(("group", "expert"), None),
        P("expert", None, "tensor"),
        P("expert", None, "tensor"),
        P("expert", "tensor", None),
    )
    small = mesh.shape["expert"] == 4 and mesh.shape["tensor"] == 4
    return jax.shard_map(
        gathered_body if small else body,
        mesh=mesh,
        in_specs=placed,
        out_specs=(
            P(("group", "expert"), "tensor"),
            P(("group", "expert"), "tensor"),
            P(("group", "expert"), None, "tensor"),
            P(("group", "expert"), None, "tensor"),
            P(("group", "expert"), "tensor", None),
        ),
        check_vma=False,
    )
```

```python
import functools

import jax
import jax.numpy as jnp
from jax import lax
from jax.experimental import pallas as pl
from jax.experimental.pallas import tpu as pltpu
from jax.sharding import PartitionSpec as P

NF = 16
DE = 64


def dispatch_tables(routes, expert_total, capacity):
    row_count, pick_count = routes.shape
    flat_ids = routes.reshape(-1)
    onehot = (flat_ids[:, None] == jnp.arange(expert_total, dtype=jnp.int32)[None, :]).astype(
        jnp.int32
    )
    before = jnp.cumsum(onehot, axis=0) - onehot
    position = jnp.sum(before * onehot, axis=1)
    slot_index = flat_ids * capacity + position
    slot_count = expert_total * capacity
    tables = slot_index[:, None] == jnp.arange(slot_count, dtype=jnp.int32)[None, :]
    tables = tables.reshape(row_count, pick_count, slot_count)
    return jnp.transpose(tables, (1, 2, 0)).astype(jnp.bfloat16)


def body(inputs, cotangent, gate_values, routes, pair_weight, up_weight, down_weight):
    local_count = up_weight.shape[0]
    expert_count = lax.axis_size("expert")
    tensor_count = lax.axis_size("tensor")
    expert_total = local_count * expert_count
    row_count, pick_count = routes.shape
    feature_width = inputs.shape[1]
    capacity = 2 * row_count * pick_count // expert_total
    expert_rows = expert_count * capacity
    part_width = feature_width // tensor_count
    tensor_index = lax.axis_index("tensor")
    feature_start = tensor_index * part_width
    tables = dispatch_tables(routes, expert_total, capacity)
    any_table = jnp.sum(tables, axis=0)
    scaled = (gate_values[:, :, None] * cotangent[:, None, :].astype(jnp.float32)).astype(
        jnp.bfloat16
    )
    input_slice = lax.dynamic_slice_in_dim(inputs, feature_start, part_width, 1)
    cotangent_slice = lax.dynamic_slice_in_dim(cotangent, feature_start, part_width, 1)
    input_slots = jnp.dot(any_table, inputs, preferred_element_type=jnp.float32).astype(
        jnp.bfloat16
    )
    grad_slots = jnp.einsum(
        "ksr,rkd->sd", tables, scaled, preferred_element_type=jnp.float32
    ).astype(jnp.bfloat16)
    send_shape = (expert_count, local_count, capacity, feature_width)
    input_homes, grad_homes = (
        lax.all_to_all(
            input_slots.reshape(send_shape), "expert", split_axis=0, concat_axis=2, tiled=True
        ),
        lax.all_to_all(
            grad_slots.reshape(send_shape), "expert", split_axis=0, concat_axis=2, tiled=True
        ),
    )
    input_rows = input_homes.reshape(local_count, expert_rows, feature_width)
    grad_rows = grad_homes.reshape(local_count, expert_rows, feature_width)
    cells = jnp.transpose(input_rows.reshape(local_count, expert_rows, NF, DE), (0, 2, 3, 1))
    gram = jnp.einsum("eidr,ejdr->eijr", cells, cells, preferred_element_type=jnp.float32) / DE
    gram_flat = gram.reshape(local_count, NF * NF, expert_rows).astype(jnp.bfloat16)
    input_mine = lax.dynamic_slice_in_dim(input_rows, feature_start, part_width, 2)
    cross_sum = input_mine.astype(jnp.float32) + jnp.einsum(
        "epr,epd->erd", gram_flat, pair_weight, preferred_element_type=jnp.float32
    )
    cross_part = cross_sum.astype(jnp.bfloat16)
    cross_whole = lax.all_gather(cross_part, "tensor", axis=2, tiled=True)
    hidden_pre = jnp.einsum(
        "erd,edh->erh", cross_whole, up_weight, preferred_element_type=jnp.float32
    )
    hidden_act = jax.nn.silu(hidden_pre).astype(jnp.bfloat16)
    out_terms = jnp.einsum(
        "erh,ehd->erd", hidden_act, down_weight, preferred_element_type=jnp.float32
    )
    out_mine = lax.psum_scatter(
        out_terms.astype(jnp.bfloat16), "tensor", scatter_dimension=2, tiled=True
    )
    grad_act = jnp.einsum(
        "erd,ehd->erh", grad_rows, down_weight, preferred_element_type=jnp.float32
    )
    sigmoid_pre = jax.nn.sigmoid(hidden_pre)
    grad_pre = (grad_act * sigmoid_pre * (1.0 + hidden_pre * (1.0 - sigmoid_pre))).astype(
        jnp.bfloat16
    )
    grad_down = jnp.einsum(
        "erh,erd->ehd", hidden_act, grad_rows, preferred_element_type=jnp.float32
    ).astype(jnp.bfloat16)
    grad_up = jnp.einsum(
        "erd,erh->edh", cross_whole, grad_pre, preferred_element_type=jnp.float32
    ).astype(jnp.bfloat16)
    cross_terms = jnp.einsum(
        "erh,edh->erd", grad_pre, up_weight, preferred_element_type=jnp.float32
    )
    grad_cross = lax.psum_scatter(
        cross_terms.astype(jnp.bfloat16), "tensor", scatter_dimension=2, tiled=True
    )
    grad_pair = jnp.einsum(
        "epr,erd->epd", gram_flat, grad_cross, preferred_element_type=jnp.float32
    ).astype(jnp.bfloat16)
    pair_terms = jnp.einsum(
        "erd,epd->epr", grad_cross, pair_weight, preferred_element_type=jnp.float32
    )
    grad_gram = (
        lax.psum(pair_terms.astype(jnp.bfloat16), "tensor")
        .astype(jnp.float32)
        .reshape(local_count, NF, NF, expert_rows)
    )
    symmetric = grad_gram + jnp.swapaxes(grad_gram, 1, 2)
    field_count = part_width // DE
    symmetric_mine = lax.dynamic_slice_in_dim(symmetric, tensor_index * field_count, field_count, 1)
    gram_back = (
        jnp.einsum(
            "eijr,ejdr->eidr",
            symmetric_mine,
            cells.astype(jnp.float32),
            precision=lax.Precision.HIGHEST,
        )
        / DE
    )
    gram_back = jnp.transpose(gram_back, (0, 3, 1, 2)).reshape(local_count, expert_rows, part_width)
    grad_mine = (grad_cross.astype(jnp.float32) + gram_back).astype(jnp.bfloat16)
    back_shape = (1, local_count, expert_rows, part_width)
    out_back, grad_back = (
        lax.all_to_all(
            out_mine.reshape(back_shape), "expert", split_axis=2, concat_axis=0, tiled=True
        ),
        lax.all_to_all(
            grad_mine.reshape(back_shape), "expert", split_axis=2, concat_axis=0, tiled=True
        ),
    )
    out_back = out_back.reshape(expert_total * capacity, part_width)
    grad_back = grad_back.reshape(expert_total * capacity, part_width)
    picked = jnp.einsum("ksr,sd->rkd", tables, out_back, preferred_element_type=jnp.float32)
    mixed = (
        input_slice.astype(jnp.float32) + jnp.sum(gate_values[:, :, None] * picked, axis=1)
    ).astype(jnp.bfloat16)
    grad_input = (
        cotangent_slice.astype(jnp.float32)
        + jnp.dot(any_table.T, grad_back, preferred_element_type=jnp.float32)
    ).astype(jnp.bfloat16)
    return (mixed, grad_input, grad_pair, grad_up, grad_down)


F32 = jnp.float32
BF16 = jnp.bfloat16
NT = (((1,), (1,)), ((), ()))
TN = (((0,), (0,)), ((), ()))
WIDTH = 1024
HALF = 64


def mm(a, b, dims=None):
    if dims is None:
        return jnp.dot(a, b, preferred_element_type=F32)
    return lax.dot_general(a, b, dims, preferred_element_type=F32)


def kernel_call(kernel, out_shape, where, scratch=(), flops=0, nbytes=0, vmem=48):
    kinds = {"v": pltpu.VMEM, "a": pl.ANY, "h": pltpu.HBM}
    return pl.pallas_call(
        kernel,
        out_shape=out_shape,
        in_specs=[pl.BlockSpec(memory_space=kinds[w]) for w in where],
        scratch_shapes=list(scratch),
        compiler_params=pltpu.CompilerParams(vmem_limit_bytes=vmem * 1024 * 1024),
        cost_estimate=pl.CostEstimate(flops=flops, bytes_accessed=nbytes, transcendentals=0),
    )


def shape(dims, dtype=BF16):
    return jax.ShapeDtypeStruct(dims, dtype)


def load(pairs, sems):
    copies = [pltpu.make_async_copy(a, b, sems.at[n]) for n, (a, b) in enumerate(pairs)]
    for copy in copies:
        copy.start()
    return copies


def payload_kernel(x, c, gates_in, routes_in, out_o, meta_o, gates, routes, sems):
    core = lax.rem(lax.axis_index("tensor"), 2)
    mine = pl.ds(pl.multiple_of(core * HALF, HALF), HALF)
    copies = load(
        [
            (gates_in, gates),
            (routes_in, routes),
            (x.at[mine, :], out_o.at[:, 0:WIDTH]),
            (c.at[mine, :], out_o.at[:, WIDTH : 2 * WIDTH]),
        ],
        sems,
    )
    copies[0].wait()
    copies[1].wait()
    high = gates[...].astype(BF16).astype(F32)
    low = gates[...] - high
    meta = jnp.concatenate(
        [routes[...].astype(F32), high, low, jnp.zeros((122, 128), F32)], axis=0
    )
    columns = meta.T
    meta_o[...] = columns.astype(BF16)
    out_o[:, 2 * WIDTH :] = jnp.where(core == 0, columns[0:HALF], columns[HALF:]).astype(BF16)
    for copy in copies[2:]:
        copy.wait()


def after_kernel(value, after, out_o):
    out_o[...] = value[...]


def stage_kernel(x, c, meta, pair, own_o, pair_o):
    own_o[:, 0:WIDTH] = x[...]
    own_o[:, WIDTH : 2 * WIDTH] = c[...]
    own_o[:, 2 * WIDTH :] = meta[...]
    pair_o[...] = pair[...]


def join_kernel(a, b, after, out_o):
    out_o[0:HALF, :] = a[...]
    out_o[HALF : 2 * HALF, :] = b[...]


def place_rows(whole, info, block, core, near, far):
    for at, piece in ((core, near), (1 - core, far)):
        rows = pl.ds(pl.multiple_of(block * 128 + at * HALF, HALF), HALF)
        whole[rows, :] = piece[:, 0 : 2 * WIDTH]
        info[rows, :] = piece[:, 2 * WIDTH :]


def towers(meta, whole, up, down, ready, pair, outs, scratch):
    keep, send_here, send_away, send_last, cross_o, act_o, grad_o, pre_o, gram_o, pick_o, gate_o = outs
    flipped, partial, half_gram, terms, rows, slope, outs_s, backs = scratch
    j = lax.axis_index("tensor")
    core = lax.rem(j, 2)
    xi = j // 2
    first = lax.axis_index("expert") * 2
    tokens = meta.shape[1]
    before = (
        lax.broadcasted_iota(jnp.int32, (tokens, tokens), 0)
        < lax.broadcasted_iota(jnp.int32, (tokens, tokens), 1)
    ).astype(F32).astype(BF16)
    a = lax.broadcasted_iota(jnp.int32, (256, 144), 0)
    n = lax.broadcasted_iota(jnp.int32, (256, 144), 1)
    low = jnp.minimum(a // 16, a % 16)
    high = jnp.maximum(a // 16, a % 16)
    spread = jnp.where(low * 16 - low * (low - 1) // 2 + high - low == n, 1.0, 0.0).astype(BF16)
    a = lax.broadcasted_iota(jnp.int32, (256, 256), 0)
    b = lax.broadcasted_iota(jnp.int32, (256, 256), 1)
    swapped = (a % 16) * 16 + a // 16
    both = (jnp.where(a == b, 1.0, 0.0) + jnp.where(swapped == b, 1.0, 0.0)).astype(BF16)
    slots = lax.broadcasted_iota(jnp.int32, (128, tokens), 0).astype(F32)
    both_e = range(2)
    for e in both_e:
        mine = (first + e).astype(F32)
        s0 = meta[0:1, :] == mine
        s1 = meta[1:2, :] == mine
        named = jnp.where(s0, 1.0, 0.0) + jnp.where(s1, 1.0, 0.0)
        gate = jnp.where(s0, meta[2:3, :], 0.0) + jnp.where(s1, meta[3:4, :], 0.0)
        place = mm(jnp.broadcast_to(named, (8, tokens)).astype(BF16), before)[0:1, :]
        place = jnp.where(named > 0.5, place, -1.0)
        hit = slots == place
        pick_o[e] = jnp.where(hit, 1.0, 0.0).astype(BF16)
        weight = jnp.sum(jnp.where(hit, gate, 0.0), axis=1, keepdims=True)
        gate_o[e] = jnp.broadcast_to(weight, (128, 128))
    for e in both_e:
        rows[e] = mm(pick_o[e], whole[:, 0:WIDTH])
    for e in both_e:
        flipped[e] = rows[e].T
    for e in both_e:
        grad = mm(pick_o[e], whole[:, WIDTH : 2 * WIDTH])
        grad_o[e] = (gate_o[e][:, 0:1] * grad).astype(BF16)
    for e in both_e:
        half_gram[e, 136:144, :] = jnp.zeros((8, 128), F32)
        at = 0
        for i in range(16):
            left = flipped[e, i * 64 : i * 64 + 64, :]
            for q in range(i, 16):
                prod = left * flipped[e, q * 64 : q * 64 + 64, :]
                partial[e, at * 8 : at * 8 + 8, :] = jnp.sum(prod.reshape(8, 8, 128), axis=0)
                at += 1
        for g in range(17):
            acc = partial[e, pl.ds(g * 64, 8, stride=8), :]
            for q in range(1, 8):
                acc = acc + partial[e, pl.ds(g * 64 + q, 8, stride=8), :]
            half_gram[e, g * 8 : g * 8 + 8, :] = acc * (1.0 / DE)
        gram_o[e] = mm(spread, half_gram[e].astype(BF16)).astype(BF16)
    for copy in ready[2:]:
        copy.wait()
    for e in both_e:
        cross_o[e] = (rows[e] + mm(gram_o[e], pair[e], TN)).astype(BF16)
    for copy in ready[:2]:
        copy.wait()
    for e in both_e:
        slope[e] = mm(grad_o[e], down[e], NT)
    for e in both_e:
        pre = mm(cross_o[e], up[e])
        sig = jax.nn.sigmoid(pre)
        act_o[e] = (pre * sig).astype(BF16)
        pre_o[e] = (slope[e] * sig * (1.0 + pre * (1.0 - sig))).astype(BF16)
    for e in both_e:
        terms[e] = mm(pre_o[e], up[e], NT).astype(BF16)
    for e in both_e:
        outs_s[e] = mm(act_o[e], down[e]).astype(BF16)
    for e in both_e:
        back = mm(pair[e], terms[e], NT).astype(BF16)
        backs[e] = mm(both, back).astype(BF16)
    for xr in (1, 0):
        for part in (1, 0):
            block = 2 * (xi ^ xr) + (core ^ part)
            cols = pl.ds(pl.multiple_of(block * 256, 256), 256)
            if part == 0:
                low, high = keep.at[xr, 0:320], keep.at[xr, 320:576]
            elif xr == 0:
                low, high = send_here.at[0:320], send_here.at[320:576]
            else:
                low, high = send_away, send_last
            for e in both_e:
                mine = slice(e * 128, e * 128 + 128)
                low[mine, :] = terms[e, :, cols]
                high[mine, :] = outs_s[e, :, cols]
                rows64 = pl.ds(pl.multiple_of(block * 64, 64), 64)
                low[256:320, mine] = backs[e, rows64, :]


def read_meta(info):
    rows = info[...].astype(F32).T
    return jnp.concatenate([rows[0:2], rows[2:4] + rows[4:6]], axis=0)


def own_chunk_kernel(*refs):
    own, p0, near, far, p1, p2, p3, up_in, down_in = refs[:9]
    outs, pair_o = refs[9:20], refs[20]
    whole, info, up, down, sems = refs[21:26]
    j = lax.axis_index("tensor")
    pairs = []
    for k, piece in enumerate((p0, p1, p2, p3)):
        cols = pl.ds(pl.multiple_of((j ^ k) * 256, 256), 256)
        pairs.append((piece, pair_o.at[:, :, cols]))
    copies = load([(up_in, up), (down_in, down), *pairs], sems)
    whole[0:128, :] = own[:, 0 : 2 * WIDTH]
    info[0:128, :] = own[:, 2 * WIDTH :]
    place_rows(whole, info, 1, lax.rem(j, 2), near, far)
    towers(read_meta(info), whole, up, down, copies, pair_o, outs, refs[26:])


def far_chunk_kernel(*refs):
    near, far, pair, up_in, down_in = refs[:5]
    outs = refs[5:16]
    whole, info, up, down, sems = refs[16:21]
    core = lax.rem(lax.axis_index("tensor"), 2)
    copies = load([(up_in, up), (down_in, down)], sems)
    for r in range(2):
        rows = slice(r * HALF, r * HALF + HALF)
        place_rows(whole, info, r, core, near.at[rows, :], far.at[rows, :])
    towers(read_meta(info), whole, up, down, copies, pair, outs, refs[21:])


def weights_kernel(act0, grad0, cross0, pre0, act1, grad1, cross1, pre1, down_o, up_o, done_o):
    done_o[...] = jnp.zeros((8, 128), F32)

    def stack(a, b):
        return jnp.concatenate([a, b], axis=0)

    for e in range(2):
        down_o[e] = mm(stack(act0[e], act1[e]), stack(grad0[e], grad1[e]), TN).astype(BF16)
        up_o[e] = mm(stack(cross0[e], cross1[e]), stack(pre0[e], pre1[e]), TN).astype(BF16)


def add2(a, b):
    return (a.astype(F32) + b.astype(F32)).astype(BF16)


def combine_grads(both, picks, rows_o):
    grads = jnp.zeros((256, 256), F32)
    back = jnp.zeros((64, 256), F32)
    for e in range(2):
        rows = both[e * 128 : e * 128 + 128]
        rows_o[e] = rows
        grads = grads + mm(picks[e], rows, TN)
        back = back + mm(both[256:320, e * 128 : e * 128 + 128], picks[e])
    return grads.astype(BF16), back.astype(BF16)


def put_grads(dst, grads, back, p):
    rows = slice(p * 128, p * 128 + 128)
    dst[0:128, :] = grads[rows]
    dst[128:160, 0:128] = back[0:32, rows]
    dst[128:160, 128:256] = back[32:64, rows]


def combine_outs(both, picks, gates):
    mixed = jnp.zeros((256, 256), F32)
    for e in range(2):
        out = both[e * 128 : e * 128 + 128].astype(F32) * gates[e][:, 0:1]
        mixed = mixed + mm(picks[e], out.astype(BF16), TN)
    return mixed.astype(BF16)


def combine_kernel(mine, other, theirs, pick, gate, after, first_o, second_o, rows_o):
    both = add2(add2(mine[0], other[...]), theirs[...])
    grads, back = combine_grads(both[0:320], pick, rows_o)
    mixed = combine_outs(both[320:576], pick, gate)
    for p, dst in enumerate((first_o, second_o)):
        put_grads(dst, grads, back, p)
        dst[160:288, :] = mixed[p * 128 : p * 128 + 128]


def far_grads_kernel(mine, other, theirs, pick, after, first_o, second_o, rows_o):
    both = add2(add2(mine[0, 0:320], other[0:320]), theirs[...])
    grads, back = combine_grads(both, pick, rows_o)
    for p, dst in enumerate((first_o, second_o)):
        put_grads(dst, grads, back, p)


def far_outs_kernel(mine, other, theirs, pick, gate, after, first_o, second_o):
    both = add2(add2(mine[0, 320:576], other[320:576]), theirs[...])
    mixed = combine_outs(both, pick, gate)
    first_o[...] = mixed[0:128]
    second_o[...] = mixed[128:256]


def sum_kernel(a, b, out_o):
    out_o[...] = add2(a[...], b[...])


def pair_kernel(gram0, rows0, gram1, rows1, out_o):
    for e in range(2):
        out_o[e] = (mm(gram0[e], rows0[e]) + mm(gram1[e], rows1[e])).astype(BF16)


def final_kernel(own, g0, g1, far_grads, far_outs, mixed_o, grad_o, flipped):
    column = pl.multiple_of(lax.axis_index("tensor") * 256, 256)
    mixed = own[:, pl.ds(column, 256)].astype(F32) + far_outs[...].astype(F32)
    total = own[:, pl.ds(WIDTH + column, 256)].astype(F32)
    back = jnp.zeros((32, 256), F32)
    for g in (g0, g1, far_grads):
        total = total + g[0:128, :].astype(F32)
        back = back + g[128:160, :].astype(F32)
    for g in (g0, g1):
        mixed = mixed + g[160:288, :].astype(F32)
    mixed_o[...] = mixed.astype(BF16)
    flipped[...] = own[:, 0:WIDTH].astype(F32).T
    back = jnp.concatenate([back[:, 0:128], back[:, 128:256]], axis=0)
    pieces = []
    for i in range(4):
        acc = jnp.zeros((64, 128), F32)
        for q in range(16):
            acc = acc + back[i * 16 + q : i * 16 + q + 1, :] * flipped[q * 64 : q * 64 + 64, :]
        pieces.append(acc)
    gram_back = jnp.concatenate(pieces, axis=0) * (1.0 / DE)
    grad_o[...] = (total + gram_back.T).astype(BF16)


def swap(value, axis, mask):
    size = lax.axis_size(axis)
    return lax.ppermute(value, axis, [(i, i ^ mask) for i in range(size)])


def chunk_outs():
    return (
        shape((2, 576, 256)),
        shape((576, 256)),
        shape((320, 256)),
        shape((256, 256)),
        shape((2, 128, 1024)),
        shape((2, 128, 512)),
        shape((2, 128, 1024)),
        shape((2, 128, 512)),
        shape((2, 256, 128)),
        shape((2, 128, 256)),
        shape((2, 128, 128), F32),
    )


def chunk_scratch():
    return [
        pltpu.VMEM((2, 1024, 128), F32),
        pltpu.VMEM((2, 1088, 128), F32),
        pltpu.VMEM((2, 144, 128), F32),
        pltpu.VMEM((2, 128, 1024), BF16),
        pltpu.VMEM((2, 128, 1024), F32),
        pltpu.VMEM((2, 128, 512), F32),
        pltpu.VMEM((2, 128, 1024), BF16),
        pltpu.VMEM((2, 256, 128), BF16),
    ]


def weight_scratch():
    return [pltpu.VMEM((2, 1024, 512), BF16), pltpu.VMEM((2, 512, 1024), BF16)]


def away_kernel(keep, low, high, out_o):
    out_o[0:320, :] = add2(keep[1, 0:320], low[...])
    out_o[320:576, :] = add2(keep[1, 320:576], high[...])


def away_grads_kernel(keep, low, out_o):
    out_o[...] = add2(keep[1, 0:320], low[...])


def away_outs_kernel(keep, high, after, after2, out_o):
    out_o[...] = add2(keep[1, 320:576], high[...])


def gathered_body(inputs, cotangent, gate_values, routes, pair_weight, up_weight, down_weight):
    gates, choices = gate_values.T, routes.T
    width = 2 * WIDTH + 128
    payload, meta = kernel_call(
        payload_kernel,
        (shape((HALF, width)), shape((2 * HALF, 128))),
        "hhhh",
        scratch=[
            pltpu.VMEM((2, 128), F32),
            pltpu.VMEM((2, 128), jnp.int32),
            pltpu.SemaphoreType.DMA((4,)),
        ],
        vmem=60,
    )(inputs, cotangent, gates, choices)
    got = [swap(payload, "expert", 1), swap(payload, "expert", 2)]
    got.append(swap(got[1], "expert", 1))
    both = shape((2, 256, 256))
    own, pair_own = kernel_call(
        stage_kernel, (shape((2 * HALF, width)), both), "vvvv"
    )(inputs, cotangent, meta, pair_weight)
    pair_x = swap(pair_own, "tensor", 2)
    pair_x = kernel_call(after_kernel, both, "va", flops=30_000_000)(pair_x, got[1])
    pair_c = swap(pair_own, "tensor", 1)
    pair_d = swap(pair_x, "tensor", 1)
    near_other = swap(got[0], "tensor", 1)
    chunk = kernel_call(
        own_chunk_kernel,
        chunk_outs() + (shape((2, 256, 1024)),),
        "vvvvvvvhh",
        scratch=[
            pltpu.VMEM((256, 2048), BF16),
            pltpu.VMEM((256, 128), BF16),
        ]
        + weight_scratch()
        + [pltpu.SemaphoreType.DMA((6,))]
        + chunk_scratch(),
        flops=4_000_000_000,
        nbytes=10_000_000,
    )(
        own, pair_own, got[0], near_other,
        pair_c, pair_x, pair_d, up_weight, down_weight,
    )
    keep, here, away, last, cross, act, grad, pre, gram, pick, gate, pair_all = chunk
    away = kernel_call(away_kernel, shape((576, 256)), "vvv")(
        keep, swap(away, "tensor", 1), swap(last, "tensor", 1)
    )
    theirs = swap(away, "tensor", 2)
    far_mine = kernel_call(join_kernel, shape((2 * HALF, 2 * WIDTH + 128)), "vva")(
        got[1], got[2], away
    )
    far_other = swap(far_mine, "tensor", 1)
    chunk = kernel_call(
        far_chunk_kernel,
        chunk_outs(),
        "vvvhh",
        scratch=[pltpu.VMEM((256, 2048), BF16), pltpu.VMEM((256, 128), BF16)]
        + weight_scratch()
        + [pltpu.SemaphoreType.DMA((2,))]
        + chunk_scratch(),
        flops=4_000_000_000,
        nbytes=10_000_000,
    )(far_mine, far_other, pair_all, up_weight, down_weight)
    fkeep, fhere, faway, flast, fcross, fact, fgrad, fpre, fgram, fpick, fgate = chunk
    fother = swap(fhere, "tensor", 1)
    fgrads = kernel_call(away_grads_kernel, shape((320, 256)), "vv")(
        fkeep, swap(faway, "tensor", 1)
    )
    fouts = kernel_call(away_outs_kernel, shape((256, 256)), "vvaa")(
        fkeep, swap(flast, "tensor", 1), fgrads, theirs
    )
    fgrads_away = fgrads
    fgrads = swap(fgrads, "tensor", 2)
    here = kernel_call(after_kernel, shape((576, 256)), "va")(here, fgrads_away)
    other = swap(here, "tensor", 1)
    part = shape((288, 256))
    own_part, near_part, rows = kernel_call(
        combine_kernel, (part, part, shape((2, 128, 256))), "vvvvva"
    )(keep, other, theirs, pick, gate, fouts)
    near_got = swap(near_part, "expert", 1)
    fouts = swap(fouts, "tensor", 2)
    grad_down, grad_up, weights_done = kernel_call(
        weights_kernel,
        (shape((2, 512, 1024)), shape((2, 1024, 512)), shape((8, 128), F32)),
        "vvvvvvvv",
        flops=3_000_000_000,
        nbytes=8_000_000,
    )(act, grad, cross, pre, fact, fgrad, fcross, fpre)
    part = shape((160, 256))
    grads2, grads3, frows = kernel_call(
        far_grads_kernel, (part, part, shape((2, 128, 256))), "vvvva"
    )(fkeep, fother, fgrads, fpick, weights_done)
    grads2 = kernel_call(sum_kernel, part, "vv")(grads2, swap(grads3, "expert", 1))
    far_grads = swap(grads2, "expert", 2)
    part = shape((128, 256))
    outs2, outs3 = kernel_call(far_outs_kernel, (part, part), "vvvvva")(
        fkeep, fother, fouts, fpick, fgate, near_got
    )
    outs2 = kernel_call(sum_kernel, part, "vv")(outs2, swap(outs3, "expert", 1))
    far_outs = swap(outs2, "expert", 2)
    grad_pair = kernel_call(
        pair_kernel, shape((2, 256, 256)), "vvvv", flops=300_000_000, nbytes=2_000_000
    )(gram, rows, fgram, frows)
    mixed, grad_input = kernel_call(
        final_kernel,
        (shape((128, 256)), shape((128, 256))),
        "vvvvv",
        scratch=[pltpu.VMEM((1024, 128), F32)],
        flops=100_000_000,
        nbytes=1_000_000,
    )(own, own_part, near_got, far_grads, far_outs)
    return mixed, grad_input, grad_pair, grad_up, grad_down


def solution(mesh):
    placed = (
        P(("group", "expert"), None),
        P(("group", "expert"), None),
        P(("group", "expert"), None),
        P(("group", "expert"), None),
        P("expert", None, "tensor"),
        P("expert", None, "tensor"),
        P("expert", "tensor", None),
    )
    small = mesh.shape["expert"] == 4 and mesh.shape["tensor"] == 4
    return jax.shard_map(
        gathered_body if small else body,
        mesh=mesh,
        in_specs=placed,
        out_specs=(
            P(("group", "expert"), "tensor"),
            P(("group", "expert"), "tensor"),
            P(("group", "expert"), None, "tensor"),
            P(("group", "expert"), None, "tensor"),
            P(("group", "expert"), "tensor", None),
        ),
        check_vma=False,
    )
```
